512 devices in a mesh: top: 16 (over y, core), leaf: 32 (over x, z).
Axes of the slice: x: 4, y: 8, z: 8, core: 2. Of those that a mesh axis runs over, the one named last changes fastest.
Arguments:
- traction_vectors: float32 [4096, 192, 128], P(('top', 'leaf')), may hold values from -6 to 6
- row_basis: float32 [4096, 32, 192], P(('top', 'leaf')), may hold values from -0.4375 to 0.4375
- up_leaf: float32 [4096, 1024], P(('top', 'leaf')), may hold values from -0.75 to 0.75
- up_pair: float32 [2048, 1024], P(('top', 'leaf')), may hold values from -0.5 to 0.5
- up_device: float32 [512, 1024], P(('top', 'leaf')), may hold values from -0.1875 to 0.1875
- couple_leaf: float32 [4096, 6, 1024], P(('top', 'leaf')), may hold values from -0.4375 to 0.4375
- pair_coupling_blocks: float32 [2048, 6, 1024], P(('top', 'leaf')), may hold values from -0.4375 to 0.4375
- couple_device: float32 [512, 6, 1024], P(('top', 'leaf')), may hold values from -0.4375 to 0.4375
- couple_top: float32 [16, 4, 1024], P('top'), may hold values from -0.5 to 0.5
- list_leaf: int32 [4096, 6], P(('top', 'leaf')), may hold values from 0 to 4095, as said below
- list_pair: int32 [2048, 6], P(('top', 'leaf')), may hold values from 0 to 2047, as said below
- list_device: int32 [512, 6], P(('top', 'leaf')), may hold values from 0 to 511
- list_top: int32 [16, 4], P('top'), may hold values from 0 to 15
- mask_leaf: int32 [4096, 6], P(('top', 'leaf')), may hold values 0 or 1
- mask_pair: int32 [2048, 6], P(('top', 'leaf')), may hold values 0 or 1
- mask_device: int32 [512, 6], P(('top', 'leaf')), may hold values 0 or 1
- mask_top: int32 [16, 4], P('top'), may hold values 0 or 1
- down_leaf: float32 [4096, 1024], P(('top', 'leaf')), may hold values from -1 to 1
- down_pair: float32 [2048, 1024], P(('top', 'leaf')), may hold values from -1 to 1
- down_device: float32 [512, 1024], P(('top', 'leaf')), may hold values from -1 to 1
- col_basis: float32 [4096, 32, 192], P(('top', 'leaf')), may hold values from -0.5 to 0.5
Outputs:
- product: float32 [4096, 192, 128], P(('top', 'leaf'))
The draws below stay inside these ranges and needn't reach their ends.
Inputs may be any that keep to these rules, and one draw needn't show every extreme that they name: `list_leaf`: entry (i, k) lies in the same block of 256 leaf clusters as i, and from (i // 8 - 1) * 8 to (i // 8 + 2) * 8 - 1. `list_pair`: entry (p, k) lies in the same block of 128 pair clusters as p, and from (p // 4 - 1) * 4 to (p // 4 + 2) * 4 - 1.
All inputs are finite; a program needn't handle non-finite values. No bound on the sum of `mask_leaf` or of `mask_pair` or of `mask_device` or of `mask_top` on one device may be relied on, other than what follows from the above.
Results may differ from the reference program's by a relative error of at most 0.0001.
Values sent between devices are 32-bit elements; how exact they have to be, the bound alone decides.
No kernel may reach another device: no remote copies, remote signals or barrier semaphores. Data moves between devices by JAX's collectives and lax.ppermute only.
A program may use at most 64 MiB of HBM per device.

```python
import jax
import jax.numpy as jnp
from jax import lax

RANK = 32
ENTRIES = 192
LEAF_DEV = 8
NRHS = 128
LIST_LEAF = 6
LIST_PAIR = 6
LIST_DEV = 6
LIST_TOP = 4
PAIRS_DEV = 4
SUBS = 32
TOPS = 16
NLEAF = 4096
NPAIR = 2048
GROUP = 256
DEVICES = 512


def nearby(key, count, per_dev, group, width):
    target = jnp.arange(count, dtype=jnp.int32)
    first = target // per_dev * per_dev
    lowest = target // group * group
    offset = jax.random.randint(key, (count, width), -per_dev, 2 * per_dev, dtype=jnp.int32)
    chosen = jnp.clip(first[:, None] + offset, lowest[:, None], lowest[:, None] + group - 1)
    return chosen.astype(jnp.int32)


def draw_list_leaf(key, part):
    key = jax.random.fold_in(key, 11)
    return nearby(key, NLEAF, LEAF_DEV, GROUP, LIST_LEAF)


def draw_list_pair(key, part):
    key = jax.random.fold_in(key, 12)
    return nearby(key, NPAIR, PAIRS_DEV, GROUP // 2, LIST_PAIR)


def plant(result, own_key, low, top_value):
    shape = result.shape
    index_at = [jax.random.randint(jax.random.fold_in(own_key, axis), (), 0, shape[axis]) for axis in range(len(shape))]
    result = result.at[tuple(index_at)].set(low)
    longest = shape.index(max(shape))
    index_at[longest] = (index_at[longest] + 1) % shape[longest]
    return result.at[tuple(index_at)].set(top_value)


def shard_levels(rng, shape, split, smallest, high):
    loudness = 1.0
    for axis_at, blocks in split:
        steps = jax.random.uniform(jax.random.fold_in(jax.random.fold_in(rng, 6), axis_at), (blocks,), jnp.float32, smallest / len(split), high / len(split))
        loudness = loudness * jnp.repeat(jnp.exp(steps), shape[axis_at] // blocks).reshape((-1,) + (1,) * (len(shape) - 1 - axis_at))
    return loudness


def scatter_about(own_key, extent, spread, bound, pieces=(), held_as=jnp.bfloat16):
    array = jax.random.normal(own_key, extent, jnp.float32) * spread
    if len(pieces) > 0:
        array = shard_levels(own_key, extent, pieces, -0.22, 0.18) * array
    return jnp.clip(array, min=-bound, max=bound).astype(held_as)


def setup_inputs(seed: int = 0) -> dict:
    arg_keys = jax.random.split(jax.random.key(seed), 22)
    traction_vectors = scatter_about(arg_keys[0], (NLEAF, ENTRIES, NRHS), 1.0, 6.0, ((0, 512),), jnp.float32)
    row_basis = scatter_about(arg_keys[1], (NLEAF, RANK, ENTRIES), ENTRIES ** -0.5, 0.4375, ((0, 512),), jnp.float32)
    up_leaf = scatter_about(arg_keys[2], (NLEAF, RANK * RANK), (2 * RANK) ** -0.5, 0.75, ((0, 512),), jnp.float32)
    up_pair = scatter_about(arg_keys[3], (NPAIR, RANK * RANK), (PAIRS_DEV * RANK) ** -0.5, 0.5, ((0, 512),), jnp.float32)
    up_device = scatter_about(arg_keys[4], (DEVICES, RANK * RANK), (SUBS * RANK) ** -0.5, 0.1875, ((0, 512),), jnp.float32)
    couple_leaf = scatter_about(arg_keys[5], (NLEAF, LIST_LEAF, RANK * RANK), (LIST_LEAF * RANK) ** -0.5, 0.4375, ((0, 512),), jnp.float32)
    pair_coupling_blocks = scatter_about(arg_keys[6], (NPAIR, LIST_PAIR, RANK * RANK), (LIST_PAIR * RANK) ** -0.5, 0.4375, ((0, 512),), jnp.float32)
    couple_device = scatter_about(arg_keys[7], (DEVICES, LIST_DEV, RANK * RANK), (LIST_DEV * RANK) ** -0.5, 0.4375, ((0, 512),), jnp.float32)
    couple_top = scatter_about(arg_keys[8], (TOPS, LIST_TOP, RANK * RANK), (LIST_TOP * RANK) ** -0.5, 0.5, ((0, 16),), jnp.float32)
    list_leaf = draw_list_leaf(jax.random.fold_in(arg_keys[21], 71), 0)
    list_pair = draw_list_pair(jax.random.fold_in(arg_keys[21], 71), 0)
    list_device = plant(jax.random.randint(arg_keys[11], (DEVICES, LIST_DEV), 0, DEVICES), jax.random.fold_in(arg_keys[11], 1), 0, DEVICES - 1).astype(jnp.int32)
    list_top = plant(jax.random.randint(arg_keys[12], (TOPS, LIST_TOP), 0, TOPS), jax.random.fold_in(arg_keys[12], 1), 0, TOPS - 1).astype(jnp.int32)
    mask_leaf = plant((jax.random.randint(arg_keys[13], (NLEAF, LIST_LEAF), 0, 4) < 3).astype(jnp.int32), jax.random.fold_in(arg_keys[13], 1), 0, 1)
    mask_pair = plant((jax.random.randint(arg_keys[14], (NPAIR, LIST_PAIR), 0, 4) < 3).astype(jnp.int32), jax.random.fold_in(arg_keys[14], 1), 0, 1)
    mask_device = plant((jax.random.randint(arg_keys[15], (DEVICES, LIST_DEV), 0, 4) < 3).astype(jnp.int32), jax.random.fold_in(arg_keys[15], 1), 0, 1)
    mask_top = plant((jax.random.randint(arg_keys[16], (TOPS, LIST_TOP), 0, 4) < 3).astype(jnp.int32), jax.random.fold_in(arg_keys[16], 1), 0, 1)
    down_leaf = scatter_about(arg_keys[17], (NLEAF, RANK * RANK), RANK ** -0.5, 1.0, ((0, 512),), jnp.float32)
    down_pair = scatter_about(arg_keys[18], (NPAIR, RANK * RANK), RANK ** -0.5, 1.0, ((0, 512),), jnp.float32)
    down_device = scatter_about(arg_keys[19], (DEVICES, RANK * RANK), RANK ** -0.5, 1.0, ((0, 512),), jnp.float32)
    col_basis = scatter_about(arg_keys[20], (NLEAF, RANK, ENTRIES), (4 * RANK) ** -0.5, 0.5, ((0, 512),), jnp.float32)
    return dict(traction_vectors=traction_vectors, row_basis=row_basis, up_leaf=up_leaf, up_pair=up_pair, up_device=up_device, couple_leaf=couple_leaf, pair_coupling_blocks=pair_coupling_blocks, couple_device=couple_device, couple_top=couple_top, list_leaf=list_leaf, list_pair=list_pair, list_device=list_device, list_top=list_top, mask_leaf=mask_leaf, mask_pair=mask_pair, mask_device=mask_device, mask_top=mask_top, down_leaf=down_leaf, down_pair=down_pair, down_device=down_device, col_basis=col_basis)


TOPMOST_PRECISION = lax.Precision.HIGHEST


def square(flat_blocks):
    return flat_blocks.reshape(flat_blocks.shape[:-1] + (RANK, RANK))


def couple(blocks, sources, index, mask):
    accumulated_output = jnp.zeros((blocks.shape[0], RANK, sources.shape[-1]), jnp.float32)
    for slot in range(index.shape[1]):
        selected_entries = jnp.take(sources, index[:, slot].astype(jnp.int32), axis=0)
        quadrature_weight = square(blocks[:, slot]) * mask[:, slot].astype(jnp.float32)[:, None, None]
        accumulated_output = accumulated_output + jnp.einsum('qup,qpj->quj', quadrature_weight, selected_entries, precision=TOPMOST_PRECISION)
    return accumulated_output


def reference(traction_vectors, row_basis, up_leaf, up_pair, up_device, couple_leaf, pair_coupling_blocks, couple_device, couple_top, list_leaf, list_pair, list_device, list_top, mask_leaf, mask_pair, mask_device, mask_top, down_leaf, down_pair, down_device, col_basis):
    coeff_leaf = jnp.einsum('lre,len->lrn', row_basis, traction_vectors, precision=TOPMOST_PRECISION)
    coeff_pair = jnp.einsum('pcab,pcan->pbn', square(up_leaf).reshape(NPAIR, 2, RANK, RANK), coeff_leaf.reshape(NPAIR, 2, RANK, NRHS), precision=TOPMOST_PRECISION)
    coeff_device = jnp.einsum('dcab,dcan->dbn', square(up_pair).reshape(DEVICES, PAIRS_DEV, RANK, RANK), coeff_pair.reshape(DEVICES, PAIRS_DEV, RANK, NRHS), precision=TOPMOST_PRECISION)
    coeff_top = jnp.einsum('gcab,gcan->gbn', square(up_device).reshape(TOPS, SUBS, RANK, RANK), coeff_device.reshape(TOPS, SUBS, RANK, NRHS), precision=TOPMOST_PRECISION)
    far_leaf = couple(couple_leaf, coeff_leaf, list_leaf, mask_leaf)
    far_pair = couple(pair_coupling_blocks, coeff_pair, list_pair, mask_pair)
    far_device = couple(couple_device, coeff_device, list_device, mask_device)
    far_top = couple(couple_top, coeff_top, list_top, mask_top)
    local_device = far_device + jnp.einsum('gcab,gbn->gcan', square(down_device).reshape(TOPS, SUBS, RANK, RANK), far_top, precision=TOPMOST_PRECISION).reshape(DEVICES, RANK, NRHS)
    resident_pair_index = far_pair + jnp.einsum('dcab,dbn->dcan', square(down_pair).reshape(DEVICES, PAIRS_DEV, RANK, RANK), local_device, precision=TOPMOST_PRECISION).reshape(NPAIR, RANK, NRHS)
    local_leaf = far_leaf + jnp.einsum('pcab,pbn->pcan', square(down_leaf).reshape(NPAIR, 2, RANK, RANK), resident_pair_index, precision=TOPMOST_PRECISION).reshape(NLEAF, RANK, NRHS)
    return jnp.einsum('lre,lrn->len', col_basis, local_leaf, precision=TOPMOST_PRECISION)
```

```python
import jax
import jax.numpy as jnp
from jax import lax
from jax.experimental import pallas as pl
from jax.experimental.pallas import tpu as pltpu
from jax.sharding import PartitionSpec as P

RANK = 32
COLS = 128
QUADS = 4
ROWS8 = 8
F32 = jnp.float32
BF16 = jnp.bfloat16
VMEM_LIMIT = 32 * 1024 * 1024
ALMOST_ALL = 60 * 1024 * 1024


def split(x):
    high = x.astype(BF16)
    return high, (x - high.astype(F32)).astype(BF16)


def dot(a, b, contract=((1,), (0,))):
    return lax.dot_general(a, b, (contract, ((), ())), preferred_element_type=F32)


def dot_split(a, b_high, b_low):
    rows = a.shape[0]
    a_high, a_low = split(a)
    both = dot(jnp.concatenate([a_high, a_low], axis=0), b_high)
    return both[:rows] + both[rows:] + dot(a_high, b_low)


def dot_first(a, b):
    a_high, a_low = split(a)
    b_high, b_low = split(b)
    return dot(
        jnp.concatenate([a_high, a_high, a_low], axis=0),
        jnp.concatenate([b_high, b_low, b_high], axis=0),
        ((0,), (0,)),
    )


def lanes(rows=ROWS8):
    return lax.broadcasted_iota(jnp.int32, (rows, COLS), 1)


def square(flat):
    return jnp.concatenate([flat[:, RANK * q : RANK * (q + 1)] for q in range(QUADS)], axis=0)


def beside(flats):
    group = lanes() // RANK
    rows = []
    for q in range(QUADS):
        row = None
        for k, flat in enumerate(flats):
            shift = (RANK * (k - q)) % COLS
            moved = pltpu.roll(flat, shift, 1) if shift else flat
            row = moved if row is None else jnp.where(group == k, moved, row)
        rows.append(row)
    return jnp.concatenate(rows, axis=0)


def quad_rows(ref, start):
    return jnp.concatenate(
        [ref[pl.ds(start + q, ROWS8, stride=QUADS), :] for q in range(QUADS)], axis=0
    )


def store_natural(ref, start, x):
    for q in range(QUADS):
        ref[pl.ds(start + q, ROWS8, stride=QUADS), :] = x[ROWS8 * q : ROWS8 * (q + 1)]


def weights(couple, down, top, list_d, mask_d, list_t, mask_t, natural):
    slots, top_slots = list_d.shape[1], list_t.shape[1]
    flats = [couple[ROWS8 * k : ROWS8 * (k + 1), :] * mask_d[0, k].astype(F32) for k in range(slots)]
    lane = lanes(RANK)
    ids = jnp.zeros((RANK, COLS), F32)
    for k in range(slots):
        ids = jnp.where(lane == 64 + k, list_d[0, k].astype(F32), ids)
    for k in range(top_slots):
        ids = jnp.where(lane == 64 + slots + k, list_t[0, k].astype(F32), ids)
    tops = [
        top[pl.ds(k, ROWS8, stride=top_slots), :] * mask_t[0, k].astype(F32) for k in range(top_slots)
    ]
    store_natural(natural, 0, beside(tops))
    top_high, top_low = split(natural[...])
    return (
        beside(flats[:4]),
        jnp.where(lane < 64, beside(flats[4:]), ids),
        dot_split(square(down[...]), top_high, top_low),
    )


def first_kernel(*refs):
    count = 12
    sources, (weight_ref, stack_ref, send_ref), scratch = refs[:count], refs[count : count + 3], refs[count + 3 :]
    held, (sems, traction, traction_sems, natural) = scratch[:count - 1], scratch[count - 1 :]
    copies = [pltpu.make_async_copy(s, h, sems.at[n]) for n, (s, h) in enumerate(zip(sources[1:], held))]
    leaves = sources[0].shape[0]
    pairs = leaves // 2
    tractions = [
        pltpu.make_async_copy(sources[0].at[i], traction.at[i], traction_sems.at[i]) for i in range(leaves)
    ]
    for copy in copies + tractions:
        copy.start()
    couple, down, top, list_d, mask_d, list_t, mask_t, basis, up_leaf, up_pair, up_device = held
    for copy in copies:
        copy.wait()
    for n, block in enumerate(weights(couple, down, top, list_d, mask_d, list_t, mask_t, natural)):
        for t in range(weight_ref.shape[0]):
            weight_ref[t, RANK * n : RANK * (n + 1), :] = block
    for i in range(leaves):
        tractions[i].wait()
        high, low = split(traction[i])
        stack_ref[RANK * i : RANK * (i + 1), :] = dot_split(basis[i], high, low)
    for p in range(pairs):
        weight = [square(up_leaf[pl.ds(i, ROWS8, stride=leaves), :]) for i in (2 * p, 2 * p + 1)]
        value = [quad_rows(stack_ref, RANK * i) for i in (2 * p, 2 * p + 1)]
        at = RANK * (leaves + p)
        stack_ref[at : at + RANK, :] = dot_first(
            jnp.concatenate(weight, axis=0), jnp.concatenate(value, axis=0)
        )
    weight = [square(up_pair[pl.ds(p, ROWS8, stride=pairs), :]) for p in range(pairs)]
    value = [quad_rows(stack_ref, RANK * (leaves + p)) for p in range(pairs)]
    coeff = dot_first(jnp.concatenate(weight, axis=0), jnp.concatenate(value, axis=0))
    up = up_device[...]
    for z in range(send_ref.shape[0]):
        send_ref[z, 0:RANK, :] = coeff
        send_ref[z, RANK : RANK + ROWS8, :] = up


def far_kernel(
    low_ref, own_ref, high_ref, couple_leaf, couple_pair, down_leaf, down_pair, basis,
    list_leaf, mask_leaf, list_pair, mask_pair, fixed_ref, slope_ref, near_high, near_low, natural,
):
    leaves, slots = list_leaf.shape
    pairs = list_pair.shape[0]
    blocks = leaves + pairs
    top = lax.axis_index("y") * lax.axis_size("core") + lax.axis_index("core")
    leaf = lax.axis_index("x") * lax.axis_size("z") + lax.axis_index("z")
    position = top * (lax.axis_size("x") * lax.axis_size("z")) + leaf
    size = blocks * RANK
    for n, ref in enumerate((low_ref, own_ref, high_ref)):
        high, low = split(ref[...])
        near_high[n * size : (n + 1) * size, :] = high
        near_low[n * size : (n + 1) * size, :] = low
    none = jnp.zeros((RANK, COLS), BF16)
    near_high[3 * size : 3 * size + RANK, :] = none
    near_low[3 * size : 3 * size + RANK, :] = none

    def near(index, mask, per_dev, offset):
        relative = index - position * per_dev + per_dev
        block = relative // per_dev * blocks + offset + relative % per_dev
        start = pl.multiple_of(jnp.where(mask == 0, 3 * blocks, block) * RANK, RANK)
        return near_high[pl.ds(start, RANK), :], near_low[pl.ds(start, RANK), :]

    for p in range(pairs):
        flats = [couple_pair[pl.ds(k * ROWS8 * pairs + p, ROWS8, stride=pairs), :] for k in range(slots)]
        weight = jnp.concatenate([beside(flats[:4]), beside(flats[4:])], axis=1)
        taken = [near(list_pair[p, k], mask_pair[p, k], pairs, leaves) for k in range(slots)]
        rows = [jnp.concatenate([t[n] for t in taken] + [none, none], axis=0) for n in (0, 1)]
        at = 2 * RANK * p
        store_natural(natural, at, dot_split(weight, *rows))
        store_natural(natural, at + RANK, beside([down_pair[pl.ds(p, ROWS8, stride=pairs), :]] * 4))
        sums = split(natural[at : at + RANK, :])
        downs = split(natural[at + RANK : at + 2 * RANK, :])
        for i in (2 * p, 2 * p + 1):
            flats = [
                couple_leaf[pl.ds(k * ROWS8 * leaves + i, ROWS8, stride=leaves), :] for k in range(slots)
            ] + [down_leaf[pl.ds(i, ROWS8, stride=leaves), :]]
            weight = jnp.concatenate([beside(flats[:4]), beside(flats[4:])], axis=1)
            taken = [near(list_leaf[i, k], mask_leaf[i, k], leaves, 0) for k in range(slots)]
            rows = [
                jnp.concatenate(
                    [
                        jnp.concatenate([t[n] for t in taken] + [sums[n], none], axis=0),
                        jnp.concatenate([none] * slots + [downs[n], none], axis=0),
                    ],
                    axis=1,
                )
                for n in (0, 1)
            ]
            here = dot_split(weight, *rows)
            at = 2 * RANK * (pairs + i)
            store_natural(natural, at, here[:, :COLS])
            store_natural(natural, at + RANK, here[:, COLS:])
            here = jnp.concatenate([natural[at : at + RANK, :], natural[at + RANK : at + 2 * RANK, :]], axis=1)
            both = dot_first(basis[i], here)
            fixed_ref[i] = both[:, :COLS]
            slope = both[:, COLS:]
            slope_high = slope.astype(BF16).astype(F32)
            lane = lanes(slope.shape[0])
            slope_ref[i] = jnp.where(
                lane < 64, slope_high, jnp.where(lane < 96, slope - slope_high, 0.0)
            ).astype(BF16)


def part_kernel(*refs):
    buffers = len(refs) - 6
    coeff_refs = refs[:buffers]
    weight_ref, ids_ref, out_ref, coeff_high, coeff_low, gathered = refs[buffers:]
    targets = weight_ref.shape[0]
    across = buffers // 2
    deep = coeff_refs[0].shape[0]
    subs = across * deep
    slots, top_slots = 6, 4
    row, core, here = lax.axis_index("y"), lax.axis_index("core"), lax.axis_index("x")
    none = jnp.zeros((RANK, COLS), BF16)
    blocks = [(ref, z) for ref in coeff_refs for z in range(deep)]
    for d, (ref, z) in enumerate(blocks):
        value = ref[z, 0:RANK, :]
        gathered[RANK * d : RANK * (d + 1), :] = value
        high, low = split(value)
        coeff_high[RANK * d : RANK * (d + 1), :] = high
        coeff_low[RANK * d : RANK * (d + 1), :] = low
    coeff_high[2 * RANK * subs : RANK * (2 * subs + 1), :] = none
    coeff_low[2 * RANK * subs : RANK * (2 * subs + 1), :] = none
    tops = []
    for g in range(2):
        up = jnp.concatenate(
            [ref[z, RANK : RANK + ROWS8, :] for ref, z in blocks[g * subs : (g + 1) * subs]], axis=0
        )
        value = jnp.concatenate(
            [
                gathered[pl.ds(RANK * subs * g + q, ROWS8 * subs, stride=QUADS), :]
                for q in range(QUADS)
            ],
            axis=1,
        )
        every = dot_first(up, value)
        top = jnp.zeros((RANK, COLS), F32)
        for q in range(QUADS):
            top = top + every[RANK * q : RANK * (q + 1), COLS * q : COLS * (q + 1)]
        tops.append(split(top))
    lane_group = lanes(RANK) // RANK
    top_weight = []
    for t in range(targets):
        used = [jnp.zeros((RANK, COLS), F32)] * 2
        for k in range(top_slots):
            owner = ids_ref[t, 64 + slots + k].astype(jnp.int32)
            for g in range(2):
                group = row * 2 + (core if g == 0 else 1 - core)
                used[g] = jnp.where(lane_group == k, jnp.where(owner == group, 1.0, 0.0), used[g])
        block = weight_ref[t, 2 * RANK : 3 * RANK, :]
        top_weight.append(jnp.concatenate([block * used[0], block * used[1]], axis=1))
    top_part = dot_split(
        jnp.concatenate(top_weight, axis=0),
        jnp.concatenate([tops[0][0]] * 4 + [tops[1][0]] * 4, axis=0),
        jnp.concatenate([tops[0][1]] * 4 + [tops[1][1]] * 4, axis=0),
    )

    def starts(t):
        found = []
        for k in range(slots):
            index = ids_ref[t, 64 + k].astype(jnp.int32)
            group, sub = index // subs, index % subs
            place = (here + across - sub // deep) % across * deep + sub % deep
            place = place + jnp.where(group % 2 == core, 0, subs)
            block = jnp.where(group // 2 == row, place, 2 * subs)
            found.append(pl.multiple_of(block * RANK, RANK))
        return found

    for t in range(0, targets, 2):
        pair = [starts(t), starts(t + 1)]
        rows = [
            jnp.concatenate(
                [jnp.concatenate([ref[pl.ds(s, RANK), :] for s in one], axis=0) for one in pair], axis=1
            )
            for ref in (coeff_high, coeff_low)
        ]
        weight = [
            jnp.concatenate([weight_ref[u, 0:RANK, :], weight_ref[u, RANK : 2 * RANK, :64]], axis=1)
            for u in (t, t + 1)
        ]
        both = dot_split(jnp.concatenate(weight, axis=0), *rows)
        out_ref[t] = both[:RANK, :COLS] + top_part[RANK * t : RANK * (t + 1)]
        out_ref[t + 1] = both[RANK:, COLS:] + top_part[RANK * (t + 1) : RANK * (t + 2)]


def last_kernel(parts_ref, fixed_ref, slope_ref, out_ref, natural):
    total = parts_ref[0]
    for t in range(1, parts_ref.shape[0]):
        total = total + parts_ref[t]
    store_natural(natural, 0, total)
    high, low = split(natural[...])
    rows = jnp.concatenate([high, low, high, jnp.zeros((RANK, COLS), BF16)], axis=0)
    for i in range(out_ref.shape[0]):
        out_ref[i] = fixed_ref[i] + dot(slope_ref[i], rows)


def whole(kernel, out, args, smem=(), hbm=(), scratch=(), flops=0, limit=VMEM_LIMIT):
    vmem = pl.BlockSpec(memory_space=pltpu.VMEM)
    scalars = pl.BlockSpec(memory_space=pltpu.SMEM)
    far = pl.BlockSpec(memory_space=pltpu.HBM)
    size = sum(a.size * a.dtype.itemsize for a in args)
    outs = out if isinstance(out, tuple) else (out,)
    size += sum(o.size * o.dtype.itemsize for o in outs)
    return pl.pallas_call(
        kernel,
        out_shape=out,
        in_specs=[scalars if n in smem else far if n in hbm else vmem for n in range(len(args))],
        out_specs=tuple(vmem for _ in out) if isinstance(out, tuple) else vmem,
        scratch_shapes=list(scratch),
        compiler_params=pltpu.CompilerParams(vmem_limit_bytes=limit),
        cost_estimate=pl.CostEstimate(flops=flops, bytes_accessed=size, transcendentals=0),
    )(*args)


def rows_of(x):
    if x.ndim == 2:
        return x.reshape(x.shape[0], ROWS8, COLS).transpose(1, 0, 2).reshape(-1, COLS)
    return x.reshape(x.shape[0], x.shape[1], ROWS8, COLS).transpose(1, 2, 0, 3).reshape(-1, COLS)


def body(
    traction_vectors,
    row_basis,
    up_leaf,
    up_pair,
    up_device,
    couple_leaf,
    pair_coupling_blocks,
    couple_device,
    couple_top,
    list_leaf,
    list_pair,
    list_device,
    list_top,
    mask_leaf,
    mask_pair,
    mask_device,
    mask_top,
    down_leaf,
    down_pair,
    down_device,
    col_basis,
):
    def shape(*dims, dtype=F32):
        return jax.ShapeDtypeStruct(dims, dtype)

    leaves, entries, _ = traction_vectors.shape
    blocks = leaves + leaves // 2
    across, deep = lax.axis_size("x"), lax.axis_size("z")
    targets = lax.axis_size("y")
    subs = across * deep
    first = (
        traction_vectors, rows_of(couple_device), rows_of(down_device), rows_of(couple_top[0]),
        list_device, mask_device, list_top, mask_top,
        row_basis, rows_of(up_leaf), rows_of(up_pair), rows_of(up_device),
    )
    scalars = (4, 5, 6, 7)
    held = [
        (pltpu.SMEM if n in scalars else pltpu.VMEM)(a.shape, a.dtype) for n, a in enumerate(first) if n
    ]
    weights, stack, send = whole(
        first_kernel,
        (shape(targets, 3 * RANK, COLS), shape(blocks * RANK, COLS), shape(deep, RANK + ROWS8, COLS)),
        first,
        hbm=range(len(first)),
        scratch=[
            *held,
            pltpu.SemaphoreType.DMA((len(held),)),
            pltpu.VMEM(traction_vectors.shape, F32),
            pltpu.SemaphoreType.DMA((leaves,)),
            pltpu.VMEM((RANK, COLS), F32),
        ],
        flops=6 * 10**7,
        limit=ALMOST_ALL,
    )
    weights = lax.all_to_all(weights, "y", 0, 0, tiled=True)
    coeffs = lax.all_to_all(send, "z", 0, 0, tiled=True)
    coeffs = [coeffs] + [
        lax.ppermute(coeffs, "x", [(i, (i + step) % across) for i in range(across)])
        for step in range(1, across)
    ]
    coeffs[-1], stack = lax.optimization_barrier((coeffs[-1], stack))
    coeffs = coeffs + [lax.ppermute(block, "core", [(0, 1), (1, 0)]) for block in coeffs]
    leaf_axes = ("x", "z")
    low = lax.ppermute(stack, leaf_axes, [(i, i + 1) for i in range(subs - 1)])
    high = lax.ppermute(stack, leaf_axes, [(i + 1, i) for i in range(subs - 1)])
    near = pltpu.VMEM(((3 * blocks + 1) * RANK, COLS), BF16)
    fixed, slope = whole(
        far_kernel,
        (shape(leaves, entries, COLS), shape(leaves, entries, COLS, dtype=BF16)),
        (
            low, stack, high, rows_of(couple_leaf), rows_of(pair_coupling_blocks),
            rows_of(down_leaf), rows_of(down_pair), col_basis,
            list_leaf, mask_leaf, list_pair, mask_pair,
        ),
        smem=(8, 9, 10, 11),
        scratch=[near, near, pltpu.VMEM((2 * RANK * blocks, COLS), F32)],
        flops=10**8,
    )
    parts = whole(
        part_kernel,
        shape(targets, RANK, COLS),
        (*coeffs, weights, weights[:, RANK, :]),
        smem=(2 * across + 1,),
        scratch=[
            pltpu.VMEM(((2 * subs + 1) * RANK, COLS), BF16),
            pltpu.VMEM(((2 * subs + 1) * RANK, COLS), BF16),
            pltpu.VMEM((2 * subs * RANK, COLS), F32),
        ],
        flops=10**8,
    )
    parts = lax.all_to_all(parts, "y", 0, 0, tiled=True)
    return whole(
        last_kernel,
        shape(leaves, entries, COLS),
        (parts, fixed, slope),
        scratch=[pltpu.VMEM((RANK, COLS), F32)],
        flops=5 * 10**7,
    )


def solution(mesh):
    deep = max(1, mesh.shape["leaf"] // 4)
    sizes = (mesh.shape["top"] // 2, 2, mesh.shape["leaf"] // deep, deep)
    fine = jax.sharding.Mesh(mesh.devices.reshape(sizes), ("y", "core", "x", "z"))
    top, both = ("y", "core"), ("y", "core", "x", "z")
    return jax.shard_map(
        body,
        mesh=fine,
        in_specs=(
            P(both, None, None),
            P(both, None, None),
            P(both, None),
            P(both, None),
            P(both, None),
            P(both, None, None),
            P(both, None, None),
            P(both, None, None),
            P(top, None, None),
            P(both, None),
            P(both, None),
            P(both, None),
            P(top, None),
            P(both, None),
            P(both, None),
            P(both, None),
            P(top, None),
            P(both, None),
            P(both, None),
            P(both, None),
            P(both, None, None),
        ),
        out_specs=P(both, None, None),
        check_vma=False,
    )
```

```python
import jax
import jax.numpy as jnp
from jax import lax
from jax.experimental import pallas as pl
from jax.experimental.pallas import tpu as pltpu
from jax.sharding import PartitionSpec as P

RANK = 32
COLS = 128
QUADS = 4
ROWS8 = 8
F32 = jnp.float32
BF16 = jnp.bfloat16
VMEM_LIMIT = 32 * 1024 * 1024
ALMOST_ALL = 60 * 1024 * 1024


def split(x):
    high = x.astype(BF16)
    return high, (x - high.astype(F32)).astype(BF16)


def dot(a, b, contract=((1,), (0,))):
    return lax.dot_general(a, b, (contract, ((), ())), preferred_element_type=F32)


def dot_split(a, b_high, b_low):
    rows = a.shape[0]
    a_high, a_low = split(a)
    both = dot(jnp.concatenate([a_high, a_low], axis=0), b_high)
    return both[:rows] + both[rows:] + dot(a_high, b_low)


def dot_first(a, b):
    a_high, a_low = split(a)
    b_high, b_low = split(b)
    return dot(
        jnp.concatenate([a_high, a_high, a_low], axis=0),
        jnp.concatenate([b_high, b_low, b_high], axis=0),
        ((0,), (0,)),
    )


def lanes(rows=ROWS8):
    return lax.broadcasted_iota(jnp.int32, (rows, COLS), 1)


def square(flat):
    return jnp.concatenate([flat[:, RANK * q : RANK * (q + 1)] for q in range(QUADS)], axis=0)


def beside(flats):
    group = lanes() // RANK
    rows = []
    for q in range(QUADS):
        row = None
        for k, flat in enumerate(flats):
            shift = (RANK * (k - q)) % COLS
            moved = pltpu.roll(flat, shift, 1) if shift else flat
            row = moved if row is None else jnp.where(group == k, moved, row)
        rows.append(row)
    return jnp.concatenate(rows, axis=0)


def quad_rows(ref, start):
    return jnp.concatenate(
        [ref[pl.ds(start + q, ROWS8, stride=QUADS), :] for q in range(QUADS)], axis=0
    )


def store_natural(ref, start, x):
    for q in range(QUADS):
        ref[pl.ds(start + q, ROWS8, stride=QUADS), :] = x[ROWS8 * q : ROWS8 * (q + 1)]


def weights(couple, down, top, list_d, mask_d, list_t, mask_t, natural):
    slots, top_slots = list_d.shape[1], list_t.shape[1]
    flats = [couple[ROWS8 * k : ROWS8 * (k + 1), :] * mask_d[0, k].astype(F32) for k in range(slots)]
    lane = lanes(RANK)
    ids = jnp.zeros((RANK, COLS), F32)
    for k in range(slots):
        ids = jnp.where(lane == 64 + k, list_d[0, k].astype(F32), ids)
    for k in range(top_slots):
        ids = jnp.where(lane == 64 + slots + k, list_t[0, k].astype(F32), ids)
    tops = [
        top[pl.ds(k, ROWS8, stride=top_slots), :] * mask_t[0, k].astype(F32) for k in range(top_slots)
    ]
    store_natural(natural, 0, beside(tops))
    top_high, top_low = split(natural[...])
    return (
        beside(flats[:4]),
        jnp.where(lane < 64, beside(flats[4:]), ids),
        dot_split(square(down[...]), top_high, top_low),
    )


def first_kernel(*refs):
    count = 12
    sources, (weight_ref, stack_ref, send_ref), scratch = refs[:count], refs[count : count + 3], refs[count + 3 :]
    held, (sems, traction, traction_sems, natural) = scratch[:count - 1], scratch[count - 1 :]
    copies = [pltpu.make_async_copy(s, h, sems.at[n]) for n, (s, h) in enumerate(zip(sources[1:], held))]
    leaves = sources[0].shape[0]
    pairs = leaves // 2
    tractions = [
        pltpu.make_async_copy(sources[0].at[i], traction.at[i], traction_sems.at[i]) for i in range(leaves)
    ]
    for copy in copies + tractions:
        copy.start()
    couple, down, top, list_d, mask_d, list_t, mask_t, basis, up_leaf, up_pair, up_device = held
    for copy in copies:
        copy.wait()
    for n, block in enumerate(weights(couple, down, top, list_d, mask_d, list_t, mask_t, natural)):
        for t in range(weight_ref.shape[0]):
            weight_ref[t, RANK * n : RANK * (n + 1), :] = block
    for i in range(leaves):
        tractions[i].wait()
        high, low = split(traction[i])
        stack_ref[RANK * i : RANK * (i + 1), :] = dot_split(basis[i], high, low)
    for p in range(pairs):
        weight = [square(up_leaf[pl.ds(i, ROWS8, stride=leaves), :]) for i in (2 * p, 2 * p + 1)]
        value = [quad_rows(stack_ref, RANK * i) for i in (2 * p, 2 * p + 1)]
        at = RANK * (leaves + p)
        stack_ref[at : at + RANK, :] = dot_first(
            jnp.concatenate(weight, axis=0), jnp.concatenate(value, axis=0)
        )
    weight = [square(up_pair[pl.ds(p, ROWS8, stride=pairs), :]) for p in range(pairs)]
    value = [quad_rows(stack_ref, RANK * (leaves + p)) for p in range(pairs)]
    coeff = dot_first(jnp.concatenate(weight, axis=0), jnp.concatenate(value, axis=0))
    up = up_device[...]
    for z in range(send_ref.shape[0]):
        send_ref[z, 0:RANK, :] = coeff
        send_ref[z, RANK : RANK + ROWS8, :] = up


def far_kernel(
    low_ref, own_ref, high_ref, couple_leaf, couple_pair, down_leaf, down_pair, basis,
    list_leaf, mask_leaf, list_pair, mask_pair, fixed_ref, slope_ref, near_high, near_low, natural,
):
    leaves, slots = list_leaf.shape
    pairs = list_pair.shape[0]
    blocks = leaves + pairs
    top = lax.axis_index("y") * lax.axis_size("core") + lax.axis_index("core")
    leaf = lax.axis_index("x") * lax.axis_size("z") + lax.axis_index("z")
    position = top * (lax.axis_size("x") * lax.axis_size("z")) + leaf
    size = blocks * RANK
    for n, ref in enumerate((low_ref, own_ref, high_ref)):
        high, low = split(ref[...])
        near_high[n * size : (n + 1) * size, :] = high
        near_low[n * size : (n + 1) * size, :] = low
    none = jnp.zeros((RANK, COLS), BF16)
    near_high[3 * size : 3 * size + RANK, :] = none
    near_low[3 * size : 3 * size + RANK, :] = none

    def near(index, mask, per_dev, offset):
        relative = index - position * per_dev + per_dev
        block = relative // per_dev * blocks + offset + relative % per_dev
        start = pl.multiple_of(jnp.where(mask == 0, 3 * blocks, block) * RANK, RANK)
        return near_high[pl.ds(start, RANK), :], near_low[pl.ds(start, RANK), :]

    for p in range(pairs):
        flats = [couple_pair[pl.ds(k * ROWS8 * pairs + p, ROWS8, stride=pairs), :] for k in range(slots)]
        weight = jnp.concatenate([beside(flats[:4]), beside(flats[4:])], axis=1)
        taken = [near(list_pair[p, k], mask_pair[p, k], pairs, leaves) for k in range(slots)]
        rows = [jnp.concatenate([t[n] for t in taken] + [none, none], axis=0) for n in (0, 1)]
        at = 2 * RANK * p
        store_natural(natural, at, dot_split(weight, *rows))
        store_natural(natural, at + RANK, beside([down_pair[pl.ds(p, ROWS8, stride=pairs), :]] * 4))
        sums = split(natural[at : at + RANK, :])
        downs = split(natural[at + RANK : at + 2 * RANK, :])
        for i in (2 * p, 2 * p + 1):
            flats = [
                couple_leaf[pl.ds(k * ROWS8 * leaves + i, ROWS8, stride=leaves), :] for k in range(slots)
            ] + [down_leaf[pl.ds(i, ROWS8, stride=leaves), :]]
            weight = jnp.concatenate([beside(flats[:4]), beside(flats[4:])], axis=1)
            taken = [near(list_leaf[i, k], mask_leaf[i, k], leaves, 0) for k in range(slots)]
            rows = [
                jnp.concatenate(
                    [
                        jnp.concatenate([t[n] for t in taken] + [sums[n], none], axis=0),
                        jnp.concatenate([none] * slots + [downs[n], none], axis=0),
                    ],
                    axis=1,
                )
                for n in (0, 1)
            ]
            here = dot_split(weight, *rows)
            at = 2 * RANK * (pairs + i)
            store_natural(natural, at, here[:, :COLS])
            store_natural(natural, at + RANK, here[:, COLS:])
            here = jnp.concatenate([natural[at : at + RANK, :], natural[at + RANK : at + 2 * RANK, :]], axis=1)
            both = dot_first(basis[i], here)
            fixed_ref[i] = both[:, :COLS]
            slope = both[:, COLS:]
            slope_high = slope.astype(BF16).astype(F32)
            lane = lanes(slope.shape[0])
            slope_ref[i] = jnp.where(
                lane < 64, slope_high, jnp.where(lane < 96, slope - slope_high, 0.0)
            ).astype(BF16)


def part_kernel(
    coeff_ref, weight_own, weight_other, ids_own, ids_other, out_ref, coeff_high, coeff_low, gathered
):
    rows_y = weight_own.shape[0]
    subs = coeff_ref.shape[0]
    slots, top_slots = 6, 4
    core = lax.axis_index("core")
    group = lax.axis_index("y") * 2 + core
    none = jnp.zeros((RANK, COLS), BF16)
    for d in range(subs):
        value = coeff_ref[d, 0:RANK, :]
        gathered[RANK * d : RANK * (d + 1), :] = value
        high, low = split(value)
        coeff_high[RANK * d : RANK * (d + 1), :] = high
        coeff_low[RANK * d : RANK * (d + 1), :] = low
    coeff_high[RANK * subs : RANK * (subs + 1), :] = none
    coeff_low[RANK * subs : RANK * (subs + 1), :] = none
    up = jnp.concatenate([coeff_ref[d, RANK : RANK + ROWS8, :] for d in range(subs)], axis=0)
    value = jnp.concatenate(
        [gathered[pl.ds(q, ROWS8 * subs, stride=QUADS), :] for q in range(QUADS)], axis=1
    )
    every = dot_first(up, value)
    top = jnp.zeros((RANK, COLS), F32)
    for q in range(QUADS):
        top = top + every[RANK * q : RANK * (q + 1), COLS * q : COLS * (q + 1)]
    lane_group = lanes(RANK) // RANK
    targets = [(w, ids, n, y) for n, (w, ids) in enumerate(((weight_own, ids_own), (weight_other, ids_other))) for y in range(rows_y)]
    top_weight = []
    for weight_ref, ids_ref, _, y in targets:
        used = jnp.zeros((RANK, COLS), F32)
        for k in range(top_slots):
            owner = ids_ref[y, 64 + slots + k].astype(jnp.int32)
            used = jnp.where(lane_group == k, jnp.where(owner == group, 1.0, 0.0), used)
        top_weight.append(weight_ref[y, 2 * RANK : 3 * RANK, :] * used)
    top_high, top_low = split(top)
    top_part = dot_split(
        jnp.concatenate(top_weight, axis=0),
        jnp.concatenate([top_high] * 4, axis=0),
        jnp.concatenate([top_low] * 4, axis=0),
    )

    def starts(ids_ref, y):
        found = []
        for k in range(slots):
            index = ids_ref[y, 64 + k].astype(jnp.int32)
            block = jnp.where(index // subs == group, index % subs, subs)
            found.append(pl.multiple_of(block * RANK, RANK))
        return found

    for t in range(0, len(targets), 2):
        two = targets[t : t + 2]
        pair = [starts(ids_ref, y) for _, ids_ref, _, y in two]
        rows = [
            jnp.concatenate(
                [jnp.concatenate([ref[pl.ds(s, RANK), :] for s in one], axis=0) for one in pair], axis=1
            )
            for ref in (coeff_high, coeff_low)
        ]
        weight = [
            jnp.concatenate([w[y, 0:RANK, :], w[y, RANK : 2 * RANK, :64]], axis=1) for w, _, _, y in two
        ]
        both = dot_split(jnp.concatenate(weight, axis=0), *rows)
        for n, (_, _, other, y) in enumerate(two):
            at = 2 * y + (1 - core if other else core)
            mine = both[RANK * n : RANK * (n + 1), COLS * n : COLS * (n + 1)]
            out_ref[at] = mine + top_part[RANK * (t + n) : RANK * (t + n + 1)]


def last_kernel(parts_ref, fixed_ref, slope_ref, out_ref, natural):
    total = parts_ref[0]
    for t in range(1, parts_ref.shape[0]):
        total = total + parts_ref[t]
    store_natural(natural, 0, total)
    high, low = split(natural[...])
    rows = jnp.concatenate([high, low, high, jnp.zeros((RANK, COLS), BF16)], axis=0)
    for i in range(out_ref.shape[0]):
        out_ref[i] = fixed_ref[i] + dot(slope_ref[i], rows)


def whole(kernel, out, args, smem=(), hbm=(), scratch=(), flops=0, limit=VMEM_LIMIT):
    vmem = pl.BlockSpec(memory_space=pltpu.VMEM)
    scalars = pl.BlockSpec(memory_space=pltpu.SMEM)
    far = pl.BlockSpec(memory_space=pltpu.HBM)
    size = sum(a.size * a.dtype.itemsize for a in args)
    outs = out if isinstance(out, tuple) else (out,)
    size += sum(o.size * o.dtype.itemsize for o in outs)
    return pl.pallas_call(
        kernel,
        out_shape=out,
        in_specs=[scalars if n in smem else far if n in hbm else vmem for n in range(len(args))],
        out_specs=tuple(vmem for _ in out) if isinstance(out, tuple) else vmem,
        scratch_shapes=list(scratch),
        compiler_params=pltpu.CompilerParams(vmem_limit_bytes=limit),
        cost_estimate=pl.CostEstimate(flops=flops, bytes_accessed=size, transcendentals=0),
    )(*args)


def rows_of(x):
    if x.ndim == 2:
        return x.reshape(x.shape[0], ROWS8, COLS).transpose(1, 0, 2).reshape(-1, COLS)
    return x.reshape(x.shape[0], x.shape[1], ROWS8, COLS).transpose(1, 2, 0, 3).reshape(-1, COLS)


def body(
    traction_vectors,
    row_basis,
    up_leaf,
    up_pair,
    up_device,
    couple_leaf,
    pair_coupling_blocks,
    couple_device,
    couple_top,
    list_leaf,
    list_pair,
    list_device,
    list_top,
    mask_leaf,
    mask_pair,
    mask_device,
    mask_top,
    down_leaf,
    down_pair,
    down_device,
    col_basis,
):
    def shape(*dims, dtype=F32):
        return jax.ShapeDtypeStruct(dims, dtype)

    leaves, entries, _ = traction_vectors.shape
    blocks = leaves + leaves // 2
    targets = lax.axis_size("y")
    subs = lax.axis_size("x") * lax.axis_size("z")
    first = (
        traction_vectors, rows_of(couple_device), rows_of(down_device), rows_of(couple_top[0]),
        list_device, mask_device, list_top, mask_top,
        row_basis, rows_of(up_leaf), rows_of(up_pair), rows_of(up_device),
    )
    scalars = (4, 5, 6, 7)
    held = [
        (pltpu.SMEM if n in scalars else pltpu.VMEM)(a.shape, a.dtype) for n, a in enumerate(first) if n
    ]
    weights, stack, send = whole(
        first_kernel,
        (shape(targets, 3 * RANK, COLS), shape(blocks * RANK, COLS), shape(subs, RANK + ROWS8, COLS)),
        first,
        hbm=range(len(first)),
        scratch=[
            *held,
            pltpu.SemaphoreType.DMA((len(held),)),
            pltpu.VMEM(traction_vectors.shape, F32),
            pltpu.SemaphoreType.DMA((leaves,)),
            pltpu.VMEM((RANK, COLS), F32),
        ],
        flops=6 * 10**7,
        limit=ALMOST_ALL,
    )
    weights = lax.all_to_all(weights, "y", 0, 0, tiled=True)
    coeffs = lax.all_to_all(send, ("x", "z"), 0, 0, tiled=True)
    leaf_axes = ("x", "z")
    low = lax.ppermute(stack, leaf_axes, [(i, i + 1) for i in range(subs - 1)])
    high = lax.ppermute(stack, leaf_axes, [(i + 1, i) for i in range(subs - 1)])
    other = lax.ppermute(weights, "core", [(0, 1), (1, 0)])
    coeffs, low, high = lax.optimization_barrier((coeffs, low, high))
    near = pltpu.VMEM(((3 * blocks + 1) * RANK, COLS), BF16)
    fixed, slope = whole(
        far_kernel,
        (shape(leaves, entries, COLS), shape(leaves, entries, COLS, dtype=BF16)),
        (
            low, stack, high, rows_of(couple_leaf), rows_of(pair_coupling_blocks),
            rows_of(down_leaf), rows_of(down_pair), col_basis,
            list_leaf, mask_leaf, list_pair, mask_pair,
        ),
        smem=(8, 9, 10, 11),
        scratch=[near, near, pltpu.VMEM((2 * RANK * blocks, COLS), F32)],
        flops=10**8,
    )
    parts = whole(
        part_kernel,
        shape(2 * targets, RANK, COLS),
        (coeffs, weights, other, weights[:, RANK, :], other[:, RANK, :]),
        smem=(3, 4),
        scratch=[
            pltpu.VMEM(((subs + 1) * RANK, COLS), BF16),
            pltpu.VMEM(((subs + 1) * RANK, COLS), BF16),
            pltpu.VMEM((subs * RANK, COLS), F32),
        ],
        flops=10**8,
    )
    parts = lax.all_to_all(parts, ("y", "core"), 0, 0, tiled=True)
    return whole(
        last_kernel,
        shape(leaves, entries, COLS),
        (parts, fixed, slope),
        scratch=[pltpu.VMEM((RANK, COLS), F32)],
        flops=5 * 10**7,
    )


def solution(mesh):
    deep = max(1, mesh.shape["leaf"] // 4)
    sizes = (mesh.shape["top"] // 2, 2, mesh.shape["leaf"] // deep, deep)
    fine = jax.sharding.Mesh(mesh.devices.reshape(sizes), ("y", "core", "x", "z"))
    top, both = ("y", "core"), ("y", "core", "x", "z")
    return jax.shard_map(
        body,
        mesh=fine,
        in_specs=(
            P(both, None, None),
            P(both, None, None),
            P(both, None),
            P(both, None),
            P(both, None),
            P(both, None, None),
            P(both, None, None),
            P(both, None, None),
            P(top, None, None),
            P(both, None),
            P(both, None),
            P(both, None),
            P(top, None),
            P(both, None),
            P(both, None),
            P(both, None),
            P(top, None),
            P(both, None),
            P(both, None),
            P(both, None),
            P(both, None, None),
        ),
        out_specs=P(both, None, None),
        check_vma=False,
    )
```

```python
import jax
import jax.numpy as jnp
from jax import lax
from jax.experimental import pallas as pl
from jax.experimental.pallas import tpu as pltpu
from jax.sharding import PartitionSpec as P

RANK = 32
COLS = 128
QUADS = 4
ROWS8 = 8
F32 = jnp.float32
BF16 = jnp.bfloat16
VMEM_LIMIT = 32 * 1024 * 1024
ALMOST_ALL = 60 * 1024 * 1024


def split(x):
    high = x.astype(BF16)
    return high, (x - high.astype(F32)).astype(BF16)


def dot(a, b, contract=((1,), (0,))):
    return lax.dot_general(a, b, (contract, ((), ())), preferred_element_type=F32)


def dot_split(a, b_high, b_low):
    rows = a.shape[0]
    a_high, a_low = split(a)
    both = dot(jnp.concatenate([a_high, a_low], axis=0), b_high)
    return both[:rows] + both[rows:] + dot(a_high, b_low)


def dot_first(a, b):
    a_high, a_low = split(a)
    b_high, b_low = split(b)
    return dot(
        jnp.concatenate([a_high, a_high, a_low], axis=0),
        jnp.concatenate([b_high, b_low, b_high], axis=0),
        ((0,), (0,)),
    )


def lanes(rows=ROWS8):
    return lax.broadcasted_iota(jnp.int32, (rows, COLS), 1)


def square(flat):
    return jnp.concatenate([flat[:, RANK * q : RANK * (q + 1)] for q in range(QUADS)], axis=0)


def beside(flats):
    group = lanes() // RANK
    rows = []
    for q in range(QUADS):
        row = None
        for k, flat in enumerate(flats):
            shift = (RANK * (k - q)) % COLS
            moved = pltpu.roll(flat, shift, 1) if shift else flat
            row = moved if row is None else jnp.where(group == k, moved, row)
        rows.append(row)
    return jnp.concatenate(rows, axis=0)


def quad_rows(ref, start):
    return jnp.concatenate(
        [ref[pl.ds(start + q, ROWS8, stride=QUADS), :] for q in range(QUADS)], axis=0
    )


def store_natural(ref, start, x):
    for q in range(QUADS):
        ref[pl.ds(start + q, ROWS8, stride=QUADS), :] = x[ROWS8 * q : ROWS8 * (q + 1)]


def weights(couple, down, top, list_d, mask_d, list_t, mask_t, natural):
    slots, top_slots = list_d.shape[1], list_t.shape[1]
    flats = [couple[ROWS8 * k : ROWS8 * (k + 1), :] * mask_d[0, k].astype(F32) for k in range(slots)]
    lane = lanes(RANK)
    ids = jnp.zeros((RANK, COLS), F32)
    for k in range(slots):
        ids = jnp.where(lane == 64 + k, list_d[0, k].astype(F32), ids)
    for k in range(top_slots):
        ids = jnp.where(lane == 64 + slots + k, list_t[0, k].astype(F32), ids)
    tops = [
        top[pl.ds(k, ROWS8, stride=top_slots), :] * mask_t[0, k].astype(F32) for k in range(top_slots)
    ]
    store_natural(natural, 0, beside(tops))
    top_high, top_low = split(natural[...])
    return (
        beside(flats[:4]),
        jnp.where(lane < 64, beside(flats[4:]), ids),
        dot_split(square(down[...]), top_high, top_low),
    )


def first_kernel(*refs):
    count = 12
    sources, (weight_ref, stack_ref, send_ref), scratch = refs[:count], refs[count : count + 3], refs[count + 3 :]
    held, (sems, traction, traction_sems, natural) = scratch[:count - 1], scratch[count - 1 :]
    copies = [pltpu.make_async_copy(s, h, sems.at[n]) for n, (s, h) in enumerate(zip(sources[1:], held))]
    leaves = sources[0].shape[0]
    pairs = leaves // 2
    tractions = [
        pltpu.make_async_copy(sources[0].at[i], traction.at[i], traction_sems.at[i]) for i in range(leaves)
    ]
    for copy in copies + tractions:
        copy.start()
    couple, down, top, list_d, mask_d, list_t, mask_t, basis, up_leaf, up_pair, up_device = held
    for copy in copies:
        copy.wait()
    for n, block in enumerate(weights(couple, down, top, list_d, mask_d, list_t, mask_t, natural)):
        weight_ref[0, RANK * n : RANK * (n + 1), :] = block
    for i in range(leaves):
        tractions[i].wait()
        high, low = split(traction[i])
        stack_ref[RANK * i : RANK * (i + 1), :] = dot_split(basis[i], high, low)
    for p in range(pairs):
        weight = [square(up_leaf[pl.ds(i, ROWS8, stride=leaves), :]) for i in (2 * p, 2 * p + 1)]
        value = [quad_rows(stack_ref, RANK * i) for i in (2 * p, 2 * p + 1)]
        at = RANK * (leaves + p)
        stack_ref[at : at + RANK, :] = dot_first(
            jnp.concatenate(weight, axis=0), jnp.concatenate(value, axis=0)
        )
    weight = [square(up_pair[pl.ds(p, ROWS8, stride=pairs), :]) for p in range(pairs)]
    value = [quad_rows(stack_ref, RANK * (leaves + p)) for p in range(pairs)]
    coeff = dot_first(jnp.concatenate(weight, axis=0), jnp.concatenate(value, axis=0))
    up = up_device[...]
    for z in range(send_ref.shape[0]):
        send_ref[z, 0:RANK, :] = coeff
        send_ref[z, RANK : RANK + ROWS8, :] = up


def far_kernel(
    low_ref, own_ref, high_ref, couple_leaf, couple_pair, down_leaf, down_pair, basis,
    list_leaf, mask_leaf, list_pair, mask_pair, fixed_ref, slope_ref, near_high, near_low, natural,
):
    leaves, slots = list_leaf.shape
    pairs = list_pair.shape[0]
    blocks = leaves + pairs
    top = lax.axis_index("y") * lax.axis_size("core") + lax.axis_index("core")
    leaf = lax.axis_index("x") * lax.axis_size("z") + lax.axis_index("z")
    position = top * (lax.axis_size("x") * lax.axis_size("z")) + leaf
    size = blocks * RANK
    for n, ref in enumerate((low_ref, own_ref, high_ref)):
        high, low = split(ref[...])
        near_high[n * size : (n + 1) * size, :] = high
        near_low[n * size : (n + 1) * size, :] = low
    none = jnp.zeros((RANK, COLS), BF16)
    near_high[3 * size : 3 * size + RANK, :] = none
    near_low[3 * size : 3 * size + RANK, :] = none

    def near(index, mask, per_dev, offset):
        relative = index - position * per_dev + per_dev
        block = relative // per_dev * blocks + offset + relative % per_dev
        start = pl.multiple_of(jnp.where(mask == 0, 3 * blocks, block) * RANK, RANK)
        return near_high[pl.ds(start, RANK), :], near_low[pl.ds(start, RANK), :]

    for p in range(pairs):
        flats = [couple_pair[pl.ds(k * ROWS8 * pairs + p, ROWS8, stride=pairs), :] for k in range(slots)]
        weight = jnp.concatenate([beside(flats[:4]), beside(flats[4:])], axis=1)
        taken = [near(list_pair[p, k], mask_pair[p, k], pairs, leaves) for k in range(slots)]
        rows = [jnp.concatenate([t[n] for t in taken] + [none, none], axis=0) for n in (0, 1)]
        at = 2 * RANK * p
        store_natural(natural, at, dot_split(weight, *rows))
        store_natural(natural, at + RANK, beside([down_pair[pl.ds(p, ROWS8, stride=pairs), :]] * 4))
        sums = split(natural[at : at + RANK, :])
        downs = split(natural[at + RANK : at + 2 * RANK, :])
        for i in (2 * p, 2 * p + 1):
            flats = [
                couple_leaf[pl.ds(k * ROWS8 * leaves + i, ROWS8, stride=leaves), :] for k in range(slots)
            ] + [down_leaf[pl.ds(i, ROWS8, stride=leaves), :]]
            weight = jnp.concatenate([beside(flats[:4]), beside(flats[4:])], axis=1)
            taken = [near(list_leaf[i, k], mask_leaf[i, k], leaves, 0) for k in range(slots)]
            rows = [
                jnp.concatenate(
                    [
                        jnp.concatenate([t[n] for t in taken] + [sums[n], none], axis=0),
                        jnp.concatenate([none] * slots + [downs[n], none], axis=0),
                    ],
                    axis=1,
                )
                for n in (0, 1)
            ]
            here = dot_split(weight, *rows)
            at = 2 * RANK * (pairs + i)
            store_natural(natural, at, here[:, :COLS])
            store_natural(natural, at + RANK, here[:, COLS:])
            here = jnp.concatenate([natural[at : at + RANK, :], natural[at + RANK : at + 2 * RANK, :]], axis=1)
            both = dot_first(basis[i], here)
            fixed_ref[i] = both[:, :COLS]
            slope = both[:, COLS:]
            slope_high = slope.astype(BF16).astype(F32)
            lane = lanes(slope.shape[0])
            slope_ref[i] = jnp.where(
                lane < 64, slope_high, jnp.where(lane < 96, slope - slope_high, 0.0)
            ).astype(BF16)


def steps(count):
    found = []
    while count > 1:
        count //= 2
        found.append(count)
    return found


def part_kernel(
    coeff_ref, weight_own, weight_other, ids_own, ids_other, out_ref, coeff_high, coeff_low, gathered
):
    rows_y = weight_own.shape[0]
    subs = coeff_ref.shape[0]
    slots, top_slots = 6, 4
    core, row = lax.axis_index("core"), lax.axis_index("y")
    group = row * 2 + core
    back = [0]
    for step in steps(rows_y):
        back = back + [b + step for b in back]
    none = jnp.zeros((RANK, COLS), BF16)
    for d in range(subs):
        value = coeff_ref[d, 0:RANK, :]
        gathered[RANK * d : RANK * (d + 1), :] = value
        high, low = split(value)
        coeff_high[RANK * d : RANK * (d + 1), :] = high
        coeff_low[RANK * d : RANK * (d + 1), :] = low
    coeff_high[RANK * subs : RANK * (subs + 1), :] = none
    coeff_low[RANK * subs : RANK * (subs + 1), :] = none
    up = jnp.concatenate([coeff_ref[d, RANK : RANK + ROWS8, :] for d in range(subs)], axis=0)
    value = jnp.concatenate(
        [gathered[pl.ds(q, ROWS8 * subs, stride=QUADS), :] for q in range(QUADS)], axis=1
    )
    every = dot_first(up, value)
    top = jnp.zeros((RANK, COLS), F32)
    for q in range(QUADS):
        top = top + every[RANK * q : RANK * (q + 1), COLS * q : COLS * (q + 1)]
    lane_group = lanes(RANK) // RANK
    targets = [(w, ids, n, y) for n, (w, ids) in enumerate(((weight_own, ids_own), (weight_other, ids_other))) for y in range(rows_y)]
    top_weight = []
    for weight_ref, ids_ref, _, y in targets:
        used = jnp.zeros((RANK, COLS), F32)
        for k in range(top_slots):
            owner = ids_ref[y, 64 + slots + k].astype(jnp.int32)
            used = jnp.where(lane_group == k, jnp.where(owner == group, 1.0, 0.0), used)
        top_weight.append(weight_ref[y, 2 * RANK : 3 * RANK, :] * used)
    top_high, top_low = split(top)
    top_part = dot_split(
        jnp.concatenate(top_weight, axis=0),
        jnp.concatenate([top_high] * 4, axis=0),
        jnp.concatenate([top_low] * 4, axis=0),
    )

    def starts(ids_ref, y):
        found = []
        for k in range(slots):
            index = ids_ref[y, 64 + k].astype(jnp.int32)
            block = jnp.where(index // subs == group, index % subs, subs)
            found.append(pl.multiple_of(block * RANK, RANK))
        return found

    for t in range(0, len(targets), 2):
        two = targets[t : t + 2]
        pair = [starts(ids_ref, y) for _, ids_ref, _, y in two]
        rows = [
            jnp.concatenate(
                [jnp.concatenate([ref[pl.ds(s, RANK), :] for s in one], axis=0) for one in pair], axis=1
            )
            for ref in (coeff_high, coeff_low)
        ]
        weight = [
            jnp.concatenate([w[y, 0:RANK, :], w[y, RANK : 2 * RANK, :64]], axis=1) for w, _, _, y in two
        ]
        both = dot_split(jnp.concatenate(weight, axis=0), *rows)
        for n, (_, _, other, y) in enumerate(two):
            at = 2 * ((row + rows_y - back[y]) % rows_y) + (1 - core if other else core)
            mine = both[RANK * n : RANK * (n + 1), COLS * n : COLS * (n + 1)]
            out_ref[at] = mine + top_part[RANK * (t + n) : RANK * (t + n + 1)]


def last_kernel(parts_ref, fixed_ref, slope_ref, out_ref, natural):
    total = parts_ref[0]
    for t in range(1, parts_ref.shape[0]):
        total = total + parts_ref[t]
    store_natural(natural, 0, total)
    high, low = split(natural[...])
    rows = jnp.concatenate([high, low, high, jnp.zeros((RANK, COLS), BF16)], axis=0)
    for i in range(out_ref.shape[0]):
        out_ref[i] = fixed_ref[i] + dot(slope_ref[i], rows)


def whole(kernel, out, args, smem=(), hbm=(), scratch=(), flops=0, limit=VMEM_LIMIT):
    vmem = pl.BlockSpec(memory_space=pltpu.VMEM)
    scalars = pl.BlockSpec(memory_space=pltpu.SMEM)
    far = pl.BlockSpec(memory_space=pltpu.HBM)
    size = sum(a.size * a.dtype.itemsize for a in args)
    outs = out if isinstance(out, tuple) else (out,)
    size += sum(o.size * o.dtype.itemsize for o in outs)
    return pl.pallas_call(
        kernel,
        out_shape=out,
        in_specs=[scalars if n in smem else far if n in hbm else vmem for n in range(len(args))],
        out_specs=tuple(vmem for _ in out) if isinstance(out, tuple) else vmem,
        scratch_shapes=list(scratch),
        compiler_params=pltpu.CompilerParams(vmem_limit_bytes=limit),
        cost_estimate=pl.CostEstimate(flops=flops, bytes_accessed=size, transcendentals=0),
    )(*args)


def rows_of(x):
    if x.ndim == 2:
        return x.reshape(x.shape[0], ROWS8, COLS).transpose(1, 0, 2).reshape(-1, COLS)
    return x.reshape(x.shape[0], x.shape[1], ROWS8, COLS).transpose(1, 2, 0, 3).reshape(-1, COLS)


def body(
    traction_vectors,
    row_basis,
    up_leaf,
    up_pair,
    up_device,
    couple_leaf,
    pair_coupling_blocks,
    couple_device,
    couple_top,
    list_leaf,
    list_pair,
    list_device,
    list_top,
    mask_leaf,
    mask_pair,
    mask_device,
    mask_top,
    down_leaf,
    down_pair,
    down_device,
    col_basis,
):
    def shape(*dims, dtype=F32):
        return jax.ShapeDtypeStruct(dims, dtype)

    leaves, entries, _ = traction_vectors.shape
    blocks = leaves + leaves // 2
    targets = lax.axis_size("y")
    subs = lax.axis_size("x") * lax.axis_size("z")
    first = (
        traction_vectors, rows_of(couple_device), rows_of(down_device), rows_of(couple_top[0]),
        list_device, mask_device, list_top, mask_top,
        row_basis, rows_of(up_leaf), rows_of(up_pair), rows_of(up_device),
    )
    scalars = (4, 5, 6, 7)
    held = [
        (pltpu.SMEM if n in scalars else pltpu.VMEM)(a.shape, a.dtype) for n, a in enumerate(first) if n
    ]
    weights, stack, send = whole(
        first_kernel,
        (shape(1, 3 * RANK, COLS), shape(blocks * RANK, COLS), shape(subs, RANK + ROWS8, COLS)),
        first,
        hbm=range(len(first)),
        scratch=[
            *held,
            pltpu.SemaphoreType.DMA((len(held),)),
            pltpu.VMEM(traction_vectors.shape, F32),
            pltpu.SemaphoreType.DMA((leaves,)),
            pltpu.VMEM((RANK, COLS), F32),
        ],
        flops=6 * 10**7,
        limit=ALMOST_ALL,
    )
    for step in steps(targets):
        come = lax.ppermute(weights, "y", [(i, (i + step) % targets) for i in range(targets)])
        weights = jnp.concatenate([weights, come], axis=0)
    coeffs = lax.all_to_all(send, ("x", "z"), 0, 0, tiled=True)
    leaf_axes = ("x", "z")
    low = lax.ppermute(stack, leaf_axes, [(i, i + 1) for i in range(subs - 1)])
    high = lax.ppermute(stack, leaf_axes, [(i + 1, i) for i in range(subs - 1)])
    other = lax.ppermute(weights, "core", [(0, 1), (1, 0)])
    coeffs, low, high = lax.optimization_barrier((coeffs, low, high))
    near = pltpu.VMEM(((3 * blocks + 1) * RANK, COLS), BF16)
    fixed, slope = whole(
        far_kernel,
        (shape(leaves, entries, COLS), shape(leaves, entries, COLS, dtype=BF16)),
        (
            low, stack, high, rows_of(couple_leaf), rows_of(pair_coupling_blocks),
            rows_of(down_leaf), rows_of(down_pair), col_basis,
            list_leaf, mask_leaf, list_pair, mask_pair,
        ),
        smem=(8, 9, 10, 11),
        scratch=[near, near, pltpu.VMEM((2 * RANK * blocks, COLS), F32)],
        flops=10**8,
    )
    parts = whole(
        part_kernel,
        shape(2 * targets, RANK, COLS),
        (coeffs, weights, other, weights[:, RANK, :], other[:, RANK, :]),
        smem=(3, 4),
        scratch=[
            pltpu.VMEM(((subs + 1) * RANK, COLS), BF16),
            pltpu.VMEM(((subs + 1) * RANK, COLS), BF16),
            pltpu.VMEM((subs * RANK, COLS), F32),
        ],
        flops=10**8,
    )
    parts = lax.all_to_all(parts, ("y", "core"), 0, 0, tiled=True)
    return whole(
        last_kernel,
        shape(leaves, entries, COLS),
        (parts, fixed, slope),
        scratch=[pltpu.VMEM((RANK, COLS), F32)],
        flops=5 * 10**7,
    )


def solution(mesh):
    deep = max(1, mesh.shape["leaf"] // 4)
    sizes = (mesh.shape["top"] // 2, 2, mesh.shape["leaf"] // deep, deep)
    fine = jax.sharding.Mesh(mesh.devices.reshape(sizes), ("y", "core", "x", "z"))
    top, both = ("y", "core"), ("y", "core", "x", "z")
    return jax.shard_map(
        body,
        mesh=fine,
        in_specs=(
            P(both, None, None),
            P(both, None, None),
            P(both, None),
            P(both, None),
            P(both, None),
            P(both, None, None),
            P(both, None, None),
            P(both, None, None),
            P(top, None, None),
            P(both, None),
            P(both, None),
            P(both, None),
            P(top, None),
            P(both, None),
            P(both, None),
            P(both, None),
            P(top, None),
            P(both, None),
            P(both, None),
            P(both, None),
            P(both, None, None),
        ),
        out_specs=P(both, None, None),
        check_vma=False,
    )
```

```python
import jax
import jax.numpy as jnp
from jax import lax
from jax.experimental import pallas as pl
from jax.experimental.pallas import tpu as pltpu
from jax.sharding import PartitionSpec as P

RANK = 32
COLS = 128
QUADS = 4
ROWS8 = 8
F32 = jnp.float32
BF16 = jnp.bfloat16
VMEM_LIMIT = 32 * 1024 * 1024
ALMOST_ALL = 60 * 1024 * 1024


def split(x):
    high = x.astype(BF16)
    return high, (x - high.astype(F32)).astype(BF16)


def dot(a, b, contract=((1,), (0,))):
    return lax.dot_general(a, b, (contract, ((), ())), preferred_element_type=F32)


def dot_split(a, b_high, b_low):
    rows = a.shape[0]
    a_high, a_low = split(a)
    both = dot(jnp.concatenate([a_high, a_low], axis=0), b_high)
    return both[:rows] + both[rows:] + dot(a_high, b_low)


def dot_first(a, b):
    a_high, a_low = split(a)
    b_high, b_low = split(b)
    return dot(
        jnp.concatenate([a_high, a_high, a_low], axis=0),
        jnp.concatenate([b_high, b_low, b_high], axis=0),
        ((0,), (0,)),
    )


def lanes(rows=ROWS8):
    return lax.broadcasted_iota(jnp.int32, (rows, COLS), 1)


def square(flat):
    return jnp.concatenate([flat[:, RANK * q : RANK * (q + 1)] for q in range(QUADS)], axis=0)


def beside(flats):
    group = lanes() // RANK
    rows = []
    for q in range(QUADS):
        row = None
        for k, flat in enumerate(flats):
            shift = (RANK * (k - q)) % COLS
            moved = pltpu.roll(flat, shift, 1) if shift else flat
            row = moved if row is None else jnp.where(group == k, moved, row)
        rows.append(row)
    return jnp.concatenate(rows, axis=0)


def quad_rows(ref, start):
    return jnp.concatenate(
        [ref[pl.ds(start + q, ROWS8, stride=QUADS), :] for q in range(QUADS)], axis=0
    )


def store_natural(ref, start, x):
    for q in range(QUADS):
        ref[pl.ds(start + q, ROWS8, stride=QUADS), :] = x[ROWS8 * q : ROWS8 * (q + 1)]


def weights(couple, down, top, list_d, mask_d, list_t, mask_t, natural):
    slots, top_slots = list_d.shape[1], list_t.shape[1]
    flats = [couple[ROWS8 * k : ROWS8 * (k + 1), :] * mask_d[0, k].astype(F32) for k in range(slots)]
    lane = lanes(RANK)
    ids = jnp.zeros((RANK, COLS), F32)
    for k in range(slots):
        ids = jnp.where(lane == 64 + k, list_d[0, k].astype(F32), ids)
    for k in range(top_slots):
        ids = jnp.where(lane == 64 + slots + k, list_t[0, k].astype(F32), ids)
    tops = [
        top[pl.ds(k, ROWS8, stride=top_slots), :] * mask_t[0, k].astype(F32) for k in range(top_slots)
    ]
    store_natural(natural, 0, beside(tops))
    top_high, top_low = split(natural[...])
    return (
        beside(flats[:4]),
        jnp.where(lane < 64, beside(flats[4:]), ids),
        dot_split(square(down[...]), top_high, top_low),
    )


def first_kernel(*refs):
    count = 12
    sources, (weight_ref, stack_ref, send_ref), scratch = refs[:count], refs[count : count + 3], refs[count + 3 :]
    held, (sems, traction, traction_sems, natural) = scratch[:count - 1], scratch[count - 1 :]
    copies = [pltpu.make_async_copy(s, h, sems.at[n]) for n, (s, h) in enumerate(zip(sources[1:], held))]
    leaves = sources[0].shape[0]
    pairs = leaves // 2
    tractions = [
        pltpu.make_async_copy(sources[0].at[i], traction.at[i], traction_sems.at[i]) for i in range(leaves)
    ]
    for copy in copies + tractions:
        copy.start()
    couple, down, top, list_d, mask_d, list_t, mask_t, basis, up_leaf, up_pair, up_device = held
    for copy in copies:
        copy.wait()
    for n, block in enumerate(weights(couple, down, top, list_d, mask_d, list_t, mask_t, natural)):
        weight_ref[0, RANK * n : RANK * (n + 1), :] = block
    for i in range(leaves):
        tractions[i].wait()
        high, low = split(traction[i])
        stack_ref[RANK * i : RANK * (i + 1), :] = dot_split(basis[i], high, low)
    for p in range(pairs):
        weight = [square(up_leaf[pl.ds(i, ROWS8, stride=leaves), :]) for i in (2 * p, 2 * p + 1)]
        value = [quad_rows(stack_ref, RANK * i) for i in (2 * p, 2 * p + 1)]
        at = RANK * (leaves + p)
        stack_ref[at : at + RANK, :] = dot_first(
            jnp.concatenate(weight, axis=0), jnp.concatenate(value, axis=0)
        )
    weight = [square(up_pair[pl.ds(p, ROWS8, stride=pairs), :]) for p in range(pairs)]
    value = [quad_rows(stack_ref, RANK * (leaves + p)) for p in range(pairs)]
    coeff = dot_first(jnp.concatenate(weight, axis=0), jnp.concatenate(value, axis=0))
    up = up_device[...]
    for z in range(send_ref.shape[0]):
        send_ref[z, 0:RANK, :] = coeff
        send_ref[z, RANK : RANK + ROWS8, :] = up


def far_kernel(
    low_ref, own_ref, high_ref, couple_leaf, couple_pair, down_leaf, down_pair, basis,
    list_leaf, mask_leaf, list_pair, mask_pair, fixed_ref, slope_ref, near_high, near_low, natural,
):
    leaves, slots = list_leaf.shape
    pairs = list_pair.shape[0]
    blocks = leaves + pairs
    top = lax.axis_index("y") * lax.axis_size("core") + lax.axis_index("core")
    leaf = lax.axis_index("x") * lax.axis_size("z") + lax.axis_index("z")
    position = top * (lax.axis_size("x") * lax.axis_size("z")) + leaf
    size = blocks * RANK
    for n, ref in enumerate((low_ref, own_ref, high_ref)):
        high, low = split(ref[...])
        near_high[n * size : (n + 1) * size, :] = high
        near_low[n * size : (n + 1) * size, :] = low
    none = jnp.zeros((RANK, COLS), BF16)
    near_high[3 * size : 3 * size + RANK, :] = none
    near_low[3 * size : 3 * size + RANK, :] = none

    def near(index, mask, per_dev, offset):
        relative = index - position * per_dev + per_dev
        block = relative // per_dev * blocks + offset + relative % per_dev
        start = pl.multiple_of(jnp.where(mask == 0, 3 * blocks, block) * RANK, RANK)
        return near_high[pl.ds(start, RANK), :], near_low[pl.ds(start, RANK), :]

    for p in range(pairs):
        flats = [couple_pair[pl.ds(k * ROWS8 * pairs + p, ROWS8, stride=pairs), :] for k in range(slots)]
        weight = jnp.concatenate([beside(flats[:4]), beside(flats[4:])], axis=1)
        taken = [near(list_pair[p, k], mask_pair[p, k], pairs, leaves) for k in range(slots)]
        rows = [jnp.concatenate([t[n] for t in taken] + [none, none], axis=0) for n in (0, 1)]
        at = 2 * RANK * p
        store_natural(natural, at, dot_split(weight, *rows))
        store_natural(natural, at + RANK, beside([down_pair[pl.ds(p, ROWS8, stride=pairs), :]] * 4))
        sums = split(natural[at : at + RANK, :])
        downs = split(natural[at + RANK : at + 2 * RANK, :])
        for i in (2 * p, 2 * p + 1):
            flats = [
                couple_leaf[pl.ds(k * ROWS8 * leaves + i, ROWS8, stride=leaves), :] for k in range(slots)
            ] + [down_leaf[pl.ds(i, ROWS8, stride=leaves), :]]
            weight = jnp.concatenate([beside(flats[:4]), beside(flats[4:])], axis=1)
            taken = [near(list_leaf[i, k], mask_leaf[i, k], leaves, 0) for k in range(slots)]
            rows = [
                jnp.concatenate(
                    [
                        jnp.concatenate([t[n] for t in taken] + [sums[n], none], axis=0),
                        jnp.concatenate([none] * slots + [downs[n], none], axis=0),
                    ],
                    axis=1,
                )
                for n in (0, 1)
            ]
            here = dot_split(weight, *rows)
            at = 2 * RANK * (pairs + i)
            store_natural(natural, at, here[:, :COLS])
            store_natural(natural, at + RANK, here[:, COLS:])
            here = jnp.concatenate([natural[at : at + RANK, :], natural[at + RANK : at + 2 * RANK, :]], axis=1)
            both = dot_first(basis[i], here)
            fixed_ref[i] = both[:, :COLS]
            slope = both[:, COLS:]
            slope_high = slope.astype(BF16).astype(F32)
            lane = lanes(slope.shape[0])
            slope_ref[i] = jnp.where(
                lane < 64, slope_high, jnp.where(lane < 96, slope - slope_high, 0.0)
            ).astype(BF16)


def shifts(count):
    half = count // 2
    return [s if s <= half // 2 else s - half for s in range(1, half)]


def part_kernel(*refs):
    buffers = (len(refs) - 6) // 2
    coeff_own, coeff_other = refs[:2]
    weight_refs, ids_refs = refs[2 : 2 + buffers], refs[2 + buffers : 2 + 2 * buffers]
    out_ref, coeff_high, coeff_low, gathered = refs[2 + 2 * buffers :]
    subs = coeff_own.shape[0]
    rows_y = 2 * buffers
    slots, top_slots = 6, 4
    row, core = lax.axis_index("y"), lax.axis_index("core")
    none = jnp.zeros((RANK, COLS), BF16)
    blocks = [(ref, d) for ref in (coeff_own, coeff_other) for d in range(subs)]
    for n, (ref, d) in enumerate(blocks):
        value = ref[d, 0:RANK, :]
        gathered[RANK * n : RANK * (n + 1), :] = value
        high, low = split(value)
        coeff_high[RANK * n : RANK * (n + 1), :] = high
        coeff_low[RANK * n : RANK * (n + 1), :] = low
    coeff_high[2 * RANK * subs : RANK * (2 * subs + 1), :] = none
    coeff_low[2 * RANK * subs : RANK * (2 * subs + 1), :] = none
    tops = []
    for g in range(2):
        up = jnp.concatenate(
            [ref[d, RANK : RANK + ROWS8, :] for ref, d in blocks[g * subs : (g + 1) * subs]], axis=0
        )
        value = jnp.concatenate(
            [
                gathered[pl.ds(RANK * subs * g + q, ROWS8 * subs, stride=QUADS), :]
                for q in range(QUADS)
            ],
            axis=1,
        )
        every = dot_first(up, value)
        top = jnp.zeros((RANK, COLS), F32)
        for q in range(QUADS):
            top = top + every[RANK * q : RANK * (q + 1), COLS * q : COLS * (q + 1)]
        tops.append(split(top))
    lane_group = lanes(RANK) // RANK
    targets = []
    for weight_ref, ids_ref, shift in zip(weight_refs, ids_refs, [0] + shifts(rows_y)):
        targets += [(weight_ref, ids_ref, n, shift + n * buffers) for n in range(2)]
    top_weight = []
    for weight_ref, ids_ref, n, _ in targets:
        used = [jnp.zeros((RANK, COLS), F32)] * 2
        for k in range(top_slots):
            owner = ids_ref[n, 64 + slots + k].astype(jnp.int32)
            for g in range(2):
                group = row * 2 + (core if g == 0 else 1 - core)
                used[g] = jnp.where(lane_group == k, jnp.where(owner == group, 1.0, 0.0), used[g])
        block = weight_ref[n, 2 * RANK : 3 * RANK, :]
        top_weight.append(jnp.concatenate([block * used[0], block * used[1]], axis=1))
    top_part = dot_split(
        jnp.concatenate(top_weight, axis=0),
        jnp.concatenate([tops[0][0]] * 4 + [tops[1][0]] * 4, axis=0),
        jnp.concatenate([tops[0][1]] * 4 + [tops[1][1]] * 4, axis=0),
    )

    def starts(ids_ref, n):
        found = []
        for k in range(slots):
            index = ids_ref[n, 64 + k].astype(jnp.int32)
            group, sub = index // subs, index % subs
            place = sub + jnp.where(group % 2 == core, 0, subs)
            block = jnp.where(group // 2 == row, place, 2 * subs)
            found.append(pl.multiple_of(block * RANK, RANK))
        return found

    for t in range(0, rows_y, 2):
        two = targets[t : t + 2]
        pair = [starts(ids_ref, n) for _, ids_ref, n, _ in two]
        rows = [
            jnp.concatenate(
                [jnp.concatenate([ref[pl.ds(s, RANK), :] for s in one], axis=0) for one in pair], axis=1
            )
            for ref in (coeff_high, coeff_low)
        ]
        weight = [
            jnp.concatenate([w[n, 0:RANK, :], w[n, RANK : 2 * RANK, :64]], axis=1) for w, _, n, _ in two
        ]
        both = dot_split(jnp.concatenate(weight, axis=0), *rows)
        for m, (_, _, _, offset) in enumerate(two):
            at = (row + 2 * rows_y - offset) % rows_y
            mine = both[RANK * m : RANK * (m + 1), COLS * m : COLS * (m + 1)]
            out_ref[at] = mine + top_part[RANK * (t + m) : RANK * (t + m + 1)]


def last_kernel(parts_ref, fixed_ref, slope_ref, out_ref, natural):
    total = parts_ref[0]
    for t in range(1, parts_ref.shape[0]):
        total = total + parts_ref[t]
    store_natural(natural, 0, total)
    high, low = split(natural[...])
    rows = jnp.concatenate([high, low, high, jnp.zeros((RANK, COLS), BF16)], axis=0)
    for i in range(out_ref.shape[0]):
        out_ref[i] = fixed_ref[i] + dot(slope_ref[i], rows)


def whole(kernel, out, args, smem=(), hbm=(), scratch=(), flops=0, limit=VMEM_LIMIT):
    vmem = pl.BlockSpec(memory_space=pltpu.VMEM)
    scalars = pl.BlockSpec(memory_space=pltpu.SMEM)
    far = pl.BlockSpec(memory_space=pltpu.HBM)
    size = sum(a.size * a.dtype.itemsize for a in args)
    outs = out if isinstance(out, tuple) else (out,)
    size += sum(o.size * o.dtype.itemsize for o in outs)
    return pl.pallas_call(
        kernel,
        out_shape=out,
        in_specs=[scalars if n in smem else far if n in hbm else vmem for n in range(len(args))],
        out_specs=tuple(vmem for _ in out) if isinstance(out, tuple) else vmem,
        scratch_shapes=list(scratch),
        compiler_params=pltpu.CompilerParams(vmem_limit_bytes=limit),
        cost_estimate=pl.CostEstimate(flops=flops, bytes_accessed=size, transcendentals=0),
    )(*args)


def rows_of(x):
    if x.ndim == 2:
        return x.reshape(x.shape[0], ROWS8, COLS).transpose(1, 0, 2).reshape(-1, COLS)
    return x.reshape(x.shape[0], x.shape[1], ROWS8, COLS).transpose(1, 2, 0, 3).reshape(-1, COLS)


def body(
    traction_vectors,
    row_basis,
    up_leaf,
    up_pair,
    up_device,
    couple_leaf,
    pair_coupling_blocks,
    couple_device,
    couple_top,
    list_leaf,
    list_pair,
    list_device,
    list_top,
    mask_leaf,
    mask_pair,
    mask_device,
    mask_top,
    down_leaf,
    down_pair,
    down_device,
    col_basis,
):
    def shape(*dims, dtype=F32):
        return jax.ShapeDtypeStruct(dims, dtype)

    leaves, entries, _ = traction_vectors.shape
    blocks = leaves + leaves // 2
    targets = lax.axis_size("y")
    subs = lax.axis_size("x") * lax.axis_size("z")
    first = (
        traction_vectors, rows_of(couple_device), rows_of(down_device), rows_of(couple_top[0]),
        list_device, mask_device, list_top, mask_top,
        row_basis, rows_of(up_leaf), rows_of(up_pair), rows_of(up_device),
    )
    scalars = (4, 5, 6, 7)
    held = [
        (pltpu.SMEM if n in scalars else pltpu.VMEM)(a.shape, a.dtype) for n, a in enumerate(first) if n
    ]
    weights, stack, send = whole(
        first_kernel,
        (shape(1, 3 * RANK, COLS), shape(blocks * RANK, COLS), shape(subs, RANK + ROWS8, COLS)),
        first,
        hbm=range(len(first)),
        scratch=[
            *held,
            pltpu.SemaphoreType.DMA((len(held),)),
            pltpu.VMEM(traction_vectors.shape, F32),
            pltpu.SemaphoreType.DMA((leaves,)),
            pltpu.VMEM((RANK, COLS), F32),
        ],
        flops=6 * 10**7,
        limit=ALMOST_ALL,
    )
    def over_y(block, step):
        return lax.ppermute(block, "y", [(i, (i + step) % targets) for i in range(targets)])

    weights = jnp.concatenate([weights, over_y(weights, targets // 2)], axis=0)
    coeffs = lax.all_to_all(send, ("x", "z"), 0, 0, tiled=True)
    weights = [weights] + [over_y(weights, step) for step in shifts(targets)]
    leaf_axes = ("x", "z")
    low = lax.ppermute(stack, leaf_axes, [(i, i + 1) for i in range(subs - 1)])
    high = lax.ppermute(stack, leaf_axes, [(i + 1, i) for i in range(subs - 1)])
    coeffs, low, high, weights = lax.optimization_barrier((coeffs, low, high, weights))
    other = lax.ppermute(coeffs, "core", [(0, 1), (1, 0)])
    near = pltpu.VMEM(((3 * blocks + 1) * RANK, COLS), BF16)
    fixed, slope = whole(
        far_kernel,
        (shape(leaves, entries, COLS), shape(leaves, entries, COLS, dtype=BF16)),
        (
            low, stack, high, rows_of(couple_leaf), rows_of(pair_coupling_blocks),
            rows_of(down_leaf), rows_of(down_pair), col_basis,
            list_leaf, mask_leaf, list_pair, mask_pair,
        ),
        smem=(8, 9, 10, 11),
        scratch=[near, near, pltpu.VMEM((2 * RANK * blocks, COLS), F32)],
        flops=10**8,
    )
    parts = whole(
        part_kernel,
        shape(targets, RANK, COLS),
        (coeffs, other, *weights, *(block[:, RANK, :] for block in weights)),
        smem=range(2 + len(weights), 2 + 2 * len(weights)),
        scratch=[
            pltpu.VMEM(((2 * subs + 1) * RANK, COLS), BF16),
            pltpu.VMEM(((2 * subs + 1) * RANK, COLS), BF16),
            pltpu.VMEM((2 * subs * RANK, COLS), F32),
        ],
        flops=10**8,
    )
    parts = lax.all_to_all(parts, "y", 0, 0, tiled=True)
    return whole(
        last_kernel,
        shape(leaves, entries, COLS),
        (parts, fixed, slope),
        scratch=[pltpu.VMEM((RANK, COLS), F32)],
        flops=5 * 10**7,
    )


def solution(mesh):
    deep = max(1, mesh.shape["leaf"] // 4)
    sizes = (mesh.shape["top"] // 2, 2, mesh.shape["leaf"] // deep, deep)
    fine = jax.sharding.Mesh(mesh.devices.reshape(sizes), ("y", "core", "x", "z"))
    top, both = ("y", "core"), ("y", "core", "x", "z")
    return jax.shard_map(
        body,
        mesh=fine,
        in_specs=(
            P(both, None, None),
            P(both, None, None),
            P(both, None),
            P(both, None),
            P(both, None),
            P(both, None, None),
            P(both, None, None),
            P(both, None, None),
            P(top, None, None),
            P(both, None),
            P(both, None),
            P(both, None),
            P(top, None),
            P(both, None),
            P(both, None),
            P(both, None),
            P(top, None),
            P(both, None),
            P(both, None),
            P(both, None),
            P(both, None, None),
        ),
        out_specs=P(both, None, None),
        check_vma=False,
    )
```

```python
import functools

import jax
import jax.numpy as jnp
from jax import lax
from jax.experimental import pallas as pl
from jax.experimental.pallas import tpu as pltpu
from jax.sharding import PartitionSpec as P

RANK = 32
COLS = 128
QUADS = 4
ROWS8 = 8
F32 = jnp.float32
BF16 = jnp.bfloat16
VMEM_LIMIT = 32 * 1024 * 1024
ALMOST_ALL = 60 * 1024 * 1024


def split(x):
    high = x.astype(BF16)
    return high, (x - high.astype(F32)).astype(BF16)


def dot(a, b, contract=((1,), (0,))):
    return lax.dot_general(a, b, (contract, ((), ())), preferred_element_type=F32)


def dot_split(a, b_high, b_low):
    rows = a.shape[0]
    a_high, a_low = split(a)
    both = dot(jnp.concatenate([a_high, a_low], axis=0), b_high)
    return both[:rows] + both[rows:] + dot(a_high, b_low)


def dot_first(a, b):
    a_high, a_low = split(a)
    b_high, b_low = split(b)
    return dot(
        jnp.concatenate([a_high, a_high, a_low], axis=0),
        jnp.concatenate([b_high, b_low, b_high], axis=0),
        ((0,), (0,)),
    )


def lanes(rows=ROWS8):
    return lax.broadcasted_iota(jnp.int32, (rows, COLS), 1)


def square(flat):
    return jnp.concatenate([flat[:, RANK * q : RANK * (q + 1)] for q in range(QUADS)], axis=0)


def beside(flats):
    group = lanes() // RANK
    rows = []
    for q in range(QUADS):
        row = None
        for k, flat in enumerate(flats):
            shift = (RANK * (k - q)) % COLS
            moved = pltpu.roll(flat, shift, 1) if shift else flat
            row = moved if row is None else jnp.where(group == k, moved, row)
        rows.append(row)
    return jnp.concatenate(rows, axis=0)


def quad_rows(ref, start):
    return jnp.concatenate(
        [ref[pl.ds(start + q, ROWS8, stride=QUADS), :] for q in range(QUADS)], axis=0
    )


def store_natural(ref, start, x):
    for q in range(QUADS):
        ref[pl.ds(start + q, ROWS8, stride=QUADS), :] = x[ROWS8 * q : ROWS8 * (q + 1)]


def fetch(sources, held, sems):
    copies = [pltpu.make_async_copy(s, h, sems.at[n]) for n, (s, h) in enumerate(zip(sources, held))]
    for copy in copies:
        copy.start()
    return copies


def weights_kernel(*refs):
    sources, out_ref, held, sems, natural = refs[:7], refs[7], refs[8:15], refs[15], refs[16]
    for copy in fetch(sources, held, sems):
        copy.wait()
    couple, down, top, list_d, mask_d, list_t, mask_t = held
    slots, top_slots = list_d.shape[1], list_t.shape[1]

    def entry(ref, k):
        return ref[0:1, k : k + 1].astype(F32)

    flats = [couple[ROWS8 * k : ROWS8 * (k + 1), :] * entry(mask_d, k) for k in range(slots)]
    lane = lanes(RANK)
    ids = jnp.zeros((RANK, COLS), F32)
    for k in range(slots):
        ids = jnp.where(lane == 64 + k, entry(list_d, k), ids)
    for k in range(top_slots):
        ids = jnp.where(lane == 64 + slots + k, entry(list_t, k), ids)
    tops = [top[pl.ds(k, ROWS8, stride=top_slots), :] * entry(mask_t, k) for k in range(top_slots)]
    store_natural(natural, 0, beside(tops))
    top_high, top_low = split(natural[...])
    out_ref[0, 0:RANK, :] = beside(flats[:4])
    out_ref[0, RANK : 2 * RANK, :] = jnp.where(lane < 64, beside(flats[4:]), ids)
    out_ref[0, 2 * RANK : 3 * RANK, :] = dot_split(square(down[...]), top_high, top_low)


def up_kernel(*refs):
    sources, (stack_ref, send_ref), scratch = refs[:5], refs[5:7], refs[7:]
    held, (sems, traction, traction_sems) = scratch[:4], scratch[4:]
    leaves = sources[0].shape[0]
    pairs = leaves // 2
    copies = fetch(sources[1:], held, sems)
    tractions = [
        pltpu.make_async_copy(sources[0].at[i], traction.at[i], traction_sems.at[i]) for i in range(leaves)
    ]
    for copy in tractions:
        copy.start()
    basis, up_leaf, up_pair, up_device = held
    for copy in copies:
        copy.wait()
    for i in range(leaves):
        tractions[i].wait()
        high, low = split(traction[i])
        stack_ref[RANK * i : RANK * (i + 1), :] = dot_split(basis[i], high, low)
    for p in range(pairs):
        weight = [square(up_leaf[pl.ds(i, ROWS8, stride=leaves), :]) for i in (2 * p, 2 * p + 1)]
        value = [quad_rows(stack_ref, RANK * i) for i in (2 * p, 2 * p + 1)]
        at = RANK * (leaves + p)
        stack_ref[at : at + RANK, :] = dot_first(
            jnp.concatenate(weight, axis=0), jnp.concatenate(value, axis=0)
        )
    weight = [square(up_pair[pl.ds(p, ROWS8, stride=pairs), :]) for p in range(pairs)]
    value = [quad_rows(stack_ref, RANK * (leaves + p)) for p in range(pairs)]
    coeff = dot_first(jnp.concatenate(weight, axis=0), jnp.concatenate(value, axis=0))
    up = up_device[...]
    for d in range(send_ref.shape[0]):
        send_ref[d, 0:RANK, :] = coeff
        send_ref[d, RANK : RANK + ROWS8, :] = up


def far_kernel(
    low_ref, own_ref, high_ref, couple_leaf, couple_pair, down_leaf, down_pair, basis,
    list_leaf, mask_leaf, list_pair, mask_pair, fixed_ref, slope_ref, near_high, near_low, natural,
):
    leaves, slots = list_leaf.shape
    pairs = list_pair.shape[0]
    blocks = leaves + pairs
    top = lax.axis_index("y") * lax.axis_size("core") + lax.axis_index("core")
    leaf = lax.axis_index("x") * lax.axis_size("z") + lax.axis_index("z")
    position = top * (lax.axis_size("x") * lax.axis_size("z")) + leaf
    size = blocks * RANK
    for n, ref in enumerate((low_ref, own_ref, high_ref)):
        high, low = split(ref[...])
        near_high[n * size : (n + 1) * size, :] = high
        near_low[n * size : (n + 1) * size, :] = low
    none = jnp.zeros((RANK, COLS), BF16)
    near_high[3 * size : 3 * size + RANK, :] = none
    near_low[3 * size : 3 * size + RANK, :] = none

    def near(index, mask, per_dev, offset):
        relative = index - position * per_dev + per_dev
        block = relative // per_dev * blocks + offset + relative % per_dev
        start = pl.multiple_of(jnp.where(mask == 0, 3 * blocks, block) * RANK, RANK)
        return near_high[pl.ds(start, RANK), :], near_low[pl.ds(start, RANK), :]

    for p in range(pairs):
        flats = [couple_pair[pl.ds(k * ROWS8 * pairs + p, ROWS8, stride=pairs), :] for k in range(slots)]
        weight = jnp.concatenate([beside(flats[:4]), beside(flats[4:])], axis=1)
        taken = [near(list_pair[p, k], mask_pair[p, k], pairs, leaves) for k in range(slots)]
        rows = [jnp.concatenate([t[n] for t in taken] + [none, none], axis=0) for n in (0, 1)]
        at = 2 * RANK * p
        store_natural(natural, at, dot_split(weight, *rows))
        store_natural(natural, at + RANK, beside([down_pair[pl.ds(p, ROWS8, stride=pairs), :]] * 4))
        sums = split(natural[at : at + RANK, :])
        downs = split(natural[at + RANK : at + 2 * RANK, :])
        for i in (2 * p, 2 * p + 1):
            flats = [
                couple_leaf[pl.ds(k * ROWS8 * leaves + i, ROWS8, stride=leaves), :] for k in range(slots)
            ] + [down_leaf[pl.ds(i, ROWS8, stride=leaves), :]]
            weight = jnp.concatenate([beside(flats[:4]), beside(flats[4:])], axis=1)
            taken = [near(list_leaf[i, k], mask_leaf[i, k], leaves, 0) for k in range(slots)]
            rows = [
                jnp.concatenate(
                    [
                        jnp.concatenate([t[n] for t in taken] + [sums[n], none], axis=0),
                        jnp.concatenate([none] * slots + [downs[n], none], axis=0),
                    ],
                    axis=1,
                )
                for n in (0, 1)
            ]
            here = dot_split(weight, *rows)
            at = 2 * RANK * (pairs + i)
            store_natural(natural, at, here[:, :COLS])
            store_natural(natural, at + RANK, here[:, COLS:])
            here = jnp.concatenate([natural[at : at + RANK, :], natural[at + RANK : at + 2 * RANK, :]], axis=1)
            both = dot_first(basis[i], here)
            fixed_ref[i] = both[:, :COLS]
            slope = both[:, COLS:]
            slope_high = slope.astype(BF16).astype(F32)
            lane = lanes(slope.shape[0])
            slope_ref[i] = jnp.where(
                lane < 64, slope_high, jnp.where(lane < 96, slope - slope_high, 0.0)
            ).astype(BF16)


def shifts(count):
    half = count // 2
    return [s if s <= half // 2 else s - half for s in range(1, half)]


def part_kernel(own, *refs):
    buffers = (len(refs) - (5 if own else 6)) // 2
    coeff_ref = refs[0]
    weight_refs, ids_refs = refs[1 : 1 + buffers], refs[1 + buffers : 1 + 2 * buffers]
    before_ref = None if own else refs[1 + 2 * buffers]
    out_ref, coeff_high, coeff_low, gathered = refs[-4:]
    subs = coeff_ref.shape[0]
    rows_y = 2 * buffers
    slots, top_slots = 6, 4
    row, core = lax.axis_index("y"), lax.axis_index("core")
    source = row * 2 + (core if own else 1 - core)
    none = jnp.zeros((RANK, COLS), BF16)
    for d in range(subs):
        value = coeff_ref[d, 0:RANK, :]
        gathered[RANK * d : RANK * (d + 1), :] = value
        high, low = split(value)
        coeff_high[RANK * d : RANK * (d + 1), :] = high
        coeff_low[RANK * d : RANK * (d + 1), :] = low
    coeff_high[RANK * subs : RANK * (subs + 1), :] = none
    coeff_low[RANK * subs : RANK * (subs + 1), :] = none
    up = jnp.concatenate([coeff_ref[d, RANK : RANK + ROWS8, :] for d in range(subs)], axis=0)
    value = jnp.concatenate(
        [gathered[pl.ds(q, ROWS8 * subs, stride=QUADS), :] for q in range(QUADS)], axis=1
    )
    every = dot_first(up, value)
    top = jnp.zeros((RANK, COLS), F32)
    for q in range(QUADS):
        top = top + every[RANK * q : RANK * (q + 1), COLS * q : COLS * (q + 1)]
    lane_group = lanes(RANK) // RANK
    targets = []
    for weight_ref, ids_ref, shift in zip(weight_refs, ids_refs, [0] + shifts(rows_y)):
        targets += [(weight_ref, ids_ref, n, shift + n * buffers) for n in range(2)]
    top_weight = []
    for weight_ref, ids_ref, n, _ in targets:
        used = jnp.zeros((RANK, COLS), F32)
        for k in range(top_slots):
            owner = ids_ref[n, 64 + slots + k].astype(jnp.int32)
            used = jnp.where(lane_group == k, jnp.where(owner == source, 1.0, 0.0), used)
        top_weight.append(weight_ref[n, 2 * RANK : 3 * RANK, :] * used)
    top_high, top_low = split(top)
    top_part = dot_split(
        jnp.concatenate(top_weight, axis=0),
        jnp.concatenate([top_high] * 4, axis=0),
        jnp.concatenate([top_low] * 4, axis=0),
    )

    def starts(ids_ref, n):
        found = []
        for k in range(slots):
            index = ids_ref[n, 64 + k].astype(jnp.int32)
            block = jnp.where(index // subs == source, index % subs, subs)
            found.append(pl.multiple_of(block * RANK, RANK))
        return found

    for t in range(0, rows_y, 2):
        two = targets[t : t + 2]
        pair = [starts(ids_ref, n) for _, ids_ref, n, _ in two]
        rows = [
            jnp.concatenate(
                [jnp.concatenate([ref[pl.ds(s, RANK), :] for s in one], axis=0) for one in pair], axis=1
            )
            for ref in (coeff_high, coeff_low)
        ]
        weight = [
            jnp.concatenate([w[n, 0:RANK, :], w[n, RANK : 2 * RANK, :64]], axis=1) for w, _, n, _ in two
        ]
        both = dot_split(jnp.concatenate(weight, axis=0), *rows)
        for m, (_, _, _, offset) in enumerate(two):
            at = (row + 2 * rows_y - offset) % rows_y
            mine = both[RANK * m : RANK * (m + 1), COLS * m : COLS * (m + 1)]
            mine = mine + top_part[RANK * (t + m) : RANK * (t + m + 1)]
            out_ref[at] = mine if own else mine + before_ref[at]


def last_kernel(parts_ref, fixed_ref, slope_ref, out_ref, natural):
    total = parts_ref[0]
    for t in range(1, parts_ref.shape[0]):
        total = total + parts_ref[t]
    store_natural(natural, 0, total)
    high, low = split(natural[...])
    rows = jnp.concatenate([high, low, high, jnp.zeros((RANK, COLS), BF16)], axis=0)
    for i in range(out_ref.shape[0]):
        out_ref[i] = fixed_ref[i] + dot(slope_ref[i], rows)


def whole(kernel, out, args, smem=(), hbm=(), scratch=(), flops=0, limit=VMEM_LIMIT):
    vmem = pl.BlockSpec(memory_space=pltpu.VMEM)
    scalars = pl.BlockSpec(memory_space=pltpu.SMEM)
    far = pl.BlockSpec(memory_space=pltpu.HBM)
    size = sum(a.size * a.dtype.itemsize for a in args)
    outs = out if isinstance(out, tuple) else (out,)
    size += sum(o.size * o.dtype.itemsize for o in outs)
    return pl.pallas_call(
        kernel,
        out_shape=out,
        in_specs=[scalars if n in smem else far if n in hbm else vmem for n in range(len(args))],
        out_specs=tuple(vmem for _ in out) if isinstance(out, tuple) else vmem,
        scratch_shapes=list(scratch),
        compiler_params=pltpu.CompilerParams(vmem_limit_bytes=limit),
        cost_estimate=pl.CostEstimate(flops=flops, bytes_accessed=size, transcendentals=0),
    )(*args)


def rows_of(x):
    if x.ndim == 2:
        return x.reshape(x.shape[0], ROWS8, COLS).transpose(1, 0, 2).reshape(-1, COLS)
    return x.reshape(x.shape[0], x.shape[1], ROWS8, COLS).transpose(1, 2, 0, 3).reshape(-1, COLS)


def body(
    traction_vectors,
    row_basis,
    up_leaf,
    up_pair,
    up_device,
    couple_leaf,
    pair_coupling_blocks,
    couple_device,
    couple_top,
    list_leaf,
    list_pair,
    list_device,
    list_top,
    mask_leaf,
    mask_pair,
    mask_device,
    mask_top,
    down_leaf,
    down_pair,
    down_device,
    col_basis,
):
    def shape(*dims, dtype=F32):
        return jax.ShapeDtypeStruct(dims, dtype)

    leaves, entries, _ = traction_vectors.shape
    blocks = leaves + leaves // 2
    targets = lax.axis_size("y")
    subs = lax.axis_size("x") * lax.axis_size("z")
    def fetched(args):
        return [pltpu.VMEM(a.shape, a.dtype) for a in args] + [pltpu.SemaphoreType.DMA((len(args),))]

    first = (
        rows_of(couple_device), rows_of(down_device), rows_of(couple_top[0]),
        list_device, mask_device, list_top, mask_top,
    )
    weights = whole(
        weights_kernel,
        shape(1, 3 * RANK, COLS),
        first,
        hbm=range(len(first)),
        scratch=[*fetched(first), pltpu.VMEM((RANK, COLS), F32)],
        flops=10**6,
        limit=ALMOST_ALL,
    )
    weights, traction_vectors = lax.optimization_barrier((weights, traction_vectors))
    second = (traction_vectors, row_basis, rows_of(up_leaf), rows_of(up_pair), rows_of(up_device))
    stack, send = whole(
        up_kernel,
        (shape(blocks * RANK, COLS), shape(subs, RANK + ROWS8, COLS)),
        second,
        hbm=range(len(second)),
        scratch=[
            *fetched(second[1:]),
            pltpu.VMEM(traction_vectors.shape, F32),
            pltpu.SemaphoreType.DMA((leaves,)),
        ],
        flops=6 * 10**7,
        limit=ALMOST_ALL,
    )

    def over_y(block, step):
        return lax.ppermute(block, "y", [(i, (i + step) % targets) for i in range(targets)])

    weights = jnp.concatenate([weights, over_y(weights, targets // 2)], axis=0)
    coeffs = lax.all_to_all(send, ("x", "z"), 0, 0, tiled=True)
    weights = [weights] + [over_y(weights, step) for step in shifts(targets)]
    leaf_axes = ("x", "z")
    low = lax.ppermute(stack, leaf_axes, [(i, i + 1) for i in range(subs - 1)])
    high = lax.ppermute(stack, leaf_axes, [(i + 1, i) for i in range(subs - 1)])
    coeffs, low, high, weights = lax.optimization_barrier((coeffs, low, high, weights))
    other = lax.ppermute(coeffs, "core", [(0, 1), (1, 0)])
    weights = [*weights, *(block[:, RANK, :] for block in weights)]
    count = len(weights) // 2
    parts = []
    for own, gathered in ((True, coeffs), (False, other)):
        parts = whole(
            functools.partial(part_kernel, own),
            shape(targets, RANK, COLS),
            (gathered, *weights, *([] if own else [parts])),
            smem=range(1 + count, 1 + 2 * count),
            scratch=[
                pltpu.VMEM(((subs + 1) * RANK, COLS), BF16),
                pltpu.VMEM(((subs + 1) * RANK, COLS), BF16),
                pltpu.VMEM((subs * RANK, COLS), F32),
            ],
            flops=5 * 10**7,
        )
    parts, low = lax.optimization_barrier((parts, low))
    parts = lax.all_to_all(parts, "y", 0, 0, tiled=True)
    near = pltpu.VMEM(((3 * blocks + 1) * RANK, COLS), BF16)
    fixed, slope = whole(
        far_kernel,
        (shape(leaves, entries, COLS), shape(leaves, entries, COLS, dtype=BF16)),
        (
            low, stack, high, rows_of(couple_leaf), rows_of(pair_coupling_blocks),
            rows_of(down_leaf), rows_of(down_pair), col_basis,
            list_leaf, mask_leaf, list_pair, mask_pair,
        ),
        smem=(8, 9, 10, 11),
        scratch=[near, near, pltpu.VMEM((2 * RANK * blocks, COLS), F32)],
        flops=10**8,
    )
    return whole(
        last_kernel,
        shape(leaves, entries, COLS),
        (parts, fixed, slope),
        scratch=[pltpu.VMEM((RANK, COLS), F32)],
        flops=5 * 10**7,
    )


def solution(mesh):
    deep = max(1, mesh.shape["leaf"] // 4)
    sizes = (mesh.shape["top"] // 2, 2, mesh.shape["leaf"] // deep, deep)
    fine = jax.sharding.Mesh(mesh.devices.reshape(sizes), ("y", "core", "x", "z"))
    top, both = ("y", "core"), ("y", "core", "x", "z")
    return jax.shard_map(
        body,
        mesh=fine,
        in_specs=(
            P(both, None, None),
            P(both, None, None),
            P(both, None),
            P(both, None),
            P(both, None),
            P(both, None, None),
            P(both, None, None),
            P(both, None, None),
            P(top, None, None),
            P(both, None),
            P(both, None),
            P(both, None),
            P(top, None),
            P(both, None),
            P(both, None),
            P(both, None),
            P(top, None),
            P(both, None),
            P(both, None),
            P(both, None),
            P(both, None, None),
        ),
        out_specs=P(both, None, None),
        check_vma=False,
    )
```

```python
import functools

import jax
import jax.numpy as jnp
from jax import lax
from jax.experimental import pallas as pl
from jax.experimental.pallas import tpu as pltpu
from jax.sharding import PartitionSpec as P

RANK = 32
COLS = 128
QUADS = 4
ROWS8 = 8
F32 = jnp.float32
BF16 = jnp.bfloat16
VMEM_LIMIT = 32 * 1024 * 1024
ALMOST_ALL = 60 * 1024 * 1024


def split(x):
    high = x.astype(BF16)
    return high, (x - high.astype(F32)).astype(BF16)


def dot(a, b, contract=((1,), (0,))):
    return lax.dot_general(a, b, (contract, ((), ())), preferred_element_type=F32)


def dot_split(a, b_high, b_low):
    rows = a.shape[0]
    a_high, a_low = split(a)
    both = dot(jnp.concatenate([a_high, a_low], axis=0), b_high)
    return both[:rows] + both[rows:] + dot(a_high, b_low)


def dot_first(a, b):
    a_high, a_low = split(a)
    b_high, b_low = split(b)
    return dot(
        jnp.concatenate([a_high, a_high, a_low], axis=0),
        jnp.concatenate([b_high, b_low, b_high], axis=0),
        ((0,), (0,)),
    )


def lanes(rows=ROWS8):
    return lax.broadcasted_iota(jnp.int32, (rows, COLS), 1)


def square(flat):
    return jnp.concatenate([flat[:, RANK * q : RANK * (q + 1)] for q in range(QUADS)], axis=0)


def beside(flats):
    group = lanes() // RANK
    rows = []
    for q in range(QUADS):
        row = None
        for k, flat in enumerate(flats):
            shift = (RANK * (k - q)) % COLS
            moved = pltpu.roll(flat, shift, 1) if shift else flat
            row = moved if row is None else jnp.where(group == k, moved, row)
        rows.append(row)
    return jnp.concatenate(rows, axis=0)


def quad_rows(ref, start):
    return jnp.concatenate(
        [ref[pl.ds(start + q, ROWS8, stride=QUADS), :] for q in range(QUADS)], axis=0
    )


def store_natural(ref, start, x):
    for q in range(QUADS):
        ref[pl.ds(start + q, ROWS8, stride=QUADS), :] = x[ROWS8 * q : ROWS8 * (q + 1)]


def fetch(sources, held, sems):
    copies = [pltpu.make_async_copy(s, h, sems.at[n]) for n, (s, h) in enumerate(zip(sources, held))]
    for copy in copies:
        copy.start()
    return copies


def weights_kernel(*refs):
    sources, out_ref, held, sems, natural = refs[:7], refs[7], refs[8:15], refs[15], refs[16]
    for copy in fetch(sources, held, sems):
        copy.wait()
    couple, down, top, list_d, mask_d, list_t, mask_t = held
    slots, top_slots = list_d.shape[1], list_t.shape[1]

    def entry(ref, k):
        return ref[0:1, k : k + 1].astype(F32)

    flats = [couple[ROWS8 * k : ROWS8 * (k + 1), :] * entry(mask_d, k) for k in range(slots)]
    lane = lanes(RANK)
    ids = jnp.zeros((RANK, COLS), F32)
    for k in range(slots):
        ids = jnp.where(lane == 64 + k, entry(list_d, k), ids)
    for k in range(top_slots):
        ids = jnp.where(lane == 64 + slots + k, entry(list_t, k), ids)
    tops = [top[pl.ds(k, ROWS8, stride=top_slots), :] * entry(mask_t, k) for k in range(top_slots)]
    store_natural(natural, 0, beside(tops))
    top_high, top_low = split(natural[...])
    out_ref[0, 0:RANK, :] = beside(flats[:4])
    out_ref[0, RANK : 2 * RANK, :] = jnp.where(lane < 64, beside(flats[4:]), ids)
    out_ref[0, 2 * RANK : 3 * RANK, :] = dot_split(square(down[...]), top_high, top_low)


def up_kernel(*refs):
    sources, (stack_ref, send_ref), scratch = refs[:5], refs[5:7], refs[7:]
    held, (sems, traction, traction_sems) = scratch[:4], scratch[4:]
    leaves = sources[0].shape[0]
    pairs = leaves // 2
    copies = fetch(sources[1:], held, sems)
    tractions = [
        pltpu.make_async_copy(sources[0].at[i], traction.at[i], traction_sems.at[i]) for i in range(leaves)
    ]
    for copy in tractions:
        copy.start()
    basis, up_leaf, up_pair, up_device = held
    for copy in copies:
        copy.wait()
    for i in range(leaves):
        tractions[i].wait()
        high, low = split(traction[i])
        stack_ref[RANK * i : RANK * (i + 1), :] = dot_split(basis[i], high, low)
    for p in range(pairs):
        weight = [square(up_leaf[pl.ds(i, ROWS8, stride=leaves), :]) for i in (2 * p, 2 * p + 1)]
        value = [quad_rows(stack_ref, RANK * i) for i in (2 * p, 2 * p + 1)]
        at = RANK * (leaves + p)
        stack_ref[at : at + RANK, :] = dot_first(
            jnp.concatenate(weight, axis=0), jnp.concatenate(value, axis=0)
        )
    weight = [square(up_pair[pl.ds(p, ROWS8, stride=pairs), :]) for p in range(pairs)]
    value = [quad_rows(stack_ref, RANK * (leaves + p)) for p in range(pairs)]
    coeff = dot_first(jnp.concatenate(weight, axis=0), jnp.concatenate(value, axis=0))
    up = up_device[...]
    for d in range(send_ref.shape[0]):
        send_ref[d, 0:RANK, :] = coeff
        send_ref[d, RANK : RANK + ROWS8, :] = up


def far_kernel(
    low_ref, own_ref, high_ref, couple_leaf, couple_pair, down_leaf, down_pair, basis,
    list_leaf, mask_leaf, list_pair, mask_pair, fixed_ref, slope_ref, near_high, near_low, natural,
):
    leaves, slots = list_leaf.shape
    pairs = list_pair.shape[0]
    blocks = leaves + pairs
    top = lax.axis_index("y") * lax.axis_size("core") + lax.axis_index("core")
    leaf = lax.axis_index("x") * lax.axis_size("z") + lax.axis_index("z")
    position = top * (lax.axis_size("x") * lax.axis_size("z")) + leaf
    size = blocks * RANK
    for n, ref in enumerate((low_ref, own_ref, high_ref)):
        high, low = split(ref[...])
        near_high[n * size : (n + 1) * size, :] = high
        near_low[n * size : (n + 1) * size, :] = low
    none = jnp.zeros((RANK, COLS), BF16)
    near_high[3 * size : 3 * size + RANK, :] = none
    near_low[3 * size : 3 * size + RANK, :] = none

    def near(index, mask, per_dev, offset):
        relative = index - position * per_dev + per_dev
        block = relative // per_dev * blocks + offset + relative % per_dev
        start = pl.multiple_of(jnp.where(mask == 0, 3 * blocks, block) * RANK, RANK)
        return near_high[pl.ds(start, RANK), :], near_low[pl.ds(start, RANK), :]

    for p in range(pairs):
        flats = [couple_pair[pl.ds(k * ROWS8 * pairs + p, ROWS8, stride=pairs), :] for k in range(slots)]
        weight = jnp.concatenate([beside(flats[:4]), beside(flats[4:])], axis=1)
        taken = [near(list_pair[p, k], mask_pair[p, k], pairs, leaves) for k in range(slots)]
        rows = [jnp.concatenate([t[n] for t in taken] + [none, none], axis=0) for n in (0, 1)]
        at = 2 * RANK * p
        store_natural(natural, at, dot_split(weight, *rows))
        store_natural(natural, at + RANK, beside([down_pair[pl.ds(p, ROWS8, stride=pairs), :]] * 4))
        sums = split(natural[at : at + RANK, :])
        downs = split(natural[at + RANK : at + 2 * RANK, :])
        for i in (2 * p, 2 * p + 1):
            flats = [
                couple_leaf[pl.ds(k * ROWS8 * leaves + i, ROWS8, stride=leaves), :] for k in range(slots)
            ] + [down_leaf[pl.ds(i, ROWS8, stride=leaves), :]]
            weight = jnp.concatenate([beside(flats[:4]), beside(flats[4:])], axis=1)
            taken = [near(list_leaf[i, k], mask_leaf[i, k], leaves, 0) for k in range(slots)]
            rows = [
                jnp.concatenate(
                    [
                        jnp.concatenate([t[n] for t in taken] + [sums[n], none], axis=0),
                        jnp.concatenate([none] * slots + [downs[n], none], axis=0),
                    ],
                    axis=1,
                )
                for n in (0, 1)
            ]
            here = dot_split(weight, *rows)
            at = 2 * RANK * (pairs + i)
            store_natural(natural, at, here[:, :COLS])
            store_natural(natural, at + RANK, here[:, COLS:])
            here = jnp.concatenate([natural[at : at + RANK, :], natural[at + RANK : at + 2 * RANK, :]], axis=1)
            both = dot_first(basis[i], here)
            fixed_ref[i] = both[:, :COLS]
            slope = both[:, COLS:]
            slope_high = slope.astype(BF16).astype(F32)
            lane = lanes(slope.shape[0])
            slope_ref[i] = jnp.where(
                lane < 64, slope_high, jnp.where(lane < 96, slope - slope_high, 0.0)
            ).astype(BF16)


def shifts(count):
    half = count // 2
    return [s if s <= half // 2 else s - half for s in range(1, half)]


def part_kernel(own, *refs):
    buffers = (len(refs) - (5 if own else 6)) // 2
    coeff_ref = refs[0]
    weight_refs, ids_refs = refs[1 : 1 + buffers], refs[1 + buffers : 1 + 2 * buffers]
    before_ref = None if own else refs[1 + 2 * buffers]
    out_ref, coeff_high, coeff_low, gathered = refs[-4:]
    subs = coeff_ref.shape[0]
    rows_y = 2 * buffers
    slots, top_slots = 6, 4
    row, core = lax.axis_index("y"), lax.axis_index("core")
    source = row * 2 + (core if own else 1 - core)
    none = jnp.zeros((RANK, COLS), BF16)
    for d in range(subs):
        value = coeff_ref[d, 0:RANK, :]
        gathered[RANK * d : RANK * (d + 1), :] = value
        high, low = split(value)
        coeff_high[RANK * d : RANK * (d + 1), :] = high
        coeff_low[RANK * d : RANK * (d + 1), :] = low
    coeff_high[RANK * subs : RANK * (subs + 1), :] = none
    coeff_low[RANK * subs : RANK * (subs + 1), :] = none
    up = jnp.concatenate([coeff_ref[d, RANK : RANK + ROWS8, :] for d in range(subs)], axis=0)
    value = jnp.concatenate(
        [gathered[pl.ds(q, ROWS8 * subs, stride=QUADS), :] for q in range(QUADS)], axis=1
    )
    every = dot_first(up, value)
    top = jnp.zeros((RANK, COLS), F32)
    for q in range(QUADS):
        top = top + every[RANK * q : RANK * (q + 1), COLS * q : COLS * (q + 1)]
    lane_group = lanes(RANK) // RANK
    targets = []
    for weight_ref, ids_ref, shift in zip(weight_refs, ids_refs, [0] + shifts(rows_y)):
        targets += [(weight_ref, ids_ref, n, shift + n * buffers) for n in range(2)]
    top_weight = []
    for weight_ref, ids_ref, n, _ in targets:
        used = jnp.zeros((RANK, COLS), F32)
        for k in range(top_slots):
            owner = ids_ref[n, 64 + slots + k].astype(jnp.int32)
            used = jnp.where(lane_group == k, jnp.where(owner == source, 1.0, 0.0), used)
        top_weight.append(weight_ref[n, 2 * RANK : 3 * RANK, :] * used)
    top_high, top_low = split(top)
    top_part = dot_split(
        jnp.concatenate(top_weight, axis=0),
        jnp.concatenate([top_high] * 4, axis=0),
        jnp.concatenate([top_low] * 4, axis=0),
    )

    def starts(ids_ref, n):
        found = []
        for k in range(slots):
            index = ids_ref[n, 64 + k].astype(jnp.int32)
            block = jnp.where(index // subs == source, index % subs, subs)
            found.append(pl.multiple_of(block * RANK, RANK))
        return found

    for t in range(0, rows_y, 2):
        two = targets[t : t + 2]
        pair = [starts(ids_ref, n) for _, ids_ref, n, _ in two]
        rows = [
            jnp.concatenate(
                [jnp.concatenate([ref[pl.ds(s, RANK), :] for s in one], axis=0) for one in pair], axis=1
            )
            for ref in (coeff_high, coeff_low)
        ]
        weight = [
            jnp.concatenate([w[n, 0:RANK, :], w[n, RANK : 2 * RANK, :64]], axis=1) for w, _, n, _ in two
        ]
        both = dot_split(jnp.concatenate(weight, axis=0), *rows)
        for m, (_, _, _, offset) in enumerate(two):
            at = (row + 2 * rows_y - offset) % rows_y
            mine = both[RANK * m : RANK * (m + 1), COLS * m : COLS * (m + 1)]
            mine = mine + top_part[RANK * (t + m) : RANK * (t + m + 1)]
            out_ref[at] = mine if own else mine + before_ref[at]


def last_kernel(parts_ref, fixed_ref, slope_ref, out_ref, natural):
    total = parts_ref[0]
    for t in range(1, parts_ref.shape[0]):
        total = total + parts_ref[t]
    store_natural(natural, 0, total)
    high, low = split(natural[...])
    rows = jnp.concatenate([high, low, high, jnp.zeros((RANK, COLS), BF16)], axis=0)
    for i in range(out_ref.shape[0]):
        out_ref[i] = fixed_ref[i] + dot(slope_ref[i], rows)


def whole(kernel, out, args, smem=(), hbm=(), scratch=(), flops=0, limit=VMEM_LIMIT):
    vmem = pl.BlockSpec(memory_space=pltpu.VMEM)
    scalars = pl.BlockSpec(memory_space=pltpu.SMEM)
    far = pl.BlockSpec(memory_space=pltpu.HBM)
    size = sum(a.size * a.dtype.itemsize for a in args)
    outs = out if isinstance(out, tuple) else (out,)
    size += sum(o.size * o.dtype.itemsize for o in outs)
    return pl.pallas_call(
        kernel,
        out_shape=out,
        in_specs=[scalars if n in smem else far if n in hbm else vmem for n in range(len(args))],
        out_specs=tuple(vmem for _ in out) if isinstance(out, tuple) else vmem,
        scratch_shapes=list(scratch),
        compiler_params=pltpu.CompilerParams(vmem_limit_bytes=limit),
        cost_estimate=pl.CostEstimate(flops=flops, bytes_accessed=size, transcendentals=0),
    )(*args)


def rows_of(x):
    if x.ndim == 2:
        return x.reshape(x.shape[0], ROWS8, COLS).transpose(1, 0, 2).reshape(-1, COLS)
    return x.reshape(x.shape[0], x.shape[1], ROWS8, COLS).transpose(1, 2, 0, 3).reshape(-1, COLS)


def body(
    traction_vectors,
    row_basis,
    up_leaf,
    up_pair,
    up_device,
    couple_leaf,
    pair_coupling_blocks,
    couple_device,
    couple_top,
    list_leaf,
    list_pair,
    list_device,
    list_top,
    mask_leaf,
    mask_pair,
    mask_device,
    mask_top,
    down_leaf,
    down_pair,
    down_device,
    col_basis,
):
    def shape(*dims, dtype=F32):
        return jax.ShapeDtypeStruct(dims, dtype)

    leaves, entries, _ = traction_vectors.shape
    blocks = leaves + leaves // 2
    targets = lax.axis_size("y")
    subs = lax.axis_size("x") * lax.axis_size("z")
    def fetched(args):
        return [pltpu.VMEM(a.shape, a.dtype) for a in args] + [pltpu.SemaphoreType.DMA((len(args),))]

    first = (
        rows_of(couple_device), rows_of(down_device), rows_of(couple_top[0]),
        list_device, mask_device, list_top, mask_top,
    )
    weights = whole(
        weights_kernel,
        shape(1, 3 * RANK, COLS),
        first,
        hbm=range(len(first)),
        scratch=[*fetched(first), pltpu.VMEM((RANK, COLS), F32)],
        flops=10**6,
        limit=ALMOST_ALL,
    )
    weights, traction_vectors = lax.optimization_barrier((weights, traction_vectors))
    second = (traction_vectors, row_basis, rows_of(up_leaf), rows_of(up_pair), rows_of(up_device))
    stack, send = whole(
        up_kernel,
        (shape(blocks * RANK, COLS), shape(subs, RANK + ROWS8, COLS)),
        second,
        hbm=range(len(second)),
        scratch=[
            *fetched(second[1:]),
            pltpu.VMEM(traction_vectors.shape, F32),
            pltpu.SemaphoreType.DMA((leaves,)),
        ],
        flops=6 * 10**7,
        limit=ALMOST_ALL,
    )

    def over_y(block, step):
        return lax.ppermute(block, "y", [(i, (i + step) % targets) for i in range(targets)])

    come = over_y(weights, targets // 2)
    come, send = lax.optimization_barrier((come, send))
    weights = jnp.concatenate([weights, come], axis=0)
    coeffs = lax.all_to_all(send, ("x", "z"), 0, 0, tiled=True)
    weights = [weights] + [over_y(weights, step) for step in shifts(targets)]
    leaf_axes = ("x", "z")
    low = lax.ppermute(stack, leaf_axes, [(i, i + 1) for i in range(subs - 1)])
    high = lax.ppermute(stack, leaf_axes, [(i + 1, i) for i in range(subs - 1)])
    coeffs, low, high, weights = lax.optimization_barrier((coeffs, low, high, weights))
    other = lax.ppermute(coeffs, "core", [(0, 1), (1, 0)])
    weights = [*weights, *(block[:, RANK, :] for block in weights)]
    count = len(weights) // 2
    parts = []
    for own, gathered in ((True, coeffs), (False, other)):
        parts = whole(
            functools.partial(part_kernel, own),
            shape(targets, RANK, COLS),
            (gathered, *weights, *([] if own else [parts])),
            smem=range(1 + count, 1 + 2 * count),
            scratch=[
                pltpu.VMEM(((subs + 1) * RANK, COLS), BF16),
                pltpu.VMEM(((subs + 1) * RANK, COLS), BF16),
                pltpu.VMEM((subs * RANK, COLS), F32),
            ],
            flops=5 * 10**7,
        )
    parts, low = lax.optimization_barrier((parts, low))
    parts = lax.all_to_all(parts, "y", 0, 0, tiled=True)
    near = pltpu.VMEM(((3 * blocks + 1) * RANK, COLS), BF16)
    fixed, slope = whole(
        far_kernel,
        (shape(leaves, entries, COLS), shape(leaves, entries, COLS, dtype=BF16)),
        (
            low, stack, high, rows_of(couple_leaf), rows_of(pair_coupling_blocks),
            rows_of(down_leaf), rows_of(down_pair), col_basis,
            list_leaf, mask_leaf, list_pair, mask_pair,
        ),
        smem=(8, 9, 10, 11),
        scratch=[near, near, pltpu.VMEM((2 * RANK * blocks, COLS), F32)],
        flops=10**8,
    )
    return whole(
        last_kernel,
        shape(leaves, entries, COLS),
        (parts, fixed, slope),
        scratch=[pltpu.VMEM((RANK, COLS), F32)],
        flops=5 * 10**7,
    )


def solution(mesh):
    deep = max(1, mesh.shape["leaf"] // 4)
    sizes = (mesh.shape["top"] // 2, 2, mesh.shape["leaf"] // deep, deep)
    fine = jax.sharding.Mesh(mesh.devices.reshape(sizes), ("y", "core", "x", "z"))
    top, both = ("y", "core"), ("y", "core", "x", "z")
    return jax.shard_map(
        body,
        mesh=fine,
        in_specs=(
            P(both, None, None),
            P(both, None, None),
            P(both, None),
            P(both, None),
            P(both, None),
            P(both, None, None),
            P(both, None, None),
            P(both, None, None),
            P(top, None, None),
            P(both, None),
            P(both, None),
            P(both, None),
            P(top, None),
            P(both, None),
            P(both, None),
            P(both, None),
            P(top, None),
            P(both, None),
            P(both, None),
            P(both, None),
            P(both, None, None),
        ),
        out_specs=P(both, None, None),
        check_vma=False,
    )
```

```python
import functools

import jax
import jax.numpy as jnp
from jax import lax
from jax.experimental import pallas as pl
from jax.experimental.pallas import tpu as pltpu
from jax.sharding import PartitionSpec as P

RANK = 32
COLS = 128
QUADS = 4
ROWS8 = 8
F32 = jnp.float32
BF16 = jnp.bfloat16
VMEM_LIMIT = 32 * 1024 * 1024
ALMOST_ALL = 60 * 1024 * 1024


def split(x):
    high = x.astype(BF16)
    return high, (x - high.astype(F32)).astype(BF16)


def dot(a, b, contract=((1,), (0,))):
    return lax.dot_general(a, b, (contract, ((), ())), preferred_element_type=F32)


def dot_split(a, b_high, b_low):
    rows = a.shape[0]
    a_high, a_low = split(a)
    both = dot(jnp.concatenate([a_high, a_low], axis=0), b_high)
    return both[:rows] + both[rows:] + dot(a_high, b_low)


def dot_first(a, b):
    a_high, a_low = split(a)
    b_high, b_low = split(b)
    return dot(
        jnp.concatenate([a_high, a_high, a_low], axis=0),
        jnp.concatenate([b_high, b_low, b_high], axis=0),
        ((0,), (0,)),
    )


def lanes(rows=ROWS8):
    return lax.broadcasted_iota(jnp.int32, (rows, COLS), 1)


def square(flat):
    return jnp.concatenate([flat[:, RANK * q : RANK * (q + 1)] for q in range(QUADS)], axis=0)


def beside(flats):
    group = lanes() // RANK
    rows = []
    for q in range(QUADS):
        row = None
        for k, flat in enumerate(flats):
            shift = (RANK * (k - q)) % COLS
            moved = pltpu.roll(flat, shift, 1) if shift else flat
            row = moved if row is None else jnp.where(group == k, moved, row)
        rows.append(row)
    return jnp.concatenate(rows, axis=0)


def quad_rows(ref, start):
    return jnp.concatenate(
        [ref[pl.ds(start + q, ROWS8, stride=QUADS), :] for q in range(QUADS)], axis=0
    )


def store_natural(ref, start, x):
    for q in range(QUADS):
        ref[pl.ds(start + q, ROWS8, stride=QUADS), :] = x[ROWS8 * q : ROWS8 * (q + 1)]


def fetch(sources, held, sems):
    copies = [pltpu.make_async_copy(s, h, sems.at[n]) for n, (s, h) in enumerate(zip(sources, held))]
    for copy in copies:
        copy.start()
    return copies


def weights_of(held, natural):
    couple, down, top, list_d, mask_d, list_t, mask_t = held
    slots, top_slots = list_d.shape[1], list_t.shape[1]

    def entry(ref, k):
        return ref[0:1, k : k + 1].astype(F32)

    flats = [couple[ROWS8 * k : ROWS8 * (k + 1), :] * entry(mask_d, k) for k in range(slots)]
    lane = lanes(RANK)
    ids = jnp.zeros((RANK, COLS), F32)
    for k in range(slots):
        ids = jnp.where(lane == 64 + k, entry(list_d, k), ids)
    for k in range(top_slots):
        ids = jnp.where(lane == 64 + slots + k, entry(list_t, k), ids)
    tops = [top[pl.ds(k, ROWS8, stride=top_slots), :] * entry(mask_t, k) for k in range(top_slots)]
    store_natural(natural, 0, beside(tops))
    top_high, top_low = split(natural[...])
    return (
        beside(flats[:4]),
        jnp.where(lane < 64, beside(flats[4:]), ids),
        dot_split(square(down[...]), top_high, top_low),
    )


def first_kernel(*refs):
    sources, outs, scratch = refs[:12], refs[12:15], refs[15:]
    held, (sems, traction, traction_sems, natural) = scratch[:11], scratch[11:15]
    results, out_sems = scratch[15:18], scratch[18]
    leaves = sources[0].shape[0]
    pairs = leaves // 2
    tractions = [
        pltpu.make_async_copy(sources[0].at[i], traction.at[i], traction_sems.at[i]) for i in range(leaves)
    ]
    basis_copy, *copies = fetch(sources[1:], held, sems)
    for copy in tractions:
        copy.start()
    basis, up_leaf, up_pair, up_device = held[:4]
    weight_ref, stack_ref, send_ref = results
    writes = [pltpu.make_async_copy(r, o, out_sems.at[n]) for n, (r, o) in enumerate(zip(results, outs))]
    for copy in copies:
        copy.wait()
    for n, block in enumerate(weights_of(held[4:], natural)):
        weight_ref[0, RANK * n : RANK * (n + 1), :] = block
    writes[0].start()
    basis_copy.wait()
    for i in range(leaves):
        tractions[i].wait()
        high, low = split(traction[i])
        stack_ref[RANK * i : RANK * (i + 1), :] = dot_split(basis[i], high, low)
    for p in range(pairs):
        weight = [square(up_leaf[pl.ds(i, ROWS8, stride=leaves), :]) for i in (2 * p, 2 * p + 1)]
        value = [quad_rows(stack_ref, RANK * i) for i in (2 * p, 2 * p + 1)]
        at = RANK * (leaves + p)
        stack_ref[at : at + RANK, :] = dot_first(
            jnp.concatenate(weight, axis=0), jnp.concatenate(value, axis=0)
        )
    writes[1].start()
    weight = [square(up_pair[pl.ds(p, ROWS8, stride=pairs), :]) for p in range(pairs)]
    value = [quad_rows(stack_ref, RANK * (leaves + p)) for p in range(pairs)]
    coeff = dot_first(jnp.concatenate(weight, axis=0), jnp.concatenate(value, axis=0))
    up = up_device[...]
    for d in range(send_ref.shape[0]):
        send_ref[d, 0:RANK, :] = coeff
        send_ref[d, RANK : RANK + ROWS8, :] = up
    writes[2].start()
    for write in writes:
        write.wait()


def far_kernel(
    low_ref, own_ref, high_ref, couple_leaf, couple_pair, down_leaf, down_pair, basis,
    list_leaf, mask_leaf, list_pair, mask_pair, fixed_ref, slope_ref, near_high, near_low, natural,
):
    leaves, slots = list_leaf.shape
    pairs = list_pair.shape[0]
    blocks = leaves + pairs
    top = lax.axis_index("y") * lax.axis_size("core") + lax.axis_index("core")
    leaf = lax.axis_index("x") * lax.axis_size("z") + lax.axis_index("z")
    position = top * (lax.axis_size("x") * lax.axis_size("z")) + leaf
    size = blocks * RANK
    for n, ref in enumerate((low_ref, own_ref, high_ref)):
        high, low = split(ref[...])
        near_high[n * size : (n + 1) * size, :] = high
        near_low[n * size : (n + 1) * size, :] = low
    none = jnp.zeros((RANK, COLS), BF16)
    near_high[3 * size : 3 * size + RANK, :] = none
    near_low[3 * size : 3 * size + RANK, :] = none

    def near(index, mask, per_dev, offset):
        relative = index - position * per_dev + per_dev
        block = relative // per_dev * blocks + offset + relative % per_dev
        start = pl.multiple_of(jnp.where(mask == 0, 3 * blocks, block) * RANK, RANK)
        return near_high[pl.ds(start, RANK), :], near_low[pl.ds(start, RANK), :]

    for p in range(pairs):
        flats = [couple_pair[pl.ds(k * ROWS8 * pairs + p, ROWS8, stride=pairs), :] for k in range(slots)]
        weight = jnp.concatenate([beside(flats[:4]), beside(flats[4:])], axis=1)
        taken = [near(list_pair[p, k], mask_pair[p, k], pairs, leaves) for k in range(slots)]
        rows = [jnp.concatenate([t[n] for t in taken] + [none, none], axis=0) for n in (0, 1)]
        at = 2 * RANK * p
        store_natural(natural, at, dot_split(weight, *rows))
        store_natural(natural, at + RANK, beside([down_pair[pl.ds(p, ROWS8, stride=pairs), :]] * 4))
        sums = split(natural[at : at + RANK, :])
        downs = split(natural[at + RANK : at + 2 * RANK, :])
        for i in (2 * p, 2 * p + 1):
            flats = [
                couple_leaf[pl.ds(k * ROWS8 * leaves + i, ROWS8, stride=leaves), :] for k in range(slots)
            ] + [down_leaf[pl.ds(i, ROWS8, stride=leaves), :]]
            weight = jnp.concatenate([beside(flats[:4]), beside(flats[4:])], axis=1)
            taken = [near(list_leaf[i, k], mask_leaf[i, k], leaves, 0) for k in range(slots)]
            rows = [
                jnp.concatenate(
                    [
                        jnp.concatenate([t[n] for t in taken] + [sums[n], none], axis=0),
                        jnp.concatenate([none] * slots + [downs[n], none], axis=0),
                    ],
                    axis=1,
                )
                for n in (0, 1)
            ]
            here = dot_split(weight, *rows)
            at = 2 * RANK * (pairs + i)
            store_natural(natural, at, here[:, :COLS])
            store_natural(natural, at + RANK, here[:, COLS:])
            here = jnp.concatenate([natural[at : at + RANK, :], natural[at + RANK : at + 2 * RANK, :]], axis=1)
            both = dot_first(basis[i], here)
            fixed_ref[i] = both[:, :COLS]
            slope = both[:, COLS:]
            slope_high = slope.astype(BF16).astype(F32)
            lane = lanes(slope.shape[0])
            slope_ref[i] = jnp.where(
                lane < 64, slope_high, jnp.where(lane < 96, slope - slope_high, 0.0)
            ).astype(BF16)


def shifts(count):
    half = count // 2
    return [s if s <= half // 2 else s - half for s in range(1, half)]


def part_kernel(own, *refs):
    buffers = (len(refs) - (5 if own else 6)) // 2
    coeff_ref = refs[0]
    weight_refs, ids_refs = refs[1 : 1 + buffers], refs[1 + buffers : 1 + 2 * buffers]
    before_ref = None if own else refs[1 + 2 * buffers]
    out_ref, coeff_high, coeff_low, gathered = refs[-4:]
    subs = coeff_ref.shape[0]
    rows_y = 2 * buffers
    slots, top_slots = 6, 4
    row, core = lax.axis_index("y"), lax.axis_index("core")
    source = row * 2 + (core if own else 1 - core)
    none = jnp.zeros((RANK, COLS), BF16)
    for d in range(subs):
        value = coeff_ref[d, 0:RANK, :]
        gathered[RANK * d : RANK * (d + 1), :] = value
        high, low = split(value)
        coeff_high[RANK * d : RANK * (d + 1), :] = high
        coeff_low[RANK * d : RANK * (d + 1), :] = low
    coeff_high[RANK * subs : RANK * (subs + 1), :] = none
    coeff_low[RANK * subs : RANK * (subs + 1), :] = none
    up = jnp.concatenate([coeff_ref[d, RANK : RANK + ROWS8, :] for d in range(subs)], axis=0)
    value = jnp.concatenate(
        [gathered[pl.ds(q, ROWS8 * subs, stride=QUADS), :] for q in range(QUADS)], axis=1
    )
    every = dot_first(up, value)
    top = jnp.zeros((RANK, COLS), F32)
    for q in range(QUADS):
        top = top + every[RANK * q : RANK * (q + 1), COLS * q : COLS * (q + 1)]
    lane_group = lanes(RANK) // RANK
    targets = []
    for weight_ref, ids_ref, shift in zip(weight_refs, ids_refs, [0] + shifts(rows_y)):
        targets += [(weight_ref, ids_ref, n, shift + n * buffers) for n in range(2)]
    top_weight = []
    for weight_ref, ids_ref, n, _ in targets:
        used = jnp.zeros((RANK, COLS), F32)
        for k in range(top_slots):
            owner = ids_ref[n, 64 + slots + k].astype(jnp.int32)
            used = jnp.where(lane_group == k, jnp.where(owner == source, 1.0, 0.0), used)
        top_weight.append(weight_ref[n, 2 * RANK : 3 * RANK, :] * used)
    top_high, top_low = split(top)
    top_part = dot_split(
        jnp.concatenate(top_weight, axis=0),
        jnp.concatenate([top_high] * 4, axis=0),
        jnp.concatenate([top_low] * 4, axis=0),
    )

    def starts(ids_ref, n):
        found = []
        for k in range(slots):
            index = ids_ref[n, 64 + k].astype(jnp.int32)
            block = jnp.where(index // subs == source, index % subs, subs)
            found.append(pl.multiple_of(block * RANK, RANK))
        return found

    for t in range(0, rows_y, 2):
        two = targets[t : t + 2]
        pair = [starts(ids_ref, n) for _, ids_ref, n, _ in two]
        rows = [
            jnp.concatenate(
                [jnp.concatenate([ref[pl.ds(s, RANK), :] for s in one], axis=0) for one in pair], axis=1
            )
            for ref in (coeff_high, coeff_low)
        ]
        weight = [
            jnp.concatenate([w[n, 0:RANK, :], w[n, RANK : 2 * RANK, :64]], axis=1) for w, _, n, _ in two
        ]
        both = dot_split(jnp.concatenate(weight, axis=0), *rows)
        for m, (_, _, _, offset) in enumerate(two):
            at = (row + 2 * rows_y - offset * (1 - 2 * core)) % rows_y
            mine = both[RANK * m : RANK * (m + 1), COLS * m : COLS * (m + 1)]
            mine = mine + top_part[RANK * (t + m) : RANK * (t + m + 1)]
            out_ref[at] = mine if own else mine + before_ref[at]


def last_kernel(parts_ref, fixed_ref, slope_ref, out_ref, natural, held, sems):
    total = parts_ref[0]
    for t in range(1, parts_ref.shape[0]):
        total = total + parts_ref[t]
    store_natural(natural, 0, total)
    high, low = split(natural[...])
    rows = jnp.concatenate([high, low, high, jnp.zeros((RANK, COLS), BF16)], axis=0)
    writes = [pltpu.make_async_copy(held.at[i], out_ref.at[i], sems.at[i]) for i in range(held.shape[0])]
    for i, write in enumerate(writes):
        held[i] = fixed_ref[i] + dot(slope_ref[i], rows)
        write.start()
    for write in writes:
        write.wait()


def whole(kernel, out, args, smem=(), hbm=(), scratch=(), flops=0, limit=VMEM_LIMIT, out_hbm=False):
    vmem = pl.BlockSpec(memory_space=pltpu.VMEM)
    scalars = pl.BlockSpec(memory_space=pltpu.SMEM)
    far = pl.BlockSpec(memory_space=pltpu.HBM)
    place = far if out_hbm else vmem
    size = sum(a.size * a.dtype.itemsize for a in args)
    outs = out if isinstance(out, tuple) else (out,)
    size += sum(o.size * o.dtype.itemsize for o in outs)
    return pl.pallas_call(
        kernel,
        out_shape=out,
        in_specs=[scalars if n in smem else far if n in hbm else vmem for n in range(len(args))],
        out_specs=tuple(place for _ in out) if isinstance(out, tuple) else place,
        scratch_shapes=list(scratch),
        compiler_params=pltpu.CompilerParams(vmem_limit_bytes=limit),
        cost_estimate=pl.CostEstimate(flops=flops, bytes_accessed=size, transcendentals=0),
    )(*args)


def rows_of(x):
    if x.ndim == 2:
        return x.reshape(x.shape[0], ROWS8, COLS).transpose(1, 0, 2).reshape(-1, COLS)
    return x.reshape(x.shape[0], x.shape[1], ROWS8, COLS).transpose(1, 2, 0, 3).reshape(-1, COLS)


def body(
    traction_vectors,
    row_basis,
    up_leaf,
    up_pair,
    up_device,
    couple_leaf,
    pair_coupling_blocks,
    couple_device,
    couple_top,
    list_leaf,
    list_pair,
    list_device,
    list_top,
    mask_leaf,
    mask_pair,
    mask_device,
    mask_top,
    down_leaf,
    down_pair,
    down_device,
    col_basis,
):
    def shape(*dims, dtype=F32):
        return jax.ShapeDtypeStruct(dims, dtype)

    leaves, entries, _ = traction_vectors.shape
    blocks = leaves + leaves // 2
    targets = lax.axis_size("y")
    subs = lax.axis_size("x") * lax.axis_size("z")
    def fetched(args):
        return [pltpu.VMEM(a.shape, a.dtype) for a in args] + [pltpu.SemaphoreType.DMA((len(args),))]

    first = (
        traction_vectors, row_basis, rows_of(up_leaf), rows_of(up_pair), rows_of(up_device),
        rows_of(couple_device), rows_of(down_device), rows_of(couple_top[0]),
        list_device, mask_device, list_top, mask_top,
    )
    results = (shape(1, 3 * RANK, COLS), shape(blocks * RANK, COLS), shape(subs, RANK + ROWS8, COLS))
    weights, stack, send = whole(
        first_kernel,
        results,
        first,
        hbm=range(len(first)),
        out_hbm=True,
        scratch=[
            *fetched(first[1:]),
            pltpu.VMEM(traction_vectors.shape, F32),
            pltpu.SemaphoreType.DMA((leaves,)),
            pltpu.VMEM((RANK, COLS), F32),
            *fetched(results),
        ],
        flops=6 * 10**7,
        limit=ALMOST_ALL,
    )

    def over_y(block, step):
        moves = []
        for y in range(targets):
            moves.append((2 * y, 2 * ((y + step) % targets)))
            moves.append((2 * y + 1, 2 * ((y - step) % targets) + 1))
        return lax.ppermute(block, ("y", "core"), moves)

    weights = jnp.concatenate([weights, over_y(weights, targets // 2)], axis=0)
    coeffs = lax.all_to_all(send, ("x", "z"), 0, 0, tiled=True)
    weights = [weights] + [over_y(weights, step) for step in shifts(targets)]
    leaf_axes = ("x", "z")
    low = lax.ppermute(stack, leaf_axes, [(i, i + 1) for i in range(subs - 1)])
    high = lax.ppermute(stack, leaf_axes, [(i + 1, i) for i in range(subs - 1)])
    coeffs, low, high, weights = lax.optimization_barrier((coeffs, low, high, weights))
    other = lax.ppermute(coeffs, "core", [(0, 1), (1, 0)])
    weights = [*weights, *(block[:, RANK, :] for block in weights)]
    count = len(weights) // 2
    parts = []
    for own, gathered in ((True, coeffs), (False, other)):
        parts = whole(
            functools.partial(part_kernel, own),
            shape(targets, RANK, COLS),
            (gathered, *weights, *([] if own else [parts])),
            smem=range(1 + count, 1 + 2 * count),
            scratch=[
                pltpu.VMEM(((subs + 1) * RANK, COLS), BF16),
                pltpu.VMEM(((subs + 1) * RANK, COLS), BF16),
                pltpu.VMEM((subs * RANK, COLS), F32),
            ],
            flops=5 * 10**7,
        )
    parts, low = lax.optimization_barrier((parts, low))
    parts = lax.all_to_all(parts, "y", 0, 0, tiled=True)
    near = pltpu.VMEM(((3 * blocks + 1) * RANK, COLS), BF16)
    fixed, slope = whole(
        far_kernel,
        (shape(leaves, entries, COLS), shape(leaves, entries, COLS, dtype=BF16)),
        (
            low, stack, high, rows_of(couple_leaf), rows_of(pair_coupling_blocks),
            rows_of(down_leaf), rows_of(down_pair), col_basis,
            list_leaf, mask_leaf, list_pair, mask_pair,
        ),
        smem=(8, 9, 10, 11),
        scratch=[near, near, pltpu.VMEM((2 * RANK * blocks, COLS), F32)],
        flops=10**8,
    )
    return whole(
        last_kernel,
        shape(leaves, entries, COLS),
        (parts, fixed, slope),
        out_hbm=True,
        scratch=[
            pltpu.VMEM((RANK, COLS), F32),
            pltpu.VMEM((leaves, entries, COLS), F32),
            pltpu.SemaphoreType.DMA((leaves,)),
        ],
        flops=5 * 10**7,
    )


def solution(mesh):
    deep = max(1, mesh.shape["leaf"] // 4)
    sizes = (mesh.shape["top"] // 2, 2, mesh.shape["leaf"] // deep, deep)
    fine = jax.sharding.Mesh(mesh.devices.reshape(sizes), ("y", "core", "x", "z"))
    top, both = ("y", "core"), ("y", "core", "x", "z")
    return jax.shard_map(
        body,
        mesh=fine,
        in_specs=(
            P(both, None, None),
            P(both, None, None),
            P(both, None),
            P(both, None),
            P(both, None),
            P(both, None, None),
            P(both, None, None),
            P(both, None, None),
            P(top, None, None),
            P(both, None),
            P(both, None),
            P(both, None),
            P(top, None),
            P(both, None),
            P(both, None),
            P(both, None),
            P(top, None),
            P(both, None),
            P(both, None),
            P(both, None),
            P(both, None, None),
        ),
        out_specs=P(both, None, None),
        check_vma=False,
    )
```

```python
import functools

import jax
import jax.numpy as jnp
from jax import lax
from jax.experimental import pallas as pl
from jax.experimental.pallas import tpu as pltpu
from jax.sharding import PartitionSpec as P

RANK = 32
COLS = 128
QUADS = 4
ROWS8 = 8
F32 = jnp.float32
BF16 = jnp.bfloat16
VMEM_LIMIT = 32 * 1024 * 1024
ALMOST_ALL = 60 * 1024 * 1024


def split(x):
    high = x.astype(BF16)
    return high, (x - high.astype(F32)).astype(BF16)


def dot(a, b, contract=((1,), (0,))):
    return lax.dot_general(a, b, (contract, ((), ())), preferred_element_type=F32)


def dot_split(a, b_high, b_low):
    rows = a.shape[0]
    a_high, a_low = split(a)
    both = dot(jnp.concatenate([a_high, a_low], axis=0), b_high)
    return both[:rows] + both[rows:] + dot(a_high, b_low)


def dot_first(a, b):
    a_high, a_low = split(a)
    b_high, b_low = split(b)
    return dot(
        jnp.concatenate([a_high, a_high, a_low], axis=0),
        jnp.concatenate([b_high, b_low, b_high], axis=0),
        ((0,), (0,)),
    )


def lanes(rows=ROWS8):
    return lax.broadcasted_iota(jnp.int32, (rows, COLS), 1)


def square(flat):
    return jnp.concatenate([flat[:, RANK * q : RANK * (q + 1)] for q in range(QUADS)], axis=0)


def beside(flats):
    group = lanes() // RANK
    rows = []
    for q in range(QUADS):
        row = None
        for k, flat in enumerate(flats):
            shift = (RANK * (k - q)) % COLS
            moved = pltpu.roll(flat, shift, 1) if shift else flat
            row = moved if row is None else jnp.where(group == k, moved, row)
        rows.append(row)
    return jnp.concatenate(rows, axis=0)


def quad_rows(ref, start):
    return jnp.concatenate(
        [ref[pl.ds(start + q, ROWS8, stride=QUADS), :] for q in range(QUADS)], axis=0
    )


def store_natural(ref, start, x):
    for q in range(QUADS):
        ref[pl.ds(start + q, ROWS8, stride=QUADS), :] = x[ROWS8 * q : ROWS8 * (q + 1)]


def fetch(sources, held, sems):
    copies = [pltpu.make_async_copy(s, h, sems.at[n]) for n, (s, h) in enumerate(zip(sources, held))]
    for copy in copies:
        copy.start()
    return copies


def weights_of(held, natural):
    couple, down, top, list_d, mask_d, list_t, mask_t = held
    slots, top_slots = list_d.shape[1], list_t.shape[1]

    def entry(ref, k):
        return ref[0:1, k : k + 1].astype(F32)

    flats = [couple[ROWS8 * k : ROWS8 * (k + 1), :] * entry(mask_d, k) for k in range(slots)]
    lane = lanes(RANK)
    ids = jnp.zeros((RANK, COLS), F32)
    for k in range(slots):
        ids = jnp.where(lane == 64 + k, entry(list_d, k), ids)
    for k in range(top_slots):
        ids = jnp.where(lane == 64 + slots + k, entry(list_t, k), ids)
    tops = [top[pl.ds(k, ROWS8, stride=top_slots), :] * entry(mask_t, k) for k in range(top_slots)]
    store_natural(natural, 0, beside(tops))
    top_high, top_low = split(natural[...])
    return (
        beside(flats[:4]),
        jnp.where(lane < 64, beside(flats[4:]), ids),
        dot_split(square(down[...]), top_high, top_low),
    )


def first_kernel(*refs):
    sources, outs, scratch = refs[:12], refs[12:15], refs[15:]
    held, (sems, traction, traction_sems, natural) = scratch[:11], scratch[11:15]
    results, out_sems = scratch[15:18], scratch[18]
    leaves = sources[0].shape[0]
    pairs = leaves // 2
    tractions = [
        pltpu.make_async_copy(sources[0].at[i], traction.at[i], traction_sems.at[i]) for i in range(leaves)
    ]
    basis_copy, *copies = fetch(sources[1:], held, sems)
    for copy in tractions:
        copy.start()
    basis, up_leaf, up_pair, up_device = held[:4]
    weight_ref, stack_ref, send_ref = results
    writes = [pltpu.make_async_copy(r, o, out_sems.at[n]) for n, (r, o) in enumerate(zip(results, outs))]
    for copy in copies:
        copy.wait()
    for n, block in enumerate(weights_of(held[4:], natural)):
        weight_ref[0, RANK * n : RANK * (n + 1), :] = block
    writes[0].start()
    basis_copy.wait()
    for i in range(leaves):
        tractions[i].wait()
        high, low = split(traction[i])
        stack_ref[RANK * i : RANK * (i + 1), :] = dot_split(basis[i], high, low)
    for p in range(pairs):
        weight = [square(up_leaf[pl.ds(i, ROWS8, stride=leaves), :]) for i in (2 * p, 2 * p + 1)]
        value = [quad_rows(stack_ref, RANK * i) for i in (2 * p, 2 * p + 1)]
        at = RANK * (leaves + p)
        stack_ref[at : at + RANK, :] = dot_first(
            jnp.concatenate(weight, axis=0), jnp.concatenate(value, axis=0)
        )
    writes[1].start()
    weight = [square(up_pair[pl.ds(p, ROWS8, stride=pairs), :]) for p in range(pairs)]
    value = [quad_rows(stack_ref, RANK * (leaves + p)) for p in range(pairs)]
    coeff = dot_first(jnp.concatenate(weight, axis=0), jnp.concatenate(value, axis=0))
    up = up_device[...]
    for d in range(send_ref.shape[0]):
        send_ref[d, 0:RANK, :] = coeff
        send_ref[d, RANK : RANK + ROWS8, :] = up
    writes[2].start()
    for write in writes:
        write.wait()


def far_kernel(
    low_ref, own_ref, high_ref, couple_leaf, couple_pair, down_leaf, down_pair, basis,
    list_leaf, mask_leaf, list_pair, mask_pair, fixed_ref, slope_ref, near_high, near_low, natural,
):
    leaves, slots = list_leaf.shape
    pairs = list_pair.shape[0]
    blocks = leaves + pairs
    top = lax.axis_index("y") * lax.axis_size("core") + lax.axis_index("core")
    leaf = lax.axis_index("x") * lax.axis_size("z") + lax.axis_index("z")
    position = top * (lax.axis_size("x") * lax.axis_size("z")) + leaf
    size = blocks * RANK
    for n, ref in enumerate((low_ref, own_ref, high_ref)):
        high, low = split(ref[...])
        near_high[n * size : (n + 1) * size, :] = high
        near_low[n * size : (n + 1) * size, :] = low
    none = jnp.zeros((RANK, COLS), BF16)
    near_high[3 * size : 3 * size + RANK, :] = none
    near_low[3 * size : 3 * size + RANK, :] = none

    def near(index, mask, per_dev, offset):
        relative = index - position * per_dev + per_dev
        block = relative // per_dev * blocks + offset + relative % per_dev
        start = pl.multiple_of(jnp.where(mask == 0, 3 * blocks, block) * RANK, RANK)
        return near_high[pl.ds(start, RANK), :], near_low[pl.ds(start, RANK), :]

    for p in range(pairs):
        flats = [couple_pair[pl.ds(k * ROWS8 * pairs + p, ROWS8, stride=pairs), :] for k in range(slots)]
        weight = jnp.concatenate([beside(flats[:4]), beside(flats[4:])], axis=1)
        taken = [near(list_pair[p, k], mask_pair[p, k], pairs, leaves) for k in range(slots)]
        rows = [jnp.concatenate([t[n] for t in taken] + [none, none], axis=0) for n in (0, 1)]
        at = 2 * RANK * p
        store_natural(natural, at, dot_split(weight, *rows))
        store_natural(natural, at + RANK, beside([down_pair[pl.ds(p, ROWS8, stride=pairs), :]] * 4))
        sums = split(natural[at : at + RANK, :])
        downs = split(natural[at + RANK : at + 2 * RANK, :])
        for i in (2 * p, 2 * p + 1):
            flats = [
                couple_leaf[pl.ds(k * ROWS8 * leaves + i, ROWS8, stride=leaves), :] for k in range(slots)
            ] + [down_leaf[pl.ds(i, ROWS8, stride=leaves), :]]
            weight = jnp.concatenate([beside(flats[:4]), beside(flats[4:])], axis=1)
            taken = [near(list_leaf[i, k], mask_leaf[i, k], leaves, 0) for k in range(slots)]
            rows = [
                jnp.concatenate(
                    [
                        jnp.concatenate([t[n] for t in taken] + [sums[n], none], axis=0),
                        jnp.concatenate([none] * slots + [downs[n], none], axis=0),
                    ],
                    axis=1,
                )
                for n in (0, 1)
            ]
            here = dot_split(weight, *rows)
            at = 2 * RANK * (pairs + i)
            store_natural(natural, at, here[:, :COLS])
            store_natural(natural, at + RANK, here[:, COLS:])
            here = jnp.concatenate([natural[at : at + RANK, :], natural[at + RANK : at + 2 * RANK, :]], axis=1)
            both = dot_first(basis[i], here)
            fixed_ref[i] = both[:, :COLS]
            slope = both[:, COLS:]
            slope_high = slope.astype(BF16).astype(F32)
            lane = lanes(slope.shape[0])
            slope_ref[i] = jnp.where(
                lane < 64, slope_high, jnp.where(lane < 96, slope - slope_high, 0.0)
            ).astype(BF16)


def shifts(count):
    half = count // 2
    return [s if s <= half // 2 else s - half for s in range(1, half)]


def part_kernel(own, *refs):
    buffers = (len(refs) - (5 if own else 6)) // 2
    coeff_ref = refs[0]
    weight_refs, ids_refs = refs[1 : 1 + buffers], refs[1 + buffers : 1 + 2 * buffers]
    before_ref = None if own else refs[1 + 2 * buffers]
    out_ref, coeff_high, coeff_low, gathered = refs[-4:]
    subs = coeff_ref.shape[0]
    rows_y = 2 * buffers
    slots, top_slots = 6, 4
    row, core = lax.axis_index("y"), lax.axis_index("core")
    source = row * 2 + (core if own else 1 - core)
    none = jnp.zeros((RANK, COLS), BF16)
    for d in range(subs):
        value = coeff_ref[d, 0:RANK, :]
        gathered[RANK * d : RANK * (d + 1), :] = value
        high, low = split(value)
        coeff_high[RANK * d : RANK * (d + 1), :] = high
        coeff_low[RANK * d : RANK * (d + 1), :] = low
    coeff_high[RANK * subs : RANK * (subs + 1), :] = none
    coeff_low[RANK * subs : RANK * (subs + 1), :] = none
    up = jnp.concatenate([coeff_ref[d, RANK : RANK + ROWS8, :] for d in range(subs)], axis=0)
    value = jnp.concatenate(
        [gathered[pl.ds(q, ROWS8 * subs, stride=QUADS), :] for q in range(QUADS)], axis=1
    )
    every = dot_first(up, value)
    top = jnp.zeros((RANK, COLS), F32)
    for q in range(QUADS):
        top = top + every[RANK * q : RANK * (q + 1), COLS * q : COLS * (q + 1)]
    lane_group = lanes(RANK) // RANK
    targets = []
    for weight_ref, ids_ref, shift in zip(weight_refs, ids_refs, [0] + shifts(rows_y)):
        targets += [(weight_ref, ids_ref, n, shift + n * buffers) for n in range(2)]
    top_weight = []
    for weight_ref, ids_ref, n, _ in targets:
        used = jnp.zeros((RANK, COLS), F32)
        for k in range(top_slots):
            owner = ids_ref[n, 64 + slots + k].astype(jnp.int32)
            used = jnp.where(lane_group == k, jnp.where(owner == source, 1.0, 0.0), used)
        top_weight.append(weight_ref[n, 2 * RANK : 3 * RANK, :] * used)
    top_high, top_low = split(top)
    top_part = dot_split(
        jnp.concatenate(top_weight, axis=0),
        jnp.concatenate([top_high] * 4, axis=0),
        jnp.concatenate([top_low] * 4, axis=0),
    )

    def starts(ids_ref, n):
        found = []
        for k in range(slots):
            index = ids_ref[n, 64 + k].astype(jnp.int32)
            block = jnp.where(index // subs == source, index % subs, subs)
            found.append(pl.multiple_of(block * RANK, RANK))
        return found

    for t in range(0, rows_y, 2):
        two = targets[t : t + 2]
        pair = [starts(ids_ref, n) for _, ids_ref, n, _ in two]
        rows = [
            jnp.concatenate(
                [jnp.concatenate([ref[pl.ds(s, RANK), :] for s in one], axis=0) for one in pair], axis=1
            )
            for ref in (coeff_high, coeff_low)
        ]
        weight = [
            jnp.concatenate([w[n, 0:RANK, :], w[n, RANK : 2 * RANK, :64]], axis=1) for w, _, n, _ in two
        ]
        both = dot_split(jnp.concatenate(weight, axis=0), *rows)
        for m, (_, _, _, offset) in enumerate(two):
            at = (row + 2 * rows_y - offset * (1 - 2 * core)) % rows_y
            mine = both[RANK * m : RANK * (m + 1), COLS * m : COLS * (m + 1)]
            mine = mine + top_part[RANK * (t + m) : RANK * (t + m + 1)]
            out_ref[at] = mine if own else mine + before_ref[at]


def last_kernel(parts_ref, fixed_ref, slope_ref, out_ref, natural, held, sems):
    total = parts_ref[0]
    for t in range(1, parts_ref.shape[0]):
        total = total + parts_ref[t]
    store_natural(natural, 0, total)
    high, low = split(natural[...])
    rows = jnp.concatenate([high, low, high, jnp.zeros((RANK, COLS), BF16)], axis=0)
    writes = [pltpu.make_async_copy(held.at[i], out_ref.at[i], sems.at[i]) for i in range(held.shape[0])]
    for i, write in enumerate(writes):
        held[i] = fixed_ref[i] + dot(slope_ref[i], rows)
        write.start()
    for write in writes:
        write.wait()


def whole(kernel, out, args, smem=(), hbm=(), scratch=(), flops=0, limit=VMEM_LIMIT, out_hbm=False):
    vmem = pl.BlockSpec(memory_space=pltpu.VMEM)
    scalars = pl.BlockSpec(memory_space=pltpu.SMEM)
    far = pl.BlockSpec(memory_space=pltpu.HBM)
    place = far if out_hbm else vmem
    size = sum(a.size * a.dtype.itemsize for a in args)
    outs = out if isinstance(out, tuple) else (out,)
    size += sum(o.size * o.dtype.itemsize for o in outs)
    return pl.pallas_call(
        kernel,
        out_shape=out,
        in_specs=[scalars if n in smem else far if n in hbm else vmem for n in range(len(args))],
        out_specs=tuple(place for _ in out) if isinstance(out, tuple) else place,
        scratch_shapes=list(scratch),
        compiler_params=pltpu.CompilerParams(vmem_limit_bytes=limit),
        cost_estimate=pl.CostEstimate(flops=flops, bytes_accessed=size, transcendentals=0),
    )(*args)


def rows_of(x):
    if x.ndim == 2:
        return x.reshape(x.shape[0], ROWS8, COLS).transpose(1, 0, 2).reshape(-1, COLS)
    return x.reshape(x.shape[0], x.shape[1], ROWS8, COLS).transpose(1, 2, 0, 3).reshape(-1, COLS)


def body(
    traction_vectors,
    row_basis,
    up_leaf,
    up_pair,
    up_device,
    couple_leaf,
    pair_coupling_blocks,
    couple_device,
    couple_top,
    list_leaf,
    list_pair,
    list_device,
    list_top,
    mask_leaf,
    mask_pair,
    mask_device,
    mask_top,
    down_leaf,
    down_pair,
    down_device,
    col_basis,
):
    def shape(*dims, dtype=F32):
        return jax.ShapeDtypeStruct(dims, dtype)

    leaves, entries, _ = traction_vectors.shape
    blocks = leaves + leaves // 2
    targets = lax.axis_size("y")
    subs = lax.axis_size("x") * lax.axis_size("z")
    def fetched(args):
        return [pltpu.VMEM(a.shape, a.dtype) for a in args] + [pltpu.SemaphoreType.DMA((len(args),))]

    first = (
        traction_vectors, row_basis, rows_of(up_leaf), rows_of(up_pair), rows_of(up_device),
        rows_of(couple_device), rows_of(down_device), rows_of(couple_top[0]),
        list_device, mask_device, list_top, mask_top,
    )
    results = (shape(1, 3 * RANK, COLS), shape(blocks * RANK, COLS), shape(subs, RANK + ROWS8, COLS))
    weights, stack, send = whole(
        first_kernel,
        results,
        first,
        hbm=range(len(first)),
        out_hbm=True,
        scratch=[
            *fetched(first[1:]),
            pltpu.VMEM(traction_vectors.shape, F32),
            pltpu.SemaphoreType.DMA((leaves,)),
            pltpu.VMEM((RANK, COLS), F32),
            *fetched(results),
        ],
        flops=6 * 10**7,
        limit=ALMOST_ALL,
    )

    def over_y(block, step):
        moves = []
        for y in range(targets):
            moves.append((2 * y, 2 * ((y + step) % targets)))
            moves.append((2 * y + 1, 2 * ((y - step) % targets) + 1))
        return lax.ppermute(block, ("y", "core"), moves)

    weights = jnp.concatenate([weights, over_y(weights, targets // 2)], axis=0)
    coeffs = lax.all_to_all(send, ("x", "z"), 0, 0, tiled=True)
    weights = [weights] + [over_y(weights, step) for step in shifts(targets)]
    leaf_axes = ("x", "z")
    low = lax.ppermute(stack, leaf_axes, [(i, i + 1) for i in range(subs - 1)])
    high = lax.ppermute(stack, leaf_axes, [(i + 1, i) for i in range(subs - 1)])
    near = pltpu.VMEM(((3 * blocks + 1) * RANK, COLS), BF16)
    fixed, slope = whole(
        far_kernel,
        (shape(leaves, entries, COLS), shape(leaves, entries, COLS, dtype=BF16)),
        (
            low, stack, high, rows_of(couple_leaf), rows_of(pair_coupling_blocks),
            rows_of(down_leaf), rows_of(down_pair), col_basis,
            list_leaf, mask_leaf, list_pair, mask_pair,
        ),
        smem=(8, 9, 10, 11),
        scratch=[near, near, pltpu.VMEM((2 * RANK * blocks, COLS), F32)],
        flops=10**8,
    )
    coeffs, weights, fixed, slope = lax.optimization_barrier((coeffs, weights, fixed, slope))
    other = lax.ppermute(coeffs, "core", [(0, 1), (1, 0)])
    weights = [*weights, *(block[:, RANK, :] for block in weights)]
    count = len(weights) // 2
    parts = []
    for own, gathered in ((True, coeffs), (False, other)):
        parts = whole(
            functools.partial(part_kernel, own),
            shape(targets, RANK, COLS),
            (gathered, *weights, *([] if own else [parts])),
            smem=range(1 + count, 1 + 2 * count),
            scratch=[
                pltpu.VMEM(((subs + 1) * RANK, COLS), BF16),
                pltpu.VMEM(((subs + 1) * RANK, COLS), BF16),
                pltpu.VMEM((subs * RANK, COLS), F32),
            ],
            flops=5 * 10**7,
        )
    parts = lax.all_to_all(parts, "y", 0, 0, tiled=True)
    return whole(
        last_kernel,
        shape(leaves, entries, COLS),
        (parts, fixed, slope),
        out_hbm=True,
        scratch=[
            pltpu.VMEM((RANK, COLS), F32),
            pltpu.VMEM((leaves, entries, COLS), F32),
            pltpu.SemaphoreType.DMA((leaves,)),
        ],
        flops=5 * 10**7,
    )


def solution(mesh):
    deep = max(1, mesh.shape["leaf"] // 4)
    sizes = (mesh.shape["top"] // 2, 2, mesh.shape["leaf"] // deep, deep)
    fine = jax.sharding.Mesh(mesh.devices.reshape(sizes), ("y", "core", "x", "z"))
    top, both = ("y", "core"), ("y", "core", "x", "z")
    return jax.shard_map(
        body,
        mesh=fine,
        in_specs=(
            P(both, None, None),
            P(both, None, None),
            P(both, None),
            P(both, None),
            P(both, None),
            P(both, None, None),
            P(both, None, None),
            P(both, None, None),
            P(top, None, None),
            P(both, None),
            P(both, None),
            P(both, None),
            P(top, None),
            P(both, None),
            P(both, None),
            P(both, None),
            P(top, None),
            P(both, None),
            P(both, None),
            P(both, None),
            P(both, None, None),
        ),
        out_specs=P(both, None, None),
        check_vma=False,
    )
```

```python
import functools

import jax
import jax.numpy as jnp
from jax import lax
from jax.experimental import pallas as pl
from jax.experimental.pallas import tpu as pltpu
from jax.sharding import PartitionSpec as P

RANK = 32
COLS = 128
QUADS = 4
ROWS8 = 8
F32 = jnp.float32
BF16 = jnp.bfloat16
VMEM_LIMIT = 32 * 1024 * 1024
ALMOST_ALL = 60 * 1024 * 1024


def split(x):
    high = x.astype(BF16)
    return high, (x - high.astype(F32)).astype(BF16)


def dot(a, b, contract=((1,), (0,))):
    return lax.dot_general(a, b, (contract, ((), ())), preferred_element_type=F32)


def dot_split(a, b_high, b_low):
    rows = a.shape[0]
    a_high, a_low = split(a)
    both = dot(jnp.concatenate([a_high, a_low], axis=0), b_high)
    return both[:rows] + both[rows:] + dot(a_high, b_low)


def dot_first(a, b):
    a_high, a_low = split(a)
    b_high, b_low = split(b)
    return dot(
        jnp.concatenate([a_high, a_high, a_low], axis=0),
        jnp.concatenate([b_high, b_low, b_high], axis=0),
        ((0,), (0,)),
    )


def lanes(rows=ROWS8):
    return lax.broadcasted_iota(jnp.int32, (rows, COLS), 1)


def square(flat):
    return jnp.concatenate([flat[:, RANK * q : RANK * (q + 1)] for q in range(QUADS)], axis=0)


def beside(flats):
    group = lanes() // RANK
    rows = []
    for q in range(QUADS):
        row = None
        for k, flat in enumerate(flats):
            shift = (RANK * (k - q)) % COLS
            moved = pltpu.roll(flat, shift, 1) if shift else flat
            row = moved if row is None else jnp.where(group == k, moved, row)
        rows.append(row)
    return jnp.concatenate(rows, axis=0)


def quad_rows(ref, start):
    return jnp.concatenate(
        [ref[pl.ds(start + q, ROWS8, stride=QUADS), :] for q in range(QUADS)], axis=0
    )


def store_natural(ref, start, x):
    for q in range(QUADS):
        ref[pl.ds(start + q, ROWS8, stride=QUADS), :] = x[ROWS8 * q : ROWS8 * (q + 1)]


def fetch(sources, held, sems):
    copies = [pltpu.make_async_copy(s, h, sems.at[n]) for n, (s, h) in enumerate(zip(sources, held))]
    for copy in copies:
        copy.start()
    return copies


def weights_of(held, natural):
    couple, down, top, list_d, mask_d, list_t, mask_t = held
    slots, top_slots = list_d.shape[1], list_t.shape[1]

    def entry(ref, k):
        return ref[0:1, k : k + 1].astype(F32)

    flats = [couple[ROWS8 * k : ROWS8 * (k + 1), :] * entry(mask_d, k) for k in range(slots)]
    lane = lanes(RANK)
    ids = jnp.zeros((RANK, COLS), F32)
    for k in range(slots):
        ids = jnp.where(lane == 64 + k, entry(list_d, k), ids)
    for k in range(top_slots):
        ids = jnp.where(lane == 64 + slots + k, entry(list_t, k), ids)
    tops = [top[pl.ds(k, ROWS8, stride=top_slots), :] * entry(mask_t, k) for k in range(top_slots)]
    store_natural(natural, 0, beside(tops))
    top_high, top_low = split(natural[...])
    return (
        beside(flats[:4]),
        jnp.where(lane < 64, beside(flats[4:]), ids),
        dot_split(square(down[...]), top_high, top_low),
    )


def first_kernel(*refs):
    sources, outs, scratch = refs[:12], refs[12:15], refs[15:]
    held, (sems, traction, traction_sems, natural) = scratch[:11], scratch[11:15]
    results, out_sems = scratch[15:18], scratch[18]
    leaves = sources[0].shape[0]
    pairs = leaves // 2
    tractions = [
        pltpu.make_async_copy(sources[0].at[i], traction.at[i], traction_sems.at[i]) for i in range(leaves)
    ]
    basis_copy, *copies = fetch(sources[1:], held, sems)
    for copy in tractions:
        copy.start()
    basis, up_leaf, up_pair, up_device = held[:4]
    weight_ref, stack_ref, send_ref = results
    writes = [pltpu.make_async_copy(r, o, out_sems.at[n]) for n, (r, o) in enumerate(zip(results, outs))]
    for copy in copies:
        copy.wait()
    for n, block in enumerate(weights_of(held[4:], natural)):
        weight_ref[RANK * n : RANK * (n + 1), :] = block
    writes[0].start()
    basis_copy.wait()
    for i in range(leaves):
        tractions[i].wait()
        high, low = split(traction[i])
        stack_ref[RANK * i : RANK * (i + 1), :] = dot_split(basis[i], high, low)
    for p in range(pairs):
        weight = [square(up_leaf[pl.ds(i, ROWS8, stride=leaves), :]) for i in (2 * p, 2 * p + 1)]
        value = [quad_rows(stack_ref, RANK * i) for i in (2 * p, 2 * p + 1)]
        at = RANK * (leaves + p)
        stack_ref[at : at + RANK, :] = dot_first(
            jnp.concatenate(weight, axis=0), jnp.concatenate(value, axis=0)
        )
    writes[1].start()
    weight = [square(up_pair[pl.ds(p, ROWS8, stride=pairs), :]) for p in range(pairs)]
    value = [quad_rows(stack_ref, RANK * (leaves + p)) for p in range(pairs)]
    coeff = dot_first(jnp.concatenate(weight, axis=0), jnp.concatenate(value, axis=0))
    up = up_device[...]
    for d in range(send_ref.shape[0]):
        send_ref[d, 0:RANK, :] = coeff
        send_ref[d, RANK : RANK + ROWS8, :] = up
    writes[2].start()
    for write in writes:
        write.wait()


def far_kernel(
    low_ref, own_ref, high_ref, couple_leaf, couple_pair, down_leaf, down_pair, basis,
    list_leaf, mask_leaf, list_pair, mask_pair, fixed_ref, slope_ref, near_high, near_low, natural,
):
    leaves, slots = list_leaf.shape
    pairs = list_pair.shape[0]
    blocks = leaves + pairs
    top = lax.axis_index("y") * lax.axis_size("core") + lax.axis_index("core")
    leaf = lax.axis_index("x") * lax.axis_size("z") + lax.axis_index("z")
    position = top * (lax.axis_size("x") * lax.axis_size("z")) + leaf
    size = blocks * RANK
    for n, ref in enumerate((low_ref, own_ref, high_ref)):
        high, low = split(ref[...])
        near_high[n * size : (n + 1) * size, :] = high
        near_low[n * size : (n + 1) * size, :] = low
    none = jnp.zeros((RANK, COLS), BF16)
    near_high[3 * size : 3 * size + RANK, :] = none
    near_low[3 * size : 3 * size + RANK, :] = none

    def near(index, mask, per_dev, offset):
        relative = index - position * per_dev + per_dev
        block = relative // per_dev * blocks + offset + relative % per_dev
        start = pl.multiple_of(jnp.where(mask == 0, 3 * blocks, block) * RANK, RANK)
        return near_high[pl.ds(start, RANK), :], near_low[pl.ds(start, RANK), :]

    for p in range(pairs):
        flats = [couple_pair[pl.ds(k * ROWS8 * pairs + p, ROWS8, stride=pairs), :] for k in range(slots)]
        weight = jnp.concatenate([beside(flats[:4]), beside(flats[4:])], axis=1)
        taken = [near(list_pair[p, k], mask_pair[p, k], pairs, leaves) for k in range(slots)]
        rows = [jnp.concatenate([t[n] for t in taken] + [none, none], axis=0) for n in (0, 1)]
        at = 2 * RANK * p
        store_natural(natural, at, dot_split(weight, *rows))
        store_natural(natural, at + RANK, beside([down_pair[pl.ds(p, ROWS8, stride=pairs), :]] * 4))
        sums = split(natural[at : at + RANK, :])
        downs = split(natural[at + RANK : at + 2 * RANK, :])
        for i in (2 * p, 2 * p + 1):
            flats = [
                couple_leaf[pl.ds(k * ROWS8 * leaves + i, ROWS8, stride=leaves), :] for k in range(slots)
            ] + [down_leaf[pl.ds(i, ROWS8, stride=leaves), :]]
            weight = jnp.concatenate([beside(flats[:4]), beside(flats[4:])], axis=1)
            taken = [near(list_leaf[i, k], mask_leaf[i, k], leaves, 0) for k in range(slots)]
            rows = [
                jnp.concatenate(
                    [
                        jnp.concatenate([t[n] for t in taken] + [sums[n], none], axis=0),
                        jnp.concatenate([none] * slots + [downs[n], none], axis=0),
                    ],
                    axis=1,
                )
                for n in (0, 1)
            ]
            here = dot_split(weight, *rows)
            at = 2 * RANK * (pairs + i)
            store_natural(natural, at, here[:, :COLS])
            store_natural(natural, at + RANK, here[:, COLS:])
            here = jnp.concatenate([natural[at : at + RANK, :], natural[at + RANK : at + 2 * RANK, :]], axis=1)
            both = dot_first(basis[i], here)
            fixed_ref[i] = both[:, :COLS]
            slope = both[:, COLS:]
            slope_high = slope.astype(BF16).astype(F32)
            lane = lanes(slope.shape[0])
            slope_ref[i] = jnp.where(
                lane < 64, slope_high, jnp.where(lane < 96, slope - slope_high, 0.0)
            ).astype(BF16)


NEAR = (0, 1, -1)
OFFSETS = (NEAR, tuple(3 + o for o in NEAR), tuple(-3 + o for o in NEAR[:2]))


def part_kernel(own, *refs):
    buffers = len(OFFSETS)
    coeff_ref = refs[0]
    weight_refs, ids_refs = refs[1 : 1 + buffers], refs[1 + buffers : 1 + 2 * buffers]
    before_ref = None if own else refs[1 + 2 * buffers]
    out_ref, coeff_high, coeff_low, gathered = refs[-4:]
    subs = coeff_ref.shape[0]
    rows_y = lax.axis_size("y")
    slots, top_slots = 6, 4
    row, core = lax.axis_index("y"), lax.axis_index("core")
    source = row * 2 + (core if own else 1 - core)
    none = jnp.zeros((RANK, COLS), BF16)
    for d in range(subs):
        value = coeff_ref[d, 0:RANK, :]
        gathered[RANK * d : RANK * (d + 1), :] = value
        high, low = split(value)
        coeff_high[RANK * d : RANK * (d + 1), :] = high
        coeff_low[RANK * d : RANK * (d + 1), :] = low
    coeff_high[RANK * subs : RANK * (subs + 1), :] = none
    coeff_low[RANK * subs : RANK * (subs + 1), :] = none
    up = jnp.concatenate([coeff_ref[d, RANK : RANK + ROWS8, :] for d in range(subs)], axis=0)
    value = jnp.concatenate(
        [gathered[pl.ds(q, ROWS8 * subs, stride=QUADS), :] for q in range(QUADS)], axis=1
    )
    every = dot_first(up, value)
    top = jnp.zeros((RANK, COLS), F32)
    for q in range(QUADS):
        top = top + every[RANK * q : RANK * (q + 1), COLS * q : COLS * (q + 1)]
    lane_group = lanes(RANK) // RANK
    targets = []
    for weight_ref, ids_ref, offsets in zip(weight_refs, ids_refs, OFFSETS):
        targets += [(weight_ref, ids_ref, n, offset) for n, offset in enumerate(offsets)]
    top_weight = []
    for weight_ref, ids_ref, n, _ in targets:
        used = jnp.zeros((RANK, COLS), F32)
        for k in range(top_slots):
            owner = ids_ref[n, 64 + slots + k].astype(jnp.int32)
            used = jnp.where(lane_group == k, jnp.where(owner == source, 1.0, 0.0), used)
        at = RANK * (3 * n + 2)
        top_weight.append(weight_ref[at : at + RANK, :] * used)
    top_high, top_low = split(top)
    top_part = dot_split(
        jnp.concatenate(top_weight, axis=0),
        jnp.concatenate([top_high] * 4, axis=0),
        jnp.concatenate([top_low] * 4, axis=0),
    )

    def starts(ids_ref, n):
        found = []
        for k in range(slots):
            index = ids_ref[n, 64 + k].astype(jnp.int32)
            block = jnp.where(index // subs == source, index % subs, subs)
            found.append(pl.multiple_of(block * RANK, RANK))
        return found

    for t in range(0, rows_y, 2):
        two = targets[t : t + 2]
        pair = [starts(ids_ref, n) for _, ids_ref, n, _ in two]
        rows = [
            jnp.concatenate(
                [jnp.concatenate([ref[pl.ds(s, RANK), :] for s in one], axis=0) for one in pair], axis=1
            )
            for ref in (coeff_high, coeff_low)
        ]
        weight = [
            jnp.concatenate(
                [w[3 * RANK * n : RANK * (3 * n + 1), :], w[RANK * (3 * n + 1) : RANK * (3 * n + 2), :64]],
                axis=1,
            )
            for w, _, n, _ in two
        ]
        both = dot_split(jnp.concatenate(weight, axis=0), *rows)
        for m, (_, _, _, offset) in enumerate(two):
            at = (row + 2 * rows_y - offset * (1 - 2 * core)) % rows_y
            mine = both[RANK * m : RANK * (m + 1), COLS * m : COLS * (m + 1)]
            mine = mine + top_part[RANK * (t + m) : RANK * (t + m + 1)]
            out_ref[at] = mine if own else mine + before_ref[at]


def last_kernel(parts_ref, fixed_ref, slope_ref, out_ref, natural, held, sems):
    total = parts_ref[0]
    for t in range(1, parts_ref.shape[0]):
        total = total + parts_ref[t]
    store_natural(natural, 0, total)
    high, low = split(natural[...])
    rows = jnp.concatenate([high, low, high, jnp.zeros((RANK, COLS), BF16)], axis=0)
    writes = [pltpu.make_async_copy(held.at[i], out_ref.at[i], sems.at[i]) for i in range(held.shape[0])]
    for i, write in enumerate(writes):
        held[i] = fixed_ref[i] + dot(slope_ref[i], rows)
        write.start()
    for write in writes:
        write.wait()


def whole(kernel, out, args, smem=(), hbm=(), scratch=(), flops=0, limit=VMEM_LIMIT, out_hbm=False):
    vmem = pl.BlockSpec(memory_space=pltpu.VMEM)
    scalars = pl.BlockSpec(memory_space=pltpu.SMEM)
    far = pl.BlockSpec(memory_space=pltpu.HBM)
    place = far if out_hbm else vmem
    size = sum(a.size * a.dtype.itemsize for a in args)
    outs = out if isinstance(out, tuple) else (out,)
    size += sum(o.size * o.dtype.itemsize for o in outs)
    return pl.pallas_call(
        kernel,
        out_shape=out,
        in_specs=[scalars if n in smem else far if n in hbm else vmem for n in range(len(args))],
        out_specs=tuple(place for _ in out) if isinstance(out, tuple) else place,
        scratch_shapes=list(scratch),
        compiler_params=pltpu.CompilerParams(vmem_limit_bytes=limit),
        cost_estimate=pl.CostEstimate(flops=flops, bytes_accessed=size, transcendentals=0),
    )(*args)


def rows_of(x):
    if x.ndim == 2:
        return x.reshape(x.shape[0], ROWS8, COLS).transpose(1, 0, 2).reshape(-1, COLS)
    return x.reshape(x.shape[0], x.shape[1], ROWS8, COLS).transpose(1, 2, 0, 3).reshape(-1, COLS)


def body(
    traction_vectors,
    row_basis,
    up_leaf,
    up_pair,
    up_device,
    couple_leaf,
    pair_coupling_blocks,
    couple_device,
    couple_top,
    list_leaf,
    list_pair,
    list_device,
    list_top,
    mask_leaf,
    mask_pair,
    mask_device,
    mask_top,
    down_leaf,
    down_pair,
    down_device,
    col_basis,
):
    def shape(*dims, dtype=F32):
        return jax.ShapeDtypeStruct(dims, dtype)

    leaves, entries, _ = traction_vectors.shape
    blocks = leaves + leaves // 2
    targets = lax.axis_size("y")
    subs = lax.axis_size("x") * lax.axis_size("z")
    def fetched(args):
        return [pltpu.VMEM(a.shape, a.dtype) for a in args] + [pltpu.SemaphoreType.DMA((len(args),))]

    first = (
        traction_vectors, row_basis, rows_of(up_leaf), rows_of(up_pair), rows_of(up_device),
        rows_of(couple_device), rows_of(down_device), rows_of(couple_top[0]),
        list_device, mask_device, list_top, mask_top,
    )
    results = (shape(3 * RANK, COLS), shape(blocks * RANK, COLS), shape(subs, RANK + ROWS8, COLS))
    weights, stack, send = whole(
        first_kernel,
        results,
        first,
        hbm=range(len(first)),
        out_hbm=True,
        scratch=[
            *fetched(first[1:]),
            pltpu.VMEM(traction_vectors.shape, F32),
            pltpu.SemaphoreType.DMA((leaves,)),
            pltpu.VMEM((RANK, COLS), F32),
            *fetched(results),
        ],
        flops=6 * 10**7,
        limit=ALMOST_ALL,
    )

    def over_y(block, step):
        moves = []
        for y in range(targets):
            moves.append((2 * y, 2 * ((y + step) % targets)))
            moves.append((2 * y + 1, 2 * ((y - step) % targets) + 1))
        return lax.ppermute(block, ("y", "core"), moves)

    weights = jnp.concatenate([weights, over_y(weights, 1), over_y(weights, -1)], axis=0)
    coeffs = lax.all_to_all(send, ("x", "z"), 0, 0, tiled=True)
    weights = [weights, over_y(weights, 3), over_y(weights[: 2 * 3 * RANK], -3)]
    leaf_axes = ("x", "z")
    low = lax.ppermute(stack, leaf_axes, [(i, i + 1) for i in range(subs - 1)])
    high = lax.ppermute(stack, leaf_axes, [(i + 1, i) for i in range(subs - 1)])
    near = pltpu.VMEM(((3 * blocks + 1) * RANK, COLS), BF16)
    fixed, slope = whole(
        far_kernel,
        (shape(leaves, entries, COLS), shape(leaves, entries, COLS, dtype=BF16)),
        (
            low, stack, high, rows_of(couple_leaf), rows_of(pair_coupling_blocks),
            rows_of(down_leaf), rows_of(down_pair), col_basis,
            list_leaf, mask_leaf, list_pair, mask_pair,
        ),
        smem=(8, 9, 10, 11),
        scratch=[near, near, pltpu.VMEM((2 * RANK * blocks, COLS), F32)],
        flops=10**8,
    )
    coeffs, weights, fixed, slope = lax.optimization_barrier((coeffs, weights, fixed, slope))
    other = lax.ppermute(coeffs, "core", [(0, 1), (1, 0)])
    weights = [*weights, *(block[RANK :: 3 * RANK] for block in weights)]
    count = len(weights) // 2
    parts = []
    for own, gathered in ((True, coeffs), (False, other)):
        parts = whole(
            functools.partial(part_kernel, own),
            shape(targets, RANK, COLS),
            (gathered, *weights, *([] if own else [parts])),
            smem=range(1 + count, 1 + 2 * count),
            scratch=[
                pltpu.VMEM(((subs + 1) * RANK, COLS), BF16),
                pltpu.VMEM(((subs + 1) * RANK, COLS), BF16),
                pltpu.VMEM((subs * RANK, COLS), F32),
            ],
            flops=5 * 10**7,
        )
    parts = lax.all_to_all(parts, "y", 0, 0, tiled=True)
    return whole(
        last_kernel,
        shape(leaves, entries, COLS),
        (parts, fixed, slope),
        out_hbm=True,
        scratch=[
            pltpu.VMEM((RANK, COLS), F32),
            pltpu.VMEM((leaves, entries, COLS), F32),
            pltpu.SemaphoreType.DMA((leaves,)),
        ],
        flops=5 * 10**7,
    )


def solution(mesh):
    deep = max(1, mesh.shape["leaf"] // 4)
    sizes = (mesh.shape["top"] // 2, 2, mesh.shape["leaf"] // deep, deep)
    fine = jax.sharding.Mesh(mesh.devices.reshape(sizes), ("y", "core", "x", "z"))
    top, both = ("y", "core"), ("y", "core", "x", "z")
    return jax.shard_map(
        body,
        mesh=fine,
        in_specs=(
            P(both, None, None),
            P(both, None, None),
            P(both, None),
            P(both, None),
            P(both, None),
            P(both, None, None),
            P(both, None, None),
            P(both, None, None),
            P(top, None, None),
            P(both, None),
            P(both, None),
            P(both, None),
            P(top, None),
            P(both, None),
            P(both, None),
            P(both, None),
            P(top, None),
            P(both, None),
            P(both, None),
            P(both, None),
            P(both, None, None),
        ),
        out_specs=P(both, None, None),
        check_vma=False,
    )
```

```python
import functools

import jax
import jax.numpy as jnp
from jax import lax
from jax.experimental import pallas as pl
from jax.experimental.pallas import tpu as pltpu
from jax.sharding import PartitionSpec as P

RANK = 32
COLS = 128
QUADS = 4
ROWS8 = 8
F32 = jnp.float32
BF16 = jnp.bfloat16
VMEM_LIMIT = 32 * 1024 * 1024
ALMOST_ALL = 60 * 1024 * 1024


def split(x):
    high = x.astype(BF16)
    return high, (x - high.astype(F32)).astype(BF16)


def dot(a, b, contract=((1,), (0,))):
    return lax.dot_general(a, b, (contract, ((), ())), preferred_element_type=F32)


def dot_split(a, b_high, b_low):
    rows = a.shape[0]
    a_high, a_low = split(a)
    both = dot(jnp.concatenate([a_high, a_low], axis=0), b_high)
    return both[:rows] + both[rows:] + dot(a_high, b_low)


def dot_first(a, b):
    a_high, a_low = split(a)
    b_high, b_low = split(b)
    return dot(
        jnp.concatenate([a_high, a_high, a_low], axis=0),
        jnp.concatenate([b_high, b_low, b_high], axis=0),
        ((0,), (0,)),
    )


def lanes(rows=ROWS8):
    return lax.broadcasted_iota(jnp.int32, (rows, COLS), 1)


def square(flat):
    return jnp.concatenate([flat[:, RANK * q : RANK * (q + 1)] for q in range(QUADS)], axis=0)


def beside(flats):
    group = lanes() // RANK
    rows = []
    for q in range(QUADS):
        row = None
        for k, flat in enumerate(flats):
            shift = (RANK * (k - q)) % COLS
            moved = pltpu.roll(flat, shift, 1) if shift else flat
            row = moved if row is None else jnp.where(group == k, moved, row)
        rows.append(row)
    return jnp.concatenate(rows, axis=0)


def quad_rows(ref, start):
    return jnp.concatenate(
        [ref[pl.ds(start + q, ROWS8, stride=QUADS), :] for q in range(QUADS)], axis=0
    )


def store_natural(ref, start, x):
    for q in range(QUADS):
        ref[pl.ds(start + q, ROWS8, stride=QUADS), :] = x[ROWS8 * q : ROWS8 * (q + 1)]


def fetch(sources, held, sems):
    copies = [pltpu.make_async_copy(s, h, sems.at[n]) for n, (s, h) in enumerate(zip(sources, held))]
    for copy in copies:
        copy.start()
    return copies


def weights_of(held, natural):
    couple, down, top, list_d, mask_d, list_t, mask_t = held
    slots, top_slots = list_d.shape[1], list_t.shape[1]

    def entry(ref, k):
        return ref[0:1, k : k + 1].astype(F32)

    flats = [couple[ROWS8 * k : ROWS8 * (k + 1), :] * entry(mask_d, k) for k in range(slots)]
    lane = lanes(RANK)
    ids = jnp.zeros((RANK, COLS), F32)
    for k in range(slots):
        ids = jnp.where(lane == 64 + k, entry(list_d, k), ids)
    for k in range(top_slots):
        ids = jnp.where(lane == 64 + slots + k, entry(list_t, k), ids)
    tops = [top[pl.ds(k, ROWS8, stride=top_slots), :] * entry(mask_t, k) for k in range(top_slots)]
    store_natural(natural, 0, beside(tops))
    top_high, top_low = split(natural[...])
    return (
        beside(flats[:4]),
        jnp.where(lane < 64, beside(flats[4:]), ids),
        dot_split(square(down[...]), top_high, top_low),
    )


def first_kernel(*refs):
    sources, outs, scratch = refs[:12], refs[12:15], refs[15:]
    held, (sems, traction, traction_sems, natural) = scratch[:11], scratch[11:15]
    results, out_sems = scratch[15:18], scratch[18]
    leaves = sources[0].shape[0]
    pairs = leaves // 2
    tractions = [
        pltpu.make_async_copy(sources[0].at[i], traction.at[i], traction_sems.at[i]) for i in range(leaves)
    ]
    basis_copy, *copies = fetch(sources[1:], held, sems)
    for copy in tractions:
        copy.start()
    basis, up_leaf, up_pair, up_device = held[:4]
    weight_ref, stack_ref, send_ref = results
    writes = [pltpu.make_async_copy(r, o, out_sems.at[n]) for n, (r, o) in enumerate(zip(results, outs))]
    for copy in copies:
        copy.wait()
    for n, block in enumerate(weights_of(held[4:], natural)):
        weight_ref[0, RANK * n : RANK * (n + 1), :] = block
    writes[0].start()
    basis_copy.wait()
    for i in range(leaves):
        tractions[i].wait()
        high, low = split(traction[i])
        stack_ref[RANK * i : RANK * (i + 1), :] = dot_split(basis[i], high, low)
    for p in range(pairs):
        weight = [square(up_leaf[pl.ds(i, ROWS8, stride=leaves), :]) for i in (2 * p, 2 * p + 1)]
        value = [quad_rows(stack_ref, RANK * i) for i in (2 * p, 2 * p + 1)]
        at = RANK * (leaves + p)
        stack_ref[at : at + RANK, :] = dot_first(
            jnp.concatenate(weight, axis=0), jnp.concatenate(value, axis=0)
        )
    writes[1].start()
    weight = [square(up_pair[pl.ds(p, ROWS8, stride=pairs), :]) for p in range(pairs)]
    value = [quad_rows(stack_ref, RANK * (leaves + p)) for p in range(pairs)]
    coeff = dot_first(jnp.concatenate(weight, axis=0), jnp.concatenate(value, axis=0))
    up = up_device[...]
    for d in range(send_ref.shape[0]):
        send_ref[d, 0:RANK, :] = coeff
        send_ref[d, RANK : RANK + ROWS8, :] = up
    writes[2].start()
    for write in writes:
        write.wait()


def far_kernel(
    low_ref, own_ref, high_ref, couple_leaf, couple_pair, down_leaf, down_pair, basis,
    list_leaf, mask_leaf, list_pair, mask_pair, fixed_ref, slope_ref, near_high, near_low, natural,
):
    leaves, slots = list_leaf.shape
    pairs = list_pair.shape[0]
    blocks = leaves + pairs
    top = lax.axis_index("y") * lax.axis_size("core") + lax.axis_index("core")
    leaf = lax.axis_index("x") * lax.axis_size("z") + lax.axis_index("z")
    position = top * (lax.axis_size("x") * lax.axis_size("z")) + leaf
    size = blocks * RANK
    swap = 2 * lax.axis_index("core")
    for n, ref in ((swap, low_ref), (1, own_ref), (2 - swap, high_ref)):
        high, low = split(ref[...])
        start = pl.multiple_of(n * size, size)
        near_high[pl.ds(start, size), :] = high
        near_low[pl.ds(start, size), :] = low
    none = jnp.zeros((RANK, COLS), BF16)
    near_high[3 * size : 3 * size + RANK, :] = none
    near_low[3 * size : 3 * size + RANK, :] = none

    def near(index, mask, per_dev, offset):
        relative = index - position * per_dev + per_dev
        block = relative // per_dev * blocks + offset + relative % per_dev
        start = pl.multiple_of(jnp.where(mask == 0, 3 * blocks, block) * RANK, RANK)
        return near_high[pl.ds(start, RANK), :], near_low[pl.ds(start, RANK), :]

    for p in range(pairs):
        flats = [couple_pair[pl.ds(k * ROWS8 * pairs + p, ROWS8, stride=pairs), :] for k in range(slots)]
        weight = jnp.concatenate([beside(flats[:4]), beside(flats[4:])], axis=1)
        taken = [near(list_pair[p, k], mask_pair[p, k], pairs, leaves) for k in range(slots)]
        rows = [jnp.concatenate([t[n] for t in taken] + [none, none], axis=0) for n in (0, 1)]
        at = 2 * RANK * p
        store_natural(natural, at, dot_split(weight, *rows))
        store_natural(natural, at + RANK, beside([down_pair[pl.ds(p, ROWS8, stride=pairs), :]] * 4))
        sums = split(natural[at : at + RANK, :])
        downs = split(natural[at + RANK : at + 2 * RANK, :])
        for i in (2 * p, 2 * p + 1):
            flats = [
                couple_leaf[pl.ds(k * ROWS8 * leaves + i, ROWS8, stride=leaves), :] for k in range(slots)
            ] + [down_leaf[pl.ds(i, ROWS8, stride=leaves), :]]
            weight = jnp.concatenate([beside(flats[:4]), beside(flats[4:])], axis=1)
            taken = [near(list_leaf[i, k], mask_leaf[i, k], leaves, 0) for k in range(slots)]
            rows = [
                jnp.concatenate(
                    [
                        jnp.concatenate([t[n] for t in taken] + [sums[n], none], axis=0),
                        jnp.concatenate([none] * slots + [downs[n], none], axis=0),
                    ],
                    axis=1,
                )
                for n in (0, 1)
            ]
            here = dot_split(weight, *rows)
            at = 2 * RANK * (pairs + i)
            store_natural(natural, at, here[:, :COLS])
            store_natural(natural, at + RANK, here[:, COLS:])
            here = jnp.concatenate([natural[at : at + RANK, :], natural[at + RANK : at + 2 * RANK, :]], axis=1)
            both = dot_first(basis[i], here)
            fixed_ref[i] = both[:, :COLS]
            slope = both[:, COLS:]
            slope_high = slope.astype(BF16).astype(F32)
            lane = lanes(slope.shape[0])
            slope_ref[i] = jnp.where(
                lane < 64, slope_high, jnp.where(lane < 96, slope - slope_high, 0.0)
            ).astype(BF16)


def shifts(count):
    half = count // 2
    return [s if s <= half // 2 else s - half for s in range(1, half)]


def part_kernel(own, *refs):
    buffers = (len(refs) - (5 if own else 6)) // 2
    coeff_ref = refs[0]
    weight_refs, ids_refs = refs[1 : 1 + buffers], refs[1 + buffers : 1 + 2 * buffers]
    before_ref = None if own else refs[1 + 2 * buffers]
    out_ref, coeff_high, coeff_low, gathered = refs[-4:]
    subs = coeff_ref.shape[0]
    rows_y = 2 * buffers
    slots, top_slots = 6, 4
    row, core = lax.axis_index("y"), lax.axis_index("core")
    source = row * 2 + (core if own else 1 - core)
    none = jnp.zeros((RANK, COLS), BF16)
    for d in range(subs):
        value = coeff_ref[d, 0:RANK, :]
        gathered[RANK * d : RANK * (d + 1), :] = value
        high, low = split(value)
        coeff_high[RANK * d : RANK * (d + 1), :] = high
        coeff_low[RANK * d : RANK * (d + 1), :] = low
    coeff_high[RANK * subs : RANK * (subs + 1), :] = none
    coeff_low[RANK * subs : RANK * (subs + 1), :] = none
    up = jnp.concatenate([coeff_ref[d, RANK : RANK + ROWS8, :] for d in range(subs)], axis=0)
    value = jnp.concatenate(
        [gathered[pl.ds(q, ROWS8 * subs, stride=QUADS), :] for q in range(QUADS)], axis=1
    )
    every = dot_first(up, value)
    top = jnp.zeros((RANK, COLS), F32)
    for q in range(QUADS):
        top = top + every[RANK * q : RANK * (q + 1), COLS * q : COLS * (q + 1)]
    lane_group = lanes(RANK) // RANK
    targets = []
    for weight_ref, ids_ref, shift in zip(weight_refs, ids_refs, [0] + shifts(rows_y)):
        targets += [(weight_ref, ids_ref, n, shift + n * buffers) for n in range(2)]
    top_weight = []
    for weight_ref, ids_ref, n, _ in targets:
        used = jnp.zeros((RANK, COLS), F32)
        for k in range(top_slots):
            owner = ids_ref[n, 64 + slots + k].astype(jnp.int32)
            used = jnp.where(lane_group == k, jnp.where(owner == source, 1.0, 0.0), used)
        top_weight.append(weight_ref[n, 2 * RANK : 3 * RANK, :] * used)
    top_high, top_low = split(top)
    top_part = dot_split(
        jnp.concatenate(top_weight, axis=0),
        jnp.concatenate([top_high] * 4, axis=0),
        jnp.concatenate([top_low] * 4, axis=0),
    )

    def starts(ids_ref, n):
        found = []
        for k in range(slots):
            index = ids_ref[n, 64 + k].astype(jnp.int32)
            block = jnp.where(index // subs == source, index % subs, subs)
            found.append(pl.multiple_of(block * RANK, RANK))
        return found

    for t in range(0, rows_y, 2):
        two = targets[t : t + 2]
        pair = [starts(ids_ref, n) for _, ids_ref, n, _ in two]
        rows = [
            jnp.concatenate(
                [jnp.concatenate([ref[pl.ds(s, RANK), :] for s in one], axis=0) for one in pair], axis=1
            )
            for ref in (coeff_high, coeff_low)
        ]
        weight = [
            jnp.concatenate([w[n, 0:RANK, :], w[n, RANK : 2 * RANK, :64]], axis=1) for w, _, n, _ in two
        ]
        both = dot_split(jnp.concatenate(weight, axis=0), *rows)
        for m, (_, _, _, offset) in enumerate(two):
            at = (row + 2 * rows_y - offset * (1 - 2 * core)) % rows_y
            mine = both[RANK * m : RANK * (m + 1), COLS * m : COLS * (m + 1)]
            mine = mine + top_part[RANK * (t + m) : RANK * (t + m + 1)]
            out_ref[at] = mine if own else mine + before_ref[at]


def last_kernel(parts_ref, fixed_ref, slope_ref, out_ref, natural, held, sems):
    total = parts_ref[0]
    for t in range(1, parts_ref.shape[0]):
        total = total + parts_ref[t]
    store_natural(natural, 0, total)
    high, low = split(natural[...])
    rows = jnp.concatenate([high, low, high, jnp.zeros((RANK, COLS), BF16)], axis=0)
    writes = [pltpu.make_async_copy(held.at[i], out_ref.at[i], sems.at[i]) for i in range(held.shape[0])]
    for i, write in enumerate(writes):
        held[i] = fixed_ref[i] + dot(slope_ref[i], rows)
        write.start()
    for write in writes:
        write.wait()


def whole(kernel, out, args, smem=(), hbm=(), scratch=(), flops=0, limit=VMEM_LIMIT, out_hbm=False):
    vmem = pl.BlockSpec(memory_space=pltpu.VMEM)
    scalars = pl.BlockSpec(memory_space=pltpu.SMEM)
    far = pl.BlockSpec(memory_space=pltpu.HBM)
    place = far if out_hbm else vmem
    size = sum(a.size * a.dtype.itemsize for a in args)
    outs = out if isinstance(out, tuple) else (out,)
    size += sum(o.size * o.dtype.itemsize for o in outs)
    return pl.pallas_call(
        kernel,
        out_shape=out,
        in_specs=[scalars if n in smem else far if n in hbm else vmem for n in range(len(args))],
        out_specs=tuple(place for _ in out) if isinstance(out, tuple) else place,
        scratch_shapes=list(scratch),
        compiler_params=pltpu.CompilerParams(vmem_limit_bytes=limit),
        cost_estimate=pl.CostEstimate(flops=flops, bytes_accessed=size, transcendentals=0),
    )(*args)


def rows_of(x):
    if x.ndim == 2:
        return x.reshape(x.shape[0], ROWS8, COLS).transpose(1, 0, 2).reshape(-1, COLS)
    return x.reshape(x.shape[0], x.shape[1], ROWS8, COLS).transpose(1, 2, 0, 3).reshape(-1, COLS)


def body(
    traction_vectors,
    row_basis,
    up_leaf,
    up_pair,
    up_device,
    couple_leaf,
    pair_coupling_blocks,
    couple_device,
    couple_top,
    list_leaf,
    list_pair,
    list_device,
    list_top,
    mask_leaf,
    mask_pair,
    mask_device,
    mask_top,
    down_leaf,
    down_pair,
    down_device,
    col_basis,
):
    def shape(*dims, dtype=F32):
        return jax.ShapeDtypeStruct(dims, dtype)

    leaves, entries, _ = traction_vectors.shape
    blocks = leaves + leaves // 2
    targets = lax.axis_size("y")
    subs = lax.axis_size("x") * lax.axis_size("z")
    def fetched(args):
        return [pltpu.VMEM(a.shape, a.dtype) for a in args] + [pltpu.SemaphoreType.DMA((len(args),))]

    first = (
        traction_vectors, row_basis, rows_of(up_leaf), rows_of(up_pair), rows_of(up_device),
        rows_of(couple_device), rows_of(down_device), rows_of(couple_top[0]),
        list_device, mask_device, list_top, mask_top,
    )
    results = (shape(1, 3 * RANK, COLS), shape(blocks * RANK, COLS), shape(subs, RANK + ROWS8, COLS))
    weights, stack, send = whole(
        first_kernel,
        results,
        first,
        hbm=range(len(first)),
        out_hbm=True,
        scratch=[
            *fetched(first[1:]),
            pltpu.VMEM(traction_vectors.shape, F32),
            pltpu.SemaphoreType.DMA((leaves,)),
            pltpu.VMEM((RANK, COLS), F32),
            *fetched(results),
        ],
        flops=6 * 10**7,
        limit=ALMOST_ALL,
    )

    def over_y(block, step):
        moves = []
        for y in range(targets):
            moves.append((2 * y, 2 * ((y + step) % targets)))
            moves.append((2 * y + 1, 2 * ((y - step) % targets) + 1))
        return lax.ppermute(block, ("y", "core"), moves)

    weights = jnp.concatenate([weights, over_y(weights, targets // 2)], axis=0)
    coeffs = lax.all_to_all(send, ("x", "z"), 0, 0, tiled=True)
    weights = [weights] + [over_y(weights, step) for step in shifts(targets)]
    leaf_axes = ("x", "z")
    up = [(i, i + 1) for i in range(subs - 1)]
    down = [(i + 1, i) for i in range(subs - 1)]

    def halo(first, second):
        moves = first + [(subs + i, subs + j) for i, j in second]
        return lax.ppermute(stack, ("core", *leaf_axes), moves)

    low, high = halo(up, down), halo(down, up)
    near = pltpu.VMEM(((3 * blocks + 1) * RANK, COLS), BF16)
    fixed, slope = whole(
        far_kernel,
        (shape(leaves, entries, COLS), shape(leaves, entries, COLS, dtype=BF16)),
        (
            low, stack, high, rows_of(couple_leaf), rows_of(pair_coupling_blocks),
            rows_of(down_leaf), rows_of(down_pair), col_basis,
            list_leaf, mask_leaf, list_pair, mask_pair,
        ),
        smem=(8, 9, 10, 11),
        scratch=[near, near, pltpu.VMEM((2 * RANK * blocks, COLS), F32)],
        flops=10**8,
    )
    coeffs, weights, fixed, slope = lax.optimization_barrier((coeffs, weights, fixed, slope))
    other = lax.ppermute(coeffs, "core", [(0, 1), (1, 0)])
    weights = [*weights, *(block[:, RANK, :] for block in weights)]
    count = len(weights) // 2
    parts = []
    for own, gathered in ((True, coeffs), (False, other)):
        parts = whole(
            functools.partial(part_kernel, own),
            shape(targets, RANK, COLS),
            (gathered, *weights, *([] if own else [parts])),
            smem=range(1 + count, 1 + 2 * count),
            scratch=[
                pltpu.VMEM(((subs + 1) * RANK, COLS), BF16),
                pltpu.VMEM(((subs + 1) * RANK, COLS), BF16),
                pltpu.VMEM((subs * RANK, COLS), F32),
            ],
            flops=5 * 10**7,
        )
    parts = lax.all_to_all(parts, "y", 0, 0, tiled=True)
    return whole(
        last_kernel,
        shape(leaves, entries, COLS),
        (parts, fixed, slope),
        out_hbm=True,
        scratch=[
            pltpu.VMEM((RANK, COLS), F32),
            pltpu.VMEM((leaves, entries, COLS), F32),
            pltpu.SemaphoreType.DMA((leaves,)),
        ],
        flops=5 * 10**7,
    )


def solution(mesh):
    deep = max(1, mesh.shape["leaf"] // 4)
    sizes = (mesh.shape["top"] // 2, 2, mesh.shape["leaf"] // deep, deep)
    fine = jax.sharding.Mesh(mesh.devices.reshape(sizes), ("y", "core", "x", "z"))
    top, both = ("y", "core"), ("y", "core", "x", "z")
    return jax.shard_map(
        body,
        mesh=fine,
        in_specs=(
            P(both, None, None),
            P(both, None, None),
            P(both, None),
            P(both, None),
            P(both, None),
            P(both, None, None),
            P(both, None, None),
            P(both, None, None),
            P(top, None, None),
            P(both, None),
            P(both, None),
            P(both, None),
            P(top, None),
            P(both, None),
            P(both, None),
            P(both, None),
            P(top, None),
            P(both, None),
            P(both, None),
            P(both, None),
            P(both, None, None),
        ),
        out_specs=P(both, None, None),
        check_vma=False,
    )
```

```python
import functools

import jax
import jax.numpy as jnp
from jax import lax
from jax.experimental import pallas as pl
from jax.experimental.pallas import tpu as pltpu
from jax.sharding import PartitionSpec as P

RANK = 32
COLS = 128
QUADS = 4
ROWS8 = 8
F32 = jnp.float32
BF16 = jnp.bfloat16
VMEM_LIMIT = 32 * 1024 * 1024
ALMOST_ALL = 60 * 1024 * 1024


def split(x):
    high = x.astype(BF16)
    return high, (x - high.astype(F32)).astype(BF16)


def dot(a, b, contract=((1,), (0,))):
    return lax.dot_general(a, b, (contract, ((), ())), preferred_element_type=F32)


def dot_split(a, b_high, b_low):
    rows = a.shape[0]
    a_high, a_low = split(a)
    both = dot(jnp.concatenate([a_high, a_low], axis=0), b_high)
    return both[:rows] + both[rows:] + dot(a_high, b_low)


def dot_first(a, b):
    a_high, a_low = split(a)
    b_high, b_low = split(b)
    return dot(
        jnp.concatenate([a_high, a_high, a_low], axis=0),
        jnp.concatenate([b_high, b_low, b_high], axis=0),
        ((0,), (0,)),
    )


def lanes(rows=ROWS8):
    return lax.broadcasted_iota(jnp.int32, (rows, COLS), 1)


def square(flat):
    return jnp.concatenate([flat[:, RANK * q : RANK * (q + 1)] for q in range(QUADS)], axis=0)


def beside(flats):
    group = lanes() // RANK
    rows = []
    for q in range(QUADS):
        row = None
        for k, flat in enumerate(flats):
            shift = (RANK * (k - q)) % COLS
            moved = pltpu.roll(flat, shift, 1) if shift else flat
            row = moved if row is None else jnp.where(group == k, moved, row)
        rows.append(row)
    return jnp.concatenate(rows, axis=0)


def quad_rows(ref, start):
    return jnp.concatenate(
        [ref[pl.ds(start + q, ROWS8, stride=QUADS), :] for q in range(QUADS)], axis=0
    )


def store_natural(ref, start, x):
    for q in range(QUADS):
        ref[pl.ds(start + q, ROWS8, stride=QUADS), :] = x[ROWS8 * q : ROWS8 * (q + 1)]


def fetch(sources, held, sems):
    copies = [pltpu.make_async_copy(s, h, sems.at[n]) for n, (s, h) in enumerate(zip(sources, held))]
    for copy in copies:
        copy.start()
    return copies


def weights_of(held, natural):
    couple, down, top, list_d, mask_d, list_t, mask_t = held
    slots, top_slots = list_d.shape[1], list_t.shape[1]

    def entry(ref, k):
        return ref[0:1, k : k + 1].astype(F32)

    flats = [couple[ROWS8 * k : ROWS8 * (k + 1), :] * entry(mask_d, k) for k in range(slots)]
    lane = lanes(RANK)
    ids = jnp.zeros((RANK, COLS), F32)
    for k in range(slots):
        ids = jnp.where(lane == 64 + k, entry(list_d, k), ids)
    for k in range(top_slots):
        ids = jnp.where(lane == 64 + slots + k, entry(list_t, k), ids)
    tops = [top[pl.ds(k, ROWS8, stride=top_slots), :] * entry(mask_t, k) for k in range(top_slots)]
    store_natural(natural, 0, beside(tops))
    top_high, top_low = split(natural[...])
    return (
        beside(flats[:4]),
        jnp.where(lane < 64, beside(flats[4:]), ids),
        dot_split(square(down[...]), top_high, top_low),
    )


def first_kernel(*refs):
    sources, outs, scratch = refs[:12], refs[12:15], refs[15:]
    held, (sems, traction, traction_sems, natural) = scratch[:11], scratch[11:15]
    results, out_sems = scratch[15:18], scratch[18]
    leaves = sources[0].shape[0]
    pairs = leaves // 2
    tractions = [
        pltpu.make_async_copy(sources[0].at[i], traction.at[i], traction_sems.at[i]) for i in range(leaves)
    ]
    basis_copy, *copies = fetch(sources[1:], held, sems)
    for copy in tractions:
        copy.start()
    basis, up_leaf, up_pair, up_device = held[:4]
    weight_ref, stack_ref, send_ref = results
    writes = [pltpu.make_async_copy(r, o, out_sems.at[n]) for n, (r, o) in enumerate(zip(results, outs))]
    for copy in copies:
        copy.wait()
    basis_copy.wait()
    for i in range(leaves):
        tractions[i].wait()
        high, low = split(traction[i])
        stack_ref[RANK * i : RANK * (i + 1), :] = dot_split(basis[i], high, low)
    for p in range(pairs):
        weight = [square(up_leaf[pl.ds(i, ROWS8, stride=leaves), :]) for i in (2 * p, 2 * p + 1)]
        value = [quad_rows(stack_ref, RANK * i) for i in (2 * p, 2 * p + 1)]
        at = RANK * (leaves + p)
        stack_ref[at : at + RANK, :] = dot_first(
            jnp.concatenate(weight, axis=0), jnp.concatenate(value, axis=0)
        )
    writes[1].start()
    weight = [square(up_pair[pl.ds(p, ROWS8, stride=pairs), :]) for p in range(pairs)]
    value = [quad_rows(stack_ref, RANK * (leaves + p)) for p in range(pairs)]
    coeff = dot_first(jnp.concatenate(weight, axis=0), jnp.concatenate(value, axis=0))
    up = up_device[...]
    for d in range(send_ref.shape[0]):
        send_ref[d, 0:RANK, :] = coeff
        send_ref[d, RANK : RANK + ROWS8, :] = up
    writes[2].start()
    for n, block in enumerate(weights_of(held[4:], natural)):
        weight_ref[0, RANK * n : RANK * (n + 1), :] = block
    writes[0].start()
    for write in writes:
        write.wait()


def far_kernel(
    low_ref, own_ref, high_ref, couple_leaf, couple_pair, down_leaf, down_pair, basis,
    list_leaf, mask_leaf, list_pair, mask_pair, fixed_ref, slope_ref, near_high, near_low, natural,
):
    leaves, slots = list_leaf.shape
    pairs = list_pair.shape[0]
    blocks = leaves + pairs
    top = lax.axis_index("y") * lax.axis_size("core") + lax.axis_index("core")
    leaf = lax.axis_index("x") * lax.axis_size("z") + lax.axis_index("z")
    position = top * (lax.axis_size("x") * lax.axis_size("z")) + leaf
    size = blocks * RANK
    for n, ref in enumerate((low_ref, own_ref, high_ref)):
        high, low = split(ref[...])
        near_high[n * size : (n + 1) * size, :] = high
        near_low[n * size : (n + 1) * size, :] = low
    none = jnp.zeros((RANK, COLS), BF16)
    near_high[3 * size : 3 * size + RANK, :] = none
    near_low[3 * size : 3 * size + RANK, :] = none

    def near(index, mask, per_dev, offset):
        relative = index - position * per_dev + per_dev
        block = relative // per_dev * blocks + offset + relative % per_dev
        start = pl.multiple_of(jnp.where(mask == 0, 3 * blocks, block) * RANK, RANK)
        return near_high[pl.ds(start, RANK), :], near_low[pl.ds(start, RANK), :]

    for p in range(pairs):
        flats = [couple_pair[pl.ds(k * ROWS8 * pairs + p, ROWS8, stride=pairs), :] for k in range(slots)]
        weight = jnp.concatenate([beside(flats[:4]), beside(flats[4:])], axis=1)
        taken = [near(list_pair[p, k], mask_pair[p, k], pairs, leaves) for k in range(slots)]
        rows = [jnp.concatenate([t[n] for t in taken] + [none, none], axis=0) for n in (0, 1)]
        at = 2 * RANK * p
        store_natural(natural, at, dot_split(weight, *rows))
        store_natural(natural, at + RANK, beside([down_pair[pl.ds(p, ROWS8, stride=pairs), :]] * 4))
        sums = split(natural[at : at + RANK, :])
        downs = split(natural[at + RANK : at + 2 * RANK, :])
        for i in (2 * p, 2 * p + 1):
            flats = [
                couple_leaf[pl.ds(k * ROWS8 * leaves + i, ROWS8, stride=leaves), :] for k in range(slots)
            ] + [down_leaf[pl.ds(i, ROWS8, stride=leaves), :]]
            weight = jnp.concatenate([beside(flats[:4]), beside(flats[4:])], axis=1)
            taken = [near(list_leaf[i, k], mask_leaf[i, k], leaves, 0) for k in range(slots)]
            rows = [
                jnp.concatenate(
                    [
                        jnp.concatenate([t[n] for t in taken] + [sums[n], none], axis=0),
                        jnp.concatenate([none] * slots + [downs[n], none], axis=0),
                    ],
                    axis=1,
                )
                for n in (0, 1)
            ]
            here = dot_split(weight, *rows)
            at = 2 * RANK * (pairs + i)
            store_natural(natural, at, here[:, :COLS])
            store_natural(natural, at + RANK, here[:, COLS:])
            here = jnp.concatenate([natural[at : at + RANK, :], natural[at + RANK : at + 2 * RANK, :]], axis=1)
            both = dot_first(basis[i], here)
            fixed_ref[i] = both[:, :COLS]
            slope = both[:, COLS:]
            slope_high = slope.astype(BF16).astype(F32)
            lane = lanes(slope.shape[0])
            slope_ref[i] = jnp.where(
                lane < 64, slope_high, jnp.where(lane < 96, slope - slope_high, 0.0)
            ).astype(BF16)


def shifts(count):
    half = count // 2
    return [s if s <= half // 2 else s - half for s in range(1, half)]


def part_kernel(own, *refs):
    buffers = (len(refs) - (5 if own else 6)) // 2
    coeff_ref = refs[0]
    weight_refs, ids_refs = refs[1 : 1 + buffers], refs[1 + buffers : 1 + 2 * buffers]
    before_ref = None if own else refs[1 + 2 * buffers]
    out_ref, coeff_high, coeff_low, gathered = refs[-4:]
    subs = coeff_ref.shape[0]
    rows_y = 2 * buffers
    slots, top_slots = 6, 4
    row, core = lax.axis_index("y"), lax.axis_index("core")
    source = row * 2 + (core if own else 1 - core)
    none = jnp.zeros((RANK, COLS), BF16)
    for d in range(subs):
        value = coeff_ref[d, 0:RANK, :]
        gathered[RANK * d : RANK * (d + 1), :] = value
        high, low = split(value)
        coeff_high[RANK * d : RANK * (d + 1), :] = high
        coeff_low[RANK * d : RANK * (d + 1), :] = low
    coeff_high[RANK * subs : RANK * (subs + 1), :] = none
    coeff_low[RANK * subs : RANK * (subs + 1), :] = none
    up = jnp.concatenate([coeff_ref[d, RANK : RANK + ROWS8, :] for d in range(subs)], axis=0)
    value = jnp.concatenate(
        [gathered[pl.ds(q, ROWS8 * subs, stride=QUADS), :] for q in range(QUADS)], axis=1
    )
    every = dot_first(up, value)
    top = jnp.zeros((RANK, COLS), F32)
    for q in range(QUADS):
        top = top + every[RANK * q : RANK * (q + 1), COLS * q : COLS * (q + 1)]
    lane_group = lanes(RANK) // RANK
    targets = []
    for weight_ref, ids_ref, shift in zip(weight_refs, ids_refs, [0] + shifts(rows_y)):
        targets += [(weight_ref, ids_ref, n, shift + n * buffers) for n in range(2)]
    top_weight = []
    for weight_ref, ids_ref, n, _ in targets:
        used = jnp.zeros((RANK, COLS), F32)
        for k in range(top_slots):
            owner = ids_ref[n, 64 + slots + k].astype(jnp.int32)
            used = jnp.where(lane_group == k, jnp.where(owner == source, 1.0, 0.0), used)
        top_weight.append(weight_ref[n, 2 * RANK : 3 * RANK, :] * used)
    top_high, top_low = split(top)
    top_part = dot_split(
        jnp.concatenate(top_weight, axis=0),
        jnp.concatenate([top_high] * 4, axis=0),
        jnp.concatenate([top_low] * 4, axis=0),
    )

    def starts(ids_ref, n):
        found = []
        for k in range(slots):
            index = ids_ref[n, 64 + k].astype(jnp.int32)
            block = jnp.where(index // subs == source, index % subs, subs)
            found.append(pl.multiple_of(block * RANK, RANK))
        return found

    for t in range(0, rows_y, 2):
        two = targets[t : t + 2]
        pair = [starts(ids_ref, n) for _, ids_ref, n, _ in two]
        rows = [
            jnp.concatenate(
                [jnp.concatenate([ref[pl.ds(s, RANK), :] for s in one], axis=0) for one in pair], axis=1
            )
            for ref in (coeff_high, coeff_low)
        ]
        weight = [
            jnp.concatenate([w[n, 0:RANK, :], w[n, RANK : 2 * RANK, :64]], axis=1) for w, _, n, _ in two
        ]
        both = dot_split(jnp.concatenate(weight, axis=0), *rows)
        for m, (_, _, _, offset) in enumerate(two):
            at = (row + 2 * rows_y - offset * (1 - 2 * core)) % rows_y
            mine = both[RANK * m : RANK * (m + 1), COLS * m : COLS * (m + 1)]
            mine = mine + top_part[RANK * (t + m) : RANK * (t + m + 1)]
            out_ref[at] = mine if own else mine + before_ref[at]


def last_kernel(parts_ref, fixed_ref, slope_ref, out_ref, natural, held, sems):
    total = parts_ref[0]
    for t in range(1, parts_ref.shape[0]):
        total = total + parts_ref[t]
    store_natural(natural, 0, total)
    high, low = split(natural[...])
    rows = jnp.concatenate([high, low, high, jnp.zeros((RANK, COLS), BF16)], axis=0)
    writes = [pltpu.make_async_copy(held.at[i], out_ref.at[i], sems.at[i]) for i in range(held.shape[0])]
    for i, write in enumerate(writes):
        held[i] = fixed_ref[i] + dot(slope_ref[i], rows)
        write.start()
    for write in writes:
        write.wait()


def whole(kernel, out, args, smem=(), hbm=(), scratch=(), flops=0, limit=VMEM_LIMIT, out_hbm=False):
    vmem = pl.BlockSpec(memory_space=pltpu.VMEM)
    scalars = pl.BlockSpec(memory_space=pltpu.SMEM)
    far = pl.BlockSpec(memory_space=pltpu.HBM)
    place = far if out_hbm else vmem
    size = sum(a.size * a.dtype.itemsize for a in args)
    outs = out if isinstance(out, tuple) else (out,)
    size += sum(o.size * o.dtype.itemsize for o in outs)
    return pl.pallas_call(
        kernel,
        out_shape=out,
        in_specs=[scalars if n in smem else far if n in hbm else vmem for n in range(len(args))],
        out_specs=tuple(place for _ in out) if isinstance(out, tuple) else place,
        scratch_shapes=list(scratch),
        compiler_params=pltpu.CompilerParams(vmem_limit_bytes=limit),
        cost_estimate=pl.CostEstimate(flops=flops, bytes_accessed=size, transcendentals=0),
    )(*args)


def rows_of(x):
    if x.ndim == 2:
        return x.reshape(x.shape[0], ROWS8, COLS).transpose(1, 0, 2).reshape(-1, COLS)
    return x.reshape(x.shape[0], x.shape[1], ROWS8, COLS).transpose(1, 2, 0, 3).reshape(-1, COLS)


def body(
    traction_vectors,
    row_basis,
    up_leaf,
    up_pair,
    up_device,
    couple_leaf,
    pair_coupling_blocks,
    couple_device,
    couple_top,
    list_leaf,
    list_pair,
    list_device,
    list_top,
    mask_leaf,
    mask_pair,
    mask_device,
    mask_top,
    down_leaf,
    down_pair,
    down_device,
    col_basis,
):
    def shape(*dims, dtype=F32):
        return jax.ShapeDtypeStruct(dims, dtype)

    leaves, entries, _ = traction_vectors.shape
    blocks = leaves + leaves // 2
    targets = lax.axis_size("y")
    subs = lax.axis_size("x") * lax.axis_size("z")
    def fetched(args):
        return [pltpu.VMEM(a.shape, a.dtype) for a in args] + [pltpu.SemaphoreType.DMA((len(args),))]

    first = (
        traction_vectors, row_basis, rows_of(up_leaf), rows_of(up_pair), rows_of(up_device),
        rows_of(couple_device), rows_of(down_device), rows_of(couple_top[0]),
        list_device, mask_device, list_top, mask_top,
    )
    results = (shape(1, 3 * RANK, COLS), shape(blocks * RANK, COLS), shape(subs, RANK + ROWS8, COLS))
    weights, stack, send = whole(
        first_kernel,
        results,
        first,
        hbm=range(len(first)),
        out_hbm=True,
        scratch=[
            *fetched(first[1:]),
            pltpu.VMEM(traction_vectors.shape, F32),
            pltpu.SemaphoreType.DMA((leaves,)),
            pltpu.VMEM((RANK, COLS), F32),
            *fetched(results),
        ],
        flops=6 * 10**7,
        limit=ALMOST_ALL,
    )

    def over_y(block, step):
        moves = []
        for y in range(targets):
            moves.append((2 * y, 2 * ((y + step) % targets)))
            moves.append((2 * y + 1, 2 * ((y - step) % targets) + 1))
        return lax.ppermute(block, ("y", "core"), moves)

    weights = jnp.concatenate([weights, over_y(weights, targets // 2)], axis=0)
    coeffs = lax.all_to_all(send, ("x", "z"), 0, 0, tiled=True)
    weights = [weights] + [over_y(weights, step) for step in shifts(targets)]
    leaf_axes = ("x", "z")
    low = lax.ppermute(stack, leaf_axes, [(i, i + 1) for i in range(subs - 1)])
    high = lax.ppermute(stack, leaf_axes, [(i + 1, i) for i in range(subs - 1)])
    near = pltpu.VMEM(((3 * blocks + 1) * RANK, COLS), BF16)
    fixed, slope = whole(
        far_kernel,
        (shape(leaves, entries, COLS), shape(leaves, entries, COLS, dtype=BF16)),
        (
            low, stack, high, rows_of(couple_leaf), rows_of(pair_coupling_blocks),
            rows_of(down_leaf), rows_of(down_pair), col_basis,
            list_leaf, mask_leaf, list_pair, mask_pair,
        ),
        smem=(8, 9, 10, 11),
        scratch=[near, near, pltpu.VMEM((2 * RANK * blocks, COLS), F32)],
        flops=10**8,
    )
    coeffs, weights, fixed, slope = lax.optimization_barrier((coeffs, weights, fixed, slope))
    other = lax.ppermute(coeffs, "core", [(0, 1), (1, 0)])
    weights = [*weights, *(block[:, RANK, :] for block in weights)]
    count = len(weights) // 2
    parts = []
    for own, gathered in ((True, coeffs), (False, other)):
        parts = whole(
            functools.partial(part_kernel, own),
            shape(targets, RANK, COLS),
            (gathered, *weights, *([] if own else [parts])),
            smem=range(1 + count, 1 + 2 * count),
            scratch=[
                pltpu.VMEM(((subs + 1) * RANK, COLS), BF16),
                pltpu.VMEM(((subs + 1) * RANK, COLS), BF16),
                pltpu.VMEM((subs * RANK, COLS), F32),
            ],
            flops=5 * 10**7,
        )
    parts = lax.all_to_all(parts, "y", 0, 0, tiled=True)
    return whole(
        last_kernel,
        shape(leaves, entries, COLS),
        (parts, fixed, slope),
        out_hbm=True,
        scratch=[
            pltpu.VMEM((RANK, COLS), F32),
            pltpu.VMEM((leaves, entries, COLS), F32),
            pltpu.SemaphoreType.DMA((leaves,)),
        ],
        flops=5 * 10**7,
    )


def solution(mesh):
    deep = max(1, mesh.shape["leaf"] // 4)
    sizes = (mesh.shape["top"] // 2, 2, mesh.shape["leaf"] // deep, deep)
    fine = jax.sharding.Mesh(mesh.devices.reshape(sizes), ("y", "core", "x", "z"))
    top, both = ("y", "core"), ("y", "core", "x", "z")
    return jax.shard_map(
        body,
        mesh=fine,
        in_specs=(
            P(both, None, None),
            P(both, None, None),
            P(both, None),
            P(both, None),
            P(both, None),
            P(both, None, None),
            P(both, None, None),
            P(both, None, None),
            P(top, None, None),
            P(both, None),
            P(both, None),
            P(both, None),
            P(top, None),
            P(both, None),
            P(both, None),
            P(both, None),
            P(top, None),
            P(both, None),
            P(both, None),
            P(both, None),
            P(both, None, None),
        ),
        out_specs=P(both, None, None),
        check_vma=False,
    )
```
